32 devices in a mesh: dp: 4 (over y, core), tensor: 8 (over z, x).
Axes of the slice: x: 2, y: 2, z: 4, core: 2. Of those that a mesh axis runs over, the one named last changes fastest.
Arguments:
- tokens: bfloat16 [12288, 2048], P(('dp', 'tensor')), may hold values from -6 to 6
- cotangent: bfloat16 [12288, 2048], P(('dp', 'tensor')), may hold values from -6 to 6
- w_qkv: bfloat16 [2048, 3, 2048], P(None, None, 'tensor'), may hold values from -0.1875 to 0.1875
- b_qkv: float32 [3, 2048], P(None, 'tensor'), may hold values from -3 to 3
- w_out: bfloat16 [2048, 2048], P('tensor'), may hold values from -3 to 3
- b_out: float32 [2048], replicated, may hold values from -4 to 4
- gain_one: float32 [2048], replicated, may hold values from 0.25 to 1.75
- shift_one: float32 [2048], replicated, may hold values from -3 to 3
- w_gu: bfloat16 [2048, 2, 5472], P(None, None, 'tensor'), may hold values from -0.125 to 0.125
- b_gu: float32 [2, 5472], P(None, 'tensor'), may hold values from -3 to 3
- w_down: bfloat16 [5472, 2048], P('tensor'), may hold values from -0.625 to 0.625
- b_down: float32 [2048], replicated, may hold values from -4 to 4
- gain_two: float32 [2048], replicated, may hold values from 0.25 to 1.75
- shift_two: float32 [2048], replicated, may hold values from -3 to 3
- prefix: int32 [12], P('dp'), may hold values from 256 to 768
- span_offset: int32 [12], P('dp'), may hold values from 0 to 255
- cluster: int32 [8], replicated, may hold values from 0 to 3, as said below
Outputs:
- layer_out: float32 [12288, 2048], P(('dp', 'tensor'))
- input_grad: float32 [12288, 2048], P(('dp', 'tensor'))
- grad_w_qkv: float32 [2048, 3, 2048], P(None, None, 'tensor')
- grad_b_qkv: float32 [3, 2048], P(None, 'tensor')
- grad_w_out: float32 [2048, 2048], P('tensor')
- grad_b_out: float32 [2048], replicated
- grad_gain_one: float32 [2048], replicated
- grad_shift_one: float32 [2048], replicated
- grad_w_gu: float32 [2048, 2, 5472], P(None, None, 'tensor')
- grad_b_gu: float32 [2, 5472], P(None, 'tensor')
- grad_w_down: float32 [5472, 2048], P('tensor')
- grad_b_down: float32 [2048], replicated
- grad_gain_two: float32 [2048], replicated
- grad_shift_two: float32 [2048], replicated
The draws below stay inside these ranges and needn't reach their ends.
Inputs may be any that keep to these rules, and one draw needn't show every extreme that they name: Item i stands on index cluster[i] of dp, in slots filled from the lowest; no index holds more than 3 items, and some index holds exactly 3.
All inputs are finite; a program needn't handle non-finite values.
Results may differ from the reference program's by a relative error of at most 0.025.
The reference program's roundings to bfloat16 on the way count: a program that leaves them out, or rounds other values in their place, can miss the bound.
Values may be sent and summed in bfloat16 or wider, within the bound.
A program may use at most 256 MiB of HBM per device.

```python
import math
import jax
import jax.numpy as jnp
from jax import lax

D = 2048
H = 16
HD = 128
FF = 5461
FFP = 5472
LEN = 1024
ITEM_DEV = 2
ITEMS = 8
CAP = 3
SLOTS = 12
ROWS = 12288
N_DP = 4
N_TENSOR = 8


def draw_cluster(key, part):
    key = jax.random.fold_in(key, 7)
    key_order, key_shift, key_mix = jax.random.split(key, 3)
    order = jax.random.permutation(key_order, N_DP)
    shifts = jax.random.randint(key_shift, (N_DP // 2,), -1, 2)
    shifts = shifts.at[0].set(1)
    pair_counts = jnp.stack([ITEM_DEV + shifts, ITEM_DEV - shifts], 1).reshape(-1).astype(jnp.int32)
    counts = jnp.zeros((N_DP,), jnp.int32).at[order].set(pair_counts)
    labels = jnp.repeat(jnp.arange(N_DP, dtype=jnp.int32), counts, total_repeat_length=ITEMS)
    return jax.random.permutation(key_mix, labels).astype(jnp.int32)


def place_ends(drawn, rng, smallest, top_value):
    longest = drawn.shape.index(max(drawn.shape))
    spots = []
    for shift in (0, 1):
        where = [jax.random.randint(jax.random.fold_in(rng, axis), (), 0, length) for axis, length in enumerate(drawn.shape)]
        where[longest] = (where[longest] + shift) % drawn.shape[longest]
        spots.append(tuple(where))
    return drawn.at[spots[0]].set(smallest).at[spots[1]].set(top_value)


def block_scale(key, shape, cuts, smallest, top_value):
    def one(axis_at, shards_of):
        heights = jax.random.uniform(jax.random.fold_in(jax.random.fold_in(key, 6), axis_at), (shards_of,), jnp.float32, smallest / len(cuts), top_value / len(cuts))
        return jnp.repeat(jnp.exp(heights), shape[axis_at] // shards_of).reshape((-1,) + (1,) * (len(shape) - axis_at - 1))

    factor_of = one(*cuts[0])
    for cut in cuts[1:]:
        factor_of = factor_of * one(*cut)
    return factor_of


def centred(key, dims, deviation, bound, pieces=(), kind=jnp.bfloat16):
    values = jax.random.normal(key, dims, jnp.float32) * deviation
    if len(pieces) > 0:
        values = block_scale(key, dims, pieces, -0.22, 0.18) * values
    return jnp.clip(values, min=-bound, max=bound).astype(kind)


def setup_inputs(seed: int = 0) -> dict:
    streams_of = jax.random.split(jax.random.key(seed), 18)
    return {
        "tokens": centred(streams_of[0], (ROWS, D), 1.0, 6.0, ((0, 32),)),
        "cotangent": centred(streams_of[1], (ROWS, D), 1.0, 6.0, ((0, 32),)),
        "w_qkv": centred(streams_of[2], (D, 3, D), (D // 2) ** -0.5, 0.1875, ((2, 8),)),
        "b_qkv": centred(streams_of[3], (3, D), 0.5, 3.0, ((1, 8),), jnp.float32),
        "w_out": centred(streams_of[4], (D, D), 0.5, 3.0, ((0, 8),)),
        "b_out": centred(streams_of[5], (D,), 1.0, 4.0, (), jnp.float32),
        "gain_one": jnp.clip(1.0 + 0.15 * jax.random.normal(streams_of[6], (D,), jnp.float32), 0.25, 1.75),
        "shift_one": centred(streams_of[7], (D,), 0.5, 3.0, (), jnp.float32),
        "w_gu": centred(streams_of[8], (D, 2, FFP), D ** -0.5, 0.125, ((2, 8),)),
        "b_gu": centred(streams_of[9], (2, FFP), 0.5, 3.0, ((1, 8),), jnp.float32),
        "w_down": centred(streams_of[10], (FFP, D), (max(FFP // 64, 1)) ** -0.5, 0.625, ((0, 8),)),
        "b_down": centred(streams_of[11], (D,), 1.0, 4.0, (), jnp.float32),
        "gain_two": jnp.clip(1.0 + 0.15 * jax.random.normal(streams_of[12], (D,), jnp.float32), 0.25, 1.75),
        "shift_two": centred(streams_of[13], (D,), 0.5, 3.0, (), jnp.float32),
        "prefix": place_ends(jax.random.randint(streams_of[14], (SLOTS,), LEN // 4, 3 * LEN // 4 + 1), jax.random.fold_in(streams_of[14], 1), LEN // 4, (3 * LEN // 4 + 1) - 1).astype(jnp.int32),
        "span_offset": place_ends(jax.random.randint(streams_of[15], (SLOTS,), 0, LEN // 4), jax.random.fold_in(streams_of[15], 1), 0, (LEN // 4) - 1).astype(jnp.int32),
        "cluster": draw_cluster(jax.random.fold_in(streams_of[17], 71), 0),
    }


deep_alpha = math.sqrt(48.0)
epsilon = 1e-05
negative = -1e+30
theta_base = 10000.0
highest = lax.Precision.HIGHEST

@jax.custom_vjp
def low(v):
    return lax.optimization_barrier(v.astype(jnp.bfloat16)).astype(jnp.float32)

@jax.custom_vjp
def low_back(v):
    return v

def low_keep(v):
    return (low(v), None)

def low_pass(kept, grad):
    return (grad,)

def back_keep(v):
    return (v, None)

def back_low(kept, grad):
    return (low(grad),)
low.defvjp(low_keep, low_pass)
low_back.defvjp(back_keep, back_low)

def rotary_tables(prefix_len, span_start):
    position = jnp.arange(LEN)
    placed = jnp.where(position < prefix_len, position, span_start + position - prefix_len).astype(jnp.float32)
    frequency = theta_base ** (-(jnp.arange(HD // 2).astype(jnp.float32) * 2.0 / HD))
    angles = placed[:, None] * frequency[None, :]
    return (jnp.cos(angles), jnp.sin(angles))

def rotate(vectors, cos_table, sin_table):
    halfway = vectors.shape[-1] // 2
    leading = vectors[..., :halfway]
    trailing = vectors[..., halfway:]
    cos_table = cos_table[:, None, :]
    sin_table = sin_table[:, None, :]
    return jnp.concatenate([leading * cos_table - trailing * sin_table, trailing * cos_table + leading * sin_table], -1)

def layer_norm(values, gain, shift):
    centre = values - lax.optimization_barrier(jnp.mean(values, -1, keepdims=True))
    spread = lax.optimization_barrier(jnp.mean(centre * centre, -1, keepdims=True))
    return centre * lax.rsqrt(spread + epsilon) * gain + shift

def item_layer(token_item, params, prefix_len, span_start):
    w_qkv, b_qkv, w_out, b_out, gain_one, shift_one, w_gu, b_gu, w_down, b_down, gain_two, shift_two = params
    groups = N_TENSOR
    width_qkv = D // groups
    width_ffn = FFP // groups
    cos_table, sin_table = rotary_tables(prefix_len, span_start)
    linear = jnp.einsum('td,dcn->tcn', low(token_item), w_qkv, precision=highest) + b_qkv
    linear = low_back(linear).reshape(LEN, 3, H, HD)
    queries = low(rotate(linear[:, 0], cos_table, sin_table))
    keys_rot = low(rotate(linear[:, 1], cos_table, sin_table))
    values_in = low(linear[:, 2])
    scores = low_back(jnp.einsum('qhe,khe->hqk', queries, keys_rot, precision=highest) * HD ** (-0.5))
    position = jnp.arange(LEN)
    allowed = (position[None, :] < prefix_len) | (position[None, :] <= position[:, None])
    scores = jnp.where(allowed[None], scores, negative)
    weights_raw = jnp.exp(scores - lax.optimization_barrier(jnp.max(scores, -1, keepdims=True)))
    weights = low(weights_raw / lax.optimization_barrier(jnp.sum(weights_raw, -1, keepdims=True)))
    context = jnp.einsum('hqk,khe->qhe', weights, values_in, precision=highest)
    context = low(low_back(context)).reshape(LEN, groups, width_qkv)
    partial_out = jnp.einsum('tgn,gnd->gtd', context, w_out.reshape(groups, width_qkv, D), precision=highest)
    attended = low_back(lax.optimization_barrier(jnp.sum(low(partial_out), 0))) + b_out
    hidden_one = layer_norm(deep_alpha * token_item + attended, gain_one, shift_one)
    gate_up = jnp.einsum('td,dcn->tcn', low(hidden_one), w_gu, precision=highest) + b_gu
    gate_up = low_back(gate_up)
    live_columns = jnp.arange(FFP) < FF
    inner = low(jnp.where(live_columns, jax.nn.gelu(gate_up[:, 0], approximate=True) * gate_up[:, 1], 0.0))
    partial_fed = jnp.einsum('tgn,gnd->gtd', inner.reshape(LEN, groups, width_ffn), w_down.reshape(groups, width_ffn, D), precision=highest)
    fed = low_back(lax.optimization_barrier(jnp.sum(low(partial_fed), 0))) + b_down
    return layer_norm(deep_alpha * hidden_one + fed, gain_two, shift_two)

def reference(tokens, cotangent, w_qkv, b_qkv, w_out, b_out, gain_one, shift_one, w_gu, b_gu, w_down, b_down, gain_two, shift_two, prefix, span_offset, cluster):
    params = tuple((member.astype(jnp.float32) for member in (w_qkv, b_qkv, w_out, b_out, gain_one, shift_one, w_gu, b_gu, w_down, b_down, gain_two, shift_two)))
    counts = lax.optimization_barrier(jnp.sum((cluster[None, :] == jnp.arange(N_DP)[:, None]).astype(jnp.int32), 1))
    slot_index = jnp.arange(SLOTS)
    live_slot = jnp.where(slot_index % CAP < counts[slot_index // CAP], 1.0, 0.0).astype(jnp.float32)
    token_items = tokens.astype(jnp.float32).reshape(SLOTS, LEN, D)
    cot_items = cotangent.astype(jnp.float32).reshape(SLOTS, LEN, D) * live_slot[:, None, None]
    starts = jax.tree.map(jnp.zeros_like, params)

    def one_item(totals, packed):
        token_item, cot_item, prefix_len, span_start, weight = packed

        def forward(token_arg, param_arg):
            return item_layer(token_arg, param_arg, prefix_len, span_start)
        result, pullback = jax.vjp(forward, token_item, params)
        grad_tokens, grad_params = pullback(cot_item)
        totals = jax.tree.map(jnp.add, totals, grad_params)
        return (totals, (result * weight, grad_tokens))
    totals, (layer_rows, grad_rows) = lax.scan(one_item, starts, (token_items, cot_items, prefix, span_offset, live_slot))
    return (layer_rows.reshape(ROWS, D), grad_rows.reshape(ROWS, D), totals[0], totals[1], totals[2], totals[3], totals[4], totals[5], totals[6], totals[7], totals[8], totals[9], totals[10], totals[11])
```

```python
import math

import jax
import jax.numpy as jnp
from jax import lax
from jax.sharding import PartitionSpec as P

HD = 128
FF = 5461
LEN = 1024
CAP = 3

deep_alpha = math.sqrt(48.0)
epsilon = 1e-05
negative = -1e30
theta_base = 10000.0
f32 = jnp.float32
bf16 = jnp.bfloat16


def bits_of(count):
    return [1 << b for b in range(count.bit_length() - 1)]


def permute(value, axis, size, bit):
    return lax.ppermute(value, axis, [(i, i ^ bit) for i in range(size)])


def rotate(vectors, cos_table, sin_table):
    halfway = vectors.shape[-1] // 2
    leading = vectors[..., :halfway]
    trailing = vectors[..., halfway:]
    return jnp.concatenate(
        [leading * cos_table - trailing * sin_table, trailing * cos_table + leading * sin_table], -1
    )


def norm_forward(values, gain, shift):
    centre = values - jnp.mean(values, -1, keepdims=True)
    scale_inv = lax.rsqrt(jnp.mean(centre * centre, -1, keepdims=True) + epsilon)
    normed = centre * scale_inv
    return (normed * gain + shift, normed, scale_inv)


def norm_backward(grad_out, normed, scale_inv, gain):
    grad_gain = jnp.sum(grad_out * normed, 0)
    grad_shift = jnp.sum(grad_out, 0)
    grad_normed = grad_out * gain
    centred = grad_normed - jnp.mean(grad_normed, -1, keepdims=True)
    grad_in = scale_inv * (
        centred - normed * jnp.mean(grad_normed * normed, -1, keepdims=True)
    )
    return (grad_in, grad_gain, grad_shift)


def top_bit(number):
    return 1 << (number.bit_length() - 1)


def low_bit(number):
    return number & -number


class Group:
    def __init__(self, size):
        self.size = size
        self.width = size // 2

    def gather(self, own):
        rows = own.shape[0] // 2
        got = {0: own}
        for offset in range(1, self.width):
            high, low = top_bit(offset), low_bit(offset)
            if high == low:
                got[offset] = permute(own, "tensor", self.size, high)
            else:
                got[offset] = jnp.concatenate(
                    [
                        permute(got[offset ^ high][:rows], "tensor", self.size, high),
                        permute(got[offset ^ low][rows:], "tensor", self.size, low),
                    ],
                    0,
                )
        return [got[offset] for offset in range(self.width)]

    def scatter(self, parts):
        rows = parts[0].shape[0] // 2
        low_half = {o: part[:rows] for o, part in enumerate(parts)}
        high_half = {o: part[rows:] for o, part in enumerate(parts)}
        total = parts[0].astype(f32)

        def add(mine, theirs):
            return (mine.astype(f32) + theirs.astype(f32)).astype(bf16)

        count = lambda o: bin(o).count("1")
        for offset in sorted(range(1, self.width), key=lambda o: -count(o)):
            high, low = top_bit(offset), low_bit(offset)
            if high == low:
                whole = jnp.concatenate([low_half[offset], high_half[offset]], 0)
                total = total + permute(whole, "tensor", self.size, high).astype(f32)
            else:
                a, b = offset ^ high, offset ^ low
                low_half[a] = add(low_half[a], permute(low_half[offset], "tensor", self.size, high))
                high_half[b] = add(high_half[b], permute(high_half[offset], "tensor", self.size, low))
        return total


def block_moves(size):
    width = size // 2
    edges = {0: [], 1: []}
    for b in range(CAP * size):
        slot, j = divmod(b, size)
        target = (width if slot else 0) + j // 2
        edges[1 if slot == 2 else 0].append((b // CAP, b % CAP, target, j % 2))
    plans = {}
    for kind, listed in edges.items():
        local = [e for e in listed if e[0] == e[2]]
        rounds = []
        for e in (e for e in listed if e[0] != e[2]):
            for r in rounds:
                if all(e[0] != o[0] and e[2] != o[2] for o in r):
                    r.append(e)
                    break
            else:
                rounds.append([e])
        plans[kind] = (local, rounds)
    return plans


def pick(index, values):
    out = values[0]
    for k, value in enumerate(values[1:], 1):
        out = jnp.where(index == k, value, out)
    return out


def lookup(table, index):
    return jnp.asarray(table, jnp.int32)[index]


def move_in(blocks, t, size, kind):
    local, rounds = block_moves(size)[kind]
    got = []
    for r in rounds:
        which = [0] * size
        for src, i, dst, place in r:
            which[src] = i
        send = pick(lookup(which, t), blocks)
        got.append(lax.ppermute(send, "tensor", [(e[0], e[2]) for e in r]))
    places = []
    for place in range(2):
        choice = [0] * size
        for src, i, dst, at in local:
            if at == place:
                choice[dst] = i
        for k, r in enumerate(rounds):
            for src, i, dst, at in r:
                if at == place:
                    choice[dst] = CAP + k
        places.append(pick(lookup(choice, t), blocks + got))
    return jnp.concatenate(places, 0)


def move_out(item, other, t, size):
    plans = block_moves(size)
    half = item.shape[0] // 2
    pieces = {0: [item[:half], item[half:]], 1: [other[:half], other[half:]]}
    sources = []
    choice = [[0] * size for _ in range(CAP)]
    for kind in (0, 1):
        local, rounds = plans[kind]
        for src, i, dst, at in local:
            choice[i][src] = len(sources) + at
        sources += pieces[kind]
        for r in rounds:
            which = [0] * size
            for src, i, dst, at in r:
                which[dst] = at
                choice[i][src] = len(sources)
            send = pick(lookup(which, t), pieces[kind])
            sources.append(lax.ppermute(send, "tensor", [(e[2], e[0]) for e in r]))
    return jnp.concatenate([pick(lookup(choice[i], t), sources) for i in range(CAP)], 0)


def across(value, n_dp):
    got = {0: value}
    for bit in reversed(bits_of(n_dp)):
        for offset in list(got):
            got[offset | bit] = permute(got[offset], "dp", n_dp, bit)
    return [got[offset] for offset in range(n_dp)]


def attend(queries, keys_rot, values_in, allowed):
    scores = jnp.einsum("qhe,khe->hqk", queries, keys_rot, preferred_element_type=f32)
    scores = jnp.where(allowed[None], scores * HD ** (-0.5), negative)
    row_top = jnp.max(scores, -1, keepdims=True)
    weights_raw = jnp.exp(scores - row_top)
    row_total = jnp.sum(weights_raw, -1, keepdims=True)
    weights = (weights_raw / row_total).astype(bf16)
    context = jnp.einsum("hqk,khe->qhe", weights, values_in, preferred_element_type=f32)
    return context.astype(bf16), (row_top + jnp.log(row_total))[..., 0]


def attend_back(queries, keys_rot, values_in, log_total, grad_context, allowed):
    scale = HD ** (-0.5)
    scores = jnp.einsum("qhe,khe->hqk", queries, keys_rot, preferred_element_type=f32)
    scores = jnp.where(allowed[None], scores * scale, negative)
    weights = jnp.exp(scores - log_total[..., None])
    grad_weights = jnp.einsum("qhe,khe->hqk", grad_context, values_in, preferred_element_type=f32)
    row_inner = jnp.sum(weights * grad_weights, -1, keepdims=True)
    grad_scores = (weights * (grad_weights - row_inner)).astype(bf16)
    grad_query = jnp.einsum("hqk,khe->qhe", grad_scores, keys_rot, preferred_element_type=f32) * scale
    grad_keys = jnp.einsum("hqk,qhe->khe", grad_scores, queries, preferred_element_type=f32) * scale
    grad_values = jnp.einsum(
        "hqk,qhe->khe", weights.astype(bf16), grad_context, preferred_element_type=f32
    )
    return grad_query, grad_keys, grad_values


def on_device(
    n_dp,
    n_tensor,
    tokens,
    cotangent,
    w_qkv,
    b_qkv,
    w_out,
    b_out,
    gain_one,
    shift_one,
    w_gu,
    b_gu,
    w_down,
    b_down,
    gain_two,
    shift_two,
    prefix,
    span_offset,
    cluster,
):
    d = lax.axis_index("dp")
    t = lax.axis_index("tensor")
    group = Group(n_tensor)
    width = group.width
    h = t // width
    q = t % width
    rows = LEN // width
    model = tokens.shape[1]
    block = LEN // n_tensor

    counts = jnp.sum((cluster[None, :] == jnp.arange(n_dp)[:, None]).astype(jnp.int32), 1)
    spare = jnp.maximum(2 - counts, 0)
    extra = (counts == CAP).astype(jnp.int32)
    spare_before = jnp.cumsum(spare) - spare
    extra_rank = jnp.cumsum(extra) - extra

    def overflow_source(index, place):
        rank = spare_before[index] + place - counts[index]
        hit = (extra == 1) & (extra_rank == rank)
        return jnp.sum(jnp.where(hit, jnp.arange(n_dp), 0))

    source_here = overflow_source(d, h)
    source_other = overflow_source(d, 0)
    foreign = counts[d] <= h
    any_empty = jnp.any(counts == 0)
    rank_out = extra_rank[d]
    ends = spare_before + spare
    out_index = jnp.sum((ends <= rank_out).astype(jnp.int32))
    out_place = jnp.minimum(counts[out_index], 2) + rank_out - spare_before[out_index]

    def spread(array):
        blocks = [array[i * block : (i + 1) * block] for i in range(CAP)]
        third = across(move_in(blocks, t, n_tensor, 1), n_dp)
        first = move_in(blocks, t, n_tensor, 0)

        def with_empty(first):
            sent = permute(pick(d ^ source_other, third), "tensor", n_tensor, width)
            return jnp.where((h == 0) & foreign, sent, first)

        first = lax.cond(any_empty, with_empty, lambda v: v, first)
        return jnp.where((h == 1) & foreign, pick(d ^ source_here, third), first)

    def collect(array):
        third = pick(d ^ out_index, across(array, n_dp))

        def with_empty(third):
            other = across(permute(array, "tensor", n_tensor, width), n_dp)
            return jnp.where(out_place == 0, pick(d ^ out_index, other), third)

        third = lax.cond(any_empty, with_empty, lambda v: v, third)
        third = jnp.where(counts[d] == CAP, third, 0)
        return move_out(jnp.where(foreign, 0, array), third, t, n_tensor)

    facts = jnp.stack([prefix, span_offset])
    facts_all = lax.all_gather(facts, "dp", axis=0, tiled=False)
    fact = jnp.where(foreign, facts_all[source_here][:, 2], jnp.where(h == 0, facts[:, 0], facts[:, 1]))
    prefix_len, span_start = fact[0], fact[1]

    position = ((q ^ jnp.arange(width))[:, None] * rows + jnp.arange(rows)[None, :]).reshape(LEN)
    placed = jnp.where(position < prefix_len, position, span_start + position - prefix_len).astype(f32)
    frequency = theta_base ** (-(jnp.arange(HD // 2).astype(f32) * 2.0 / HD))
    angles = placed[:, None] * frequency[None, :]
    cos_table, sin_table = jnp.cos(angles)[:, None, :], jnp.sin(angles)[:, None, :]
    allowed = (position[None, :] < prefix_len) | (position[None, :] <= position[:, None])

    def fetch(weight, axis):
        part = weight.shape[axis] // n_dp
        share = lax.dynamic_slice_in_dim(weight, d * part, part, axis)
        share = permute(share, "tensor", n_tensor, width)
        for bit in reversed(bits_of(n_dp)):
            got = permute(share, "dp", n_dp, bit)
            mine_first = (d & bit) == 0
            share = jnp.concatenate(
                [jnp.where(mine_first, share, got), jnp.where(mine_first, got, share)], axis
            )
        count = len(bits_of(n_dp))
        shaped = share.reshape(share.shape[:axis] + (2,) * count + (part,) + share.shape[axis + 1 :])
        order = (
            list(range(axis))
            + list(reversed(range(axis, axis + count)))
            + list(range(axis + count, shaped.ndim))
        )
        return shaped.transpose(order).reshape(weight.shape)

    def pair(weight, axis, cut):
        return jnp.stack([weight, fetch(weight, cut)], axis)

    width_qkv = w_qkv.shape[2]
    heads = width_qkv // HD
    width_ffn = w_gu.shape[2]

    wq = pair(w_qkv, 2, 0)
    wo = pair(w_out, 0, 1)
    wg = pair(w_gu, 2, 0)
    wd = pair(w_down, 0, 1)
    bq = jnp.stack([b_qkv, permute(b_qkv, "tensor", n_tensor, width)], 1)
    bg = jnp.stack([b_gu, permute(b_gu, "tensor", n_tensor, width)], 1)
    slices = jnp.stack([t, t ^ width])
    live_columns = slices[:, None] * width_ffn + jnp.arange(width_ffn)[None, :] < FF

    def parts_of(array):
        return [array[o * rows : (o + 1) * rows] for o in range(width)]

    own_tokens = spread(tokens)
    own_cotangent = spread(cotangent)
    tokens_all = jnp.concatenate(group.gather(own_tokens), 0)

    linear = jnp.einsum("td,dcpn->tcpn", tokens_all, wq, preferred_element_type=f32) + bq
    linear = linear.reshape(LEN, 3, 2 * heads, HD)
    queries = rotate(linear[:, 0], cos_table, sin_table).astype(bf16)
    keys_rot = rotate(linear[:, 1], cos_table, sin_table).astype(bf16)
    values_in = linear[:, 2].astype(bf16)
    context, log_total = attend(queries, keys_rot, values_in, allowed)
    context_rows = context.reshape(LEN, 2, width_qkv)
    partial_out = jnp.einsum("tpn,pnd->td", context_rows, wo, preferred_element_type=f32).astype(bf16)
    attended = group.scatter(parts_of(partial_out)) + b_out
    first_sum = deep_alpha * own_tokens.astype(f32) + attended
    hidden_one, normed_one, inv_one = norm_forward(first_sum, gain_one, shift_one)
    hidden_all = jnp.concatenate(group.gather(hidden_one.astype(bf16)), 0)

    def activate(gate_up):
        return jnp.where(
            live_columns, jax.nn.gelu(gate_up[:, 0], approximate=True) * gate_up[:, 1], 0.0
        )

    gate_up = jnp.einsum("td,dcpn->tcpn", hidden_all, wg, preferred_element_type=f32) + bg
    activated, pull_act = jax.vjp(activate, gate_up)
    inner_low = activated.astype(bf16)
    partial_fed = jnp.einsum("tpn,pnd->td", inner_low, wd, preferred_element_type=f32).astype(bf16)
    fed = group.scatter(parts_of(partial_fed)) + b_down
    second_sum = deep_alpha * hidden_one + fed
    layer_rows, normed_two, inv_two = norm_forward(second_sum, gain_two, shift_two)
    layer_out = collect(layer_rows.astype(bf16)).astype(f32)

    grad_layer = own_cotangent.astype(f32)
    grad_second, grad_gain_two, grad_shift_two = norm_backward(
        grad_layer, normed_two, inv_two, gain_two
    )
    grad_fed_all = jnp.concatenate(group.gather(grad_second.astype(bf16)), 0)
    grad_inner = jnp.einsum("td,pnd->tpn", grad_fed_all, wd, preferred_element_type=f32)
    grad_gate_up = pull_act(grad_inner)[0].astype(bf16)
    partial_hidden = jnp.einsum(
        "tcpn,dcpn->td", grad_gate_up, wg, preferred_element_type=f32
    ).astype(bf16)
    grad_w_down = jnp.einsum("tpn,td->pnd", inner_low, grad_fed_all, preferred_element_type=f32)
    grad_b_gu = jnp.sum(grad_gate_up.astype(f32), 0)
    grad_w_gu = jnp.einsum("td,tcpn->pdcn", hidden_all, grad_gate_up, preferred_element_type=f32)
    grad_hidden = group.scatter(parts_of(partial_hidden)) + deep_alpha * grad_second
    grad_first, grad_gain_one, grad_shift_one = norm_backward(
        grad_hidden, normed_one, inv_one, gain_one
    )
    grad_att_all = jnp.concatenate(group.gather(grad_first.astype(bf16)), 0)
    grad_context = jnp.einsum("td,pnd->tpn", grad_att_all, wo, preferred_element_type=f32)
    grad_context = grad_context.astype(bf16).reshape(LEN, 2 * heads, HD)
    grad_w_out = jnp.einsum("tpn,td->pnd", context_rows, grad_att_all, preferred_element_type=f32)
    grad_query, grad_keys, grad_values = attend_back(
        queries, keys_rot, values_in, log_total, grad_context, allowed
    )
    grad_linear = jnp.stack(
        [
            rotate(grad_query, cos_table, -sin_table),
            rotate(grad_keys, cos_table, -sin_table),
            grad_values,
        ],
        1,
    )
    grad_linear = grad_linear.reshape(LEN, 3, 2, width_qkv).astype(bf16)
    partial_in = jnp.einsum("tcpn,dcpn->td", grad_linear, wq, preferred_element_type=f32).astype(bf16)
    grad_b_qkv = jnp.sum(grad_linear.astype(f32), 0)
    grad_w_qkv = jnp.einsum("td,tcpn->pdcn", tokens_all, grad_linear, preferred_element_type=f32)
    input_rows = group.scatter(parts_of(partial_in)) + deep_alpha * grad_first
    input_grad = collect(input_rows.astype(bf16)).astype(f32)

    def reduce_weight(grads, axis):
        value = grads.astype(bf16)
        for bit in bits_of(n_dp):
            part = value.shape[axis + 1] // 2
            upper = ((d & bit) != 0).astype(jnp.int32)
            send = lax.dynamic_slice_in_dim(value, (1 - upper) * part, part, axis + 1)
            keep = lax.dynamic_slice_in_dim(value, upper * part, part, axis + 1)
            value = (keep.astype(f32) + permute(send, "dp", n_dp, bit).astype(f32)).astype(bf16)
        value = (
            value[0].astype(f32) + permute(value[1], "tensor", n_tensor, width).astype(f32)
        ).astype(bf16)
        for bit in reversed(bits_of(n_dp)):
            got = permute(value, "dp", n_dp, bit)
            mine_first = (d & bit) == 0
            value = jnp.concatenate(
                [jnp.where(mine_first, value, got), jnp.where(mine_first, got, value)], axis
            )
        return value.astype(f32)

    def reduce_small(everywhere, own, other):
        for bit in bits_of(n_dp):
            everywhere, own, other = jax.tree.map(
                lambda v: v + permute(v, "dp", n_dp, bit), (everywhere, own, other)
            )
        own = own + permute(other, "tensor", n_tensor, width)
        for bit in bits_of(n_tensor):
            everywhere = everywhere + permute(everywhere, "tensor", n_tensor, bit)
        return everywhere, own

    norm_grads = jnp.stack(
        [
            grad_gain_one,
            grad_shift_one,
            jnp.sum(grad_first, 0),
            grad_gain_two,
            grad_shift_two,
            jnp.sum(grad_second, 0),
        ]
    )
    bias = [
        jnp.concatenate([grad_b_qkv[:, p].reshape(-1), grad_b_gu[:, p].reshape(-1)]) for p in range(2)
    ]
    norm_grads, bias = reduce_small(norm_grads, bias[0], bias[1])
    grad_b_qkv = bias[: 3 * width_qkv].reshape(3, width_qkv)
    grad_b_gu = bias[3 * width_qkv :].reshape(2, width_ffn)
    return (
        layer_out,
        input_grad,
        reduce_weight(grad_w_qkv, 0),
        grad_b_qkv,
        reduce_weight(grad_w_out, 1),
        norm_grads[2],
        norm_grads[0],
        norm_grads[1],
        reduce_weight(grad_w_gu, 0),
        grad_b_gu,
        reduce_weight(grad_w_down, 1),
        norm_grads[5],
        norm_grads[3],
        norm_grads[4],
    )


def solution(mesh):
    rows = P(("dp", "tensor"), None)
    weights = (P(None, None, "tensor"), P(None, "tensor"), P("tensor", None), P(), P(), P())
    placed_ffn = (P(None, None, "tensor"), P(None, "tensor"), P("tensor", None), P(), P(), P())
    placed = (rows, rows) + weights + placed_ffn + (P("dp"), P("dp"), P())
    n_dp, n_tensor = mesh.shape["dp"], mesh.shape["tensor"]

    def body(*arguments):
        return on_device(n_dp, n_tensor, *arguments)

    return jax.shard_map(
        body,
        mesh=mesh,
        in_specs=placed,
        out_specs=(rows, rows) + weights + placed_ffn,
        check_vma=False,
    )
```

```python
import functools
import math

import jax
import jax.numpy as jnp
from jax import lax
from jax.experimental import pallas as pl
from jax.experimental.pallas import tpu as pltpu
from jax.sharding import PartitionSpec as P

HD = 128
FF = 5461
LEN = 1024
CAP = 3

deep_alpha = math.sqrt(48.0)
epsilon = 1e-05
negative = -1e30
theta_base = 10000.0
f32 = jnp.float32
bf16 = jnp.bfloat16


def bits_of(count):
    return [1 << b for b in range(count.bit_length() - 1)]


def permute(value, axis, size, bit):
    return lax.ppermute(value, axis, [(i, i ^ bit) for i in range(size)])


def top_bit(number):
    return 1 << (number.bit_length() - 1)


def low_bit(number):
    return number & -number


def popcount(number):
    return bin(number).count("1")


def partner(t, bit):
    return t + bit - 2 * bit * ((t // bit) % 2)


def step(ref, start, count):
    return ref.at[pl.ds(start, count)]


ROW_TILE = 16


def row_tiles(count, body):
    def run(i, carry):
        body(pl.multiple_of(i * ROW_TILE, ROW_TILE))
        return carry

    lax.fori_loop(0, count // ROW_TILE, run, 0)


class Ship:
    def __init__(self, n_dp, n_tensor, send, recv, local):
        self.n_dp, self.n_tensor = n_dp, n_tensor
        self.width = n_tensor // 2
        self.send, self.recv, self.local_sems = send, recv, local
        self.used = 0
        self.d, self.t = lax.axis_index("dp"), lax.axis_index("tensor")
        self.h, self.q = self.t // self.width, self.t % self.width

    def slots(self, count):
        self.used += count
        return self.used - count

    def far(self, source, target, axis, place, k, k_recv=None):
        return pltpu.make_async_remote_copy(
            src_ref=source,
            dst_ref=target,
            send_sem=self.send.at[k],
            recv_sem=self.recv.at[k if k_recv is None else k_recv],
            device_id={axis: place},
            device_id_type=pl.DeviceIdType.MESH,
        )

    def near(self, source, target, k):
        return pltpu.make_async_copy(source, target, self.local_sems.at[k])


def along(ref, axis, start, count):
    return ref.at[(slice(None),) * axis + (pl.ds(start, count),)]


def mixed(index, offset):
    for bit in bits_of(offset * 2):
        if offset & bit:
            index = partner(index, bit)
    return index


def mirrored(index, count):
    bits = bits_of(count)
    return sum(((index // bit) % 2) * (count // (2 * bit)) for bit in bits)


def dp_copies(n_dp):
    return n_dp - 1


def dp_steps(ship, view, first=None, only=None):
    base = ship.slots(dp_copies(ship.n_dp))
    guard = (lambda f: f()) if only is None else pl.when(only)
    offsets, copies = [0], []
    for bit in reversed(bits_of(ship.n_dp)):
        new = []
        for o in offsets:
            at = view(mixed(ship.d, o))
            source = first if (first is not None and o == 0) else at
            new.append(ship.far(source, at, "dp", partner(ship.d, bit), base + len(copies) + len(new)))

        @guard
        def _():
            for c in new:
                c.start()

        yield

        @guard
        def _():
            for c in new:
                c.wait_recv()

        copies += new
        offsets += [o | bit for o in offsets]

    @guard
    def _():
        for c in copies:
            c.wait_send()


class Cargo:
    def __init__(self, inputs, outputs, count, run):
        self.inputs, self.outputs, self.count, self.run = inputs, outputs, count, run


def send_share(weight, axis, n_dp):
    part = weight.shape[axis] // n_dp
    shape = list(weight.shape)
    shape[axis] = part

    def run(ship, ins, outs):
        c = ship.far(
            along(ins[0], axis, ship.d * part, part),
            outs[0],
            "tensor",
            partner(ship.t, ship.width),
            ship.slots(1),
        )
        c.start()
        yield
        c.wait()

    return Cargo([weight], [(tuple(shape), weight.dtype)], 1, run)


def join_shares(share, axis, n_dp):
    part = share.shape[axis]
    shape = list(share.shape)
    shape[axis] = part * n_dp

    def run(ship, ins, outs):
        view = lambda i: along(outs[0], axis, i * part, part)
        put = ship.near(ins[0], view(ship.d), ship.slots(1))
        put.start()
        yield from dp_steps(ship, view, first=ins[0])
        put.wait()

    return Cargo([share], [(tuple(shape), share.dtype)], 1 + dp_copies(n_dp), run)


def fetch(weight, axis, n_dp):
    part = weight.shape[axis] // n_dp

    def run(ship, ins, outs):
        view = lambda i: along(outs[0], axis, i * part, part)
        c = ship.far(
            along(ins[0], axis, ship.d * part, part),
            view(ship.d),
            "tensor",
            partner(ship.t, ship.width),
            ship.slots(1),
        )
        c.start()
        yield
        c.wait()
        yield from dp_steps(ship, view)

    return Cargo([weight], [(weight.shape, weight.dtype)], 1 + dp_copies(n_dp), run)


def swap_cargo(array, axis, bit):
    def run(ship, ins, outs):
        index = ship.d if axis == "dp" else ship.t
        c = ship.far(ins[0], outs[0], axis, partner(index, bit), ship.slots(1))
        c.start()
        yield
        c.wait()

    return Cargo([array], [(array.shape, array.dtype)], 1, run)


def gather_dp(share, axis, n_dp):
    part = share.shape[axis]
    shape = list(share.shape)
    shape[axis] = part * n_dp

    def run(ship, ins, outs):
        view = lambda i: along(outs[0], axis, mirrored(i, n_dp) * part, part)
        put = ship.near(ins[0], view(ship.d), ship.slots(1))
        put.start()
        yield from dp_steps(ship, view, first=ins[0])
        put.wait()

    return Cargo([share], [(tuple(shape), share.dtype)], 1 + dp_copies(n_dp), run)


def rows_dp(array, n_dp, upper=True):
    def run(ship, ins, outs):
        view = lambda i: outs[0].at[i]
        only = ship.h >= int(upper)
        k = ship.slots(1)

        @pl.when(only)
        def _():
            ship.near(ins[0], view(ship.d), k).start()

        yield from dp_steps(ship, view, first=ins[0], only=only)

        @pl.when(only)
        def _():
            ship.near(ins[0], view(ship.d), k).wait()

    return Cargo([array], [((n_dp,) + array.shape, array.dtype)], 1 + dp_copies(n_dp), run)


def spread_cargo(array, n_dp, n_tensor):
    block = array.shape[0] // CAP
    model = array.shape[1]

    def run(ship, ins, outs):
        source = ins[0]
        item, third = outs
        t, d = ship.t, ship.d
        base = ship.slots(4)

        def block_copy(i, start):
            b = CAP * t + i
            j = b % n_tensor
            target = jnp.where(b >= n_tensor, ship.width, 0) + j // 2
            at = j % 2
            rows = step(source, i * block, block)
            for kind in range(2):
                here = b >= 2 * n_tensor if kind else b < 2 * n_tensor
                into = step(third.at[d] if kind else item, at * block, block)

                @pl.when(here & (target == t))
                def _():
                    c = ship.near(rows, into, base + i)
                    c.start() if start else c.wait()

                @pl.when(here & (target != t))
                def _():
                    c = ship.far(rows, into, "tensor", target, base + i, base + 2 * kind + at)
                    c.start() if start else c.wait_send()

        def wait_place(kind, at):
            b = (2 if kind else ship.h) * n_tensor + 2 * ship.q + at

            @pl.when(b // CAP != t)
            def _():
                into = step(third.at[d] if kind else item, at * block, block)
                ship.far(into, into, "tensor", t, base, base + 2 * kind + at).wait_recv()

        for i in reversed(range(CAP)):
            block_copy(i, True)
        yield
        for i in range(CAP):
            block_copy(i, False)
        only = ship.h == 1

        @pl.when(only)
        def _():
            for at in range(2):
                wait_place(1, at)

        yield from dp_steps(ship, lambda i: third.at[i], only=only)
        for at in range(2):
            wait_place(0, at)

    outputs = [((2 * block, model), array.dtype), ((n_dp, 2 * block, model), array.dtype)]
    return Cargo([array], outputs, 4 + dp_copies(n_dp), run)


def return_cargo(item, third, n_tensor):
    block = item.shape[0] // 2
    model = item.shape[1]

    def run(ship, ins, outs):
        t = ship.t
        base = ship.slots(4)

        def send(kind, at, start):
            b = (2 if kind else ship.h) * n_tensor + 2 * ship.q + at
            target, i = b // CAP, b % CAP
            rows = step(ins[kind], at * block, block)
            into = step(outs[0], i * block, block)

            @pl.when(target == t)
            def _():
                c = ship.near(rows, into, base + 2 * kind + at)
                c.start() if start else c.wait()

            @pl.when(target != t)
            def _():
                c = ship.far(rows, into, "tensor", target, base + 2 * kind + at, base + i)
                c.start() if start else c.wait_send()

        def all_sends(start):
            for at in range(2):
                send(0, at, start)

            @pl.when(ship.h == 1)
            def _():
                for at in range(2):
                    send(1, at, start)

        all_sends(True)
        yield
        for i in range(CAP):
            b = CAP * t + i
            holder = jnp.where(b >= n_tensor, ship.width, 0) + (b % n_tensor) // 2

            @pl.when(holder != t)
            def _():
                into = step(outs[0], i * block, block)
                ship.far(into, into, "tensor", t, base, base + i).wait_recv()

        all_sends(False)

    return Cargo([item, third], [((CAP * block, model), item.dtype)], 4, run)


def exchange(
    cid,
    n_dp,
    n_tensor,
    rows,
    model,
    inputs=(),
    outputs=(),
    middle=None,
    scatter=False,
    gather=False,
    cargo=(),
    vmem_mib=40,
):
    width = n_tensor // 2
    half = rows // 2
    pieces = [(o, hs) for o in range(1, width) for hs in range(2)]
    number = {piece: k for k, piece in enumerate(pieces)}
    bits = bits_of(width)

    def last_bit(piece):
        return top_bit(piece[0]) if piece[1] == 0 else low_bit(piece[0])

    def incoming(piece):
        return [p for p in pieces if p[1] == piece[1] and p[0] ^ last_bit(p) == piece[0]]

    scatter_order = sorted(pieces, key=lambda p: (-popcount(p[0]), len(incoming(p)), p[0]))
    gather_order = sorted(
        pieces, key=lambda p: (popcount(p[0]), p[1] if last_bit(p) != bits[-1] else 1 - p[1])
    )
    n_in, n_out = len(inputs), len(outputs)
    carried = [array for c in cargo for array in c.inputs]
    landed = [shape for c in cargo for shape in c.outputs]
    cargo_copies = max(sum(c.count for c in cargo), 1)

    def kernel(*refs):
        rest = list(refs)

        def take(count):
            taken = rest[:count]
            del rest[:count]
            return taken

        ins, cargo_ins, outs, cargo_outs = take(n_in), take(len(carried)), take(n_out), take(len(landed))
        gathered = rest.pop(0) if gather else None
        ship = Ship(n_dp, n_tensor, *take(3))
        own = rest.pop(0)
        local_sem = rest.pop(0)
        if scatter:
            arrived, s_send, s_recv = rest.pop(0), rest.pop(0), rest.pop(0)
        if gather:
            g_send, g_recv = rest.pop(0), rest.pop(0)
        t, d = ship.t, ship.d
        barrier = pltpu.get_barrier_semaphore()
        greeted = [("tensor", (t + k) % n_tensor) for k in range(1, n_tensor)]
        greeted += [("dp", partner(d, bit)) for bit in bits_of(n_dp)]
        for axis, place in greeted:
            pl.semaphore_signal(
                barrier, inc=1, device_id={axis: place}, device_id_type=pl.DeviceIdType.MESH
            )
        pl.semaphore_wait(barrier, len(greeted))

        stages = []
        for c in cargo:
            c_ins, cargo_ins = cargo_ins[: len(c.inputs)], cargo_ins[len(c.inputs) :]
            c_outs, cargo_outs = cargo_outs[: len(c.outputs)], cargo_outs[len(c.outputs) :]
            stages.append(c.run(ship, c_ins, c_outs))
        for stage in stages:
            next(stage)

        if scatter:
            part = ins[0]
            copies = {}
            for piece in scatter_order:
                o, hs = piece
                came = incoming(piece)
                base = o * rows + hs * half
                for p in came:
                    copies[p].wait_recv()
                source = step(part, base, half)
                if came:
                    source = arrived.at[number[came[0]]]

                    def add(r, base=base, came=came):
                        total = part[pl.ds(base + r, ROW_TILE)].astype(f32)
                        for p in came:
                            total = total + arrived[number[p], pl.ds(r, ROW_TILE)].astype(f32)
                        arrived[number[came[0]], pl.ds(r, ROW_TILE)] = total.astype(bf16)

                    row_tiles(half, add)
                k = number[piece]
                copies[piece] = pltpu.make_async_remote_copy(
                    src_ref=source,
                    dst_ref=arrived.at[k],
                    send_sem=s_send.at[k],
                    recv_sem=s_recv.at[k],
                    device_id={"tensor": partner(t, last_bit(piece))},
                    device_id_type=pl.DeviceIdType.MESH,
                )
                copies[piece].start()
            for piece in pieces:
                if popcount(piece[0]) == 1:
                    copies[piece].wait_recv()

        def summed(hs, r):
            total = ins[0][pl.ds(hs * half + r, ROW_TILE)].astype(f32)
            for bit in bits:
                total = total + arrived[number[(bit, hs)], pl.ds(r, ROW_TILE)].astype(f32)
            return total

        if middle is not None:
            middle(half, summed, ins, outs, own)

        if gather:
            keep = pltpu.make_async_copy(own, step(gathered, 0, rows), local_sem)
            keep.start()
            sent = {}
            for piece in gather_order:
                o, hs = piece
                bit = last_bit(piece)
                before = o ^ bit
                if before:
                    sent[(before, hs)].wait_recv()
                    source = step(gathered, before * rows + hs * half, half)
                else:
                    source = step(own, hs * half, half)
                k = number[piece]
                sent[piece] = pltpu.make_async_remote_copy(
                    src_ref=source,
                    dst_ref=step(gathered, o * rows + hs * half, half),
                    send_sem=g_send.at[k],
                    recv_sem=g_recv.at[k],
                    device_id={"tensor": partner(t, bit)},
                    device_id_type=pl.DeviceIdType.MESH,
                )
                sent[piece].start()
        while stages:
            stages = [stage for stage in stages if next(stage, stage) is not stage]
        if gather:
            used = {(p[0] ^ last_bit(p), p[1]) for p in pieces if p[0] ^ last_bit(p)}
            for piece in pieces:
                if piece not in used:
                    sent[piece].wait_recv()
            keep.wait()
            for piece in pieces:
                sent[piece].wait_send()
        if scatter:
            for piece in pieces:
                copies[piece].wait_send()

    vmem = pl.BlockSpec(memory_space=pltpu.VMEM)
    anywhere = pl.BlockSpec(memory_space=pl.ANY)
    shapes = [jax.ShapeDtypeStruct(*o) for o in list(outputs) + landed]
    specs = [vmem] * n_out + [anywhere] * len(landed)
    if gather:
        shapes.append(jax.ShapeDtypeStruct((width * rows, model), bf16))
        specs.append(anywhere)
    scratch = [pltpu.SemaphoreType.DMA((cargo_copies,)) for _ in range(3)]
    scratch += [pltpu.VMEM((rows, model), bf16), pltpu.SemaphoreType.DMA]
    count = len(pieces)
    if scatter:
        scratch += [
            pltpu.VMEM((count, half, model), bf16),
            pltpu.SemaphoreType.DMA((count,)),
            pltpu.SemaphoreType.DMA((count,)),
        ]
    if gather:
        scratch += [pltpu.SemaphoreType.DMA((count,)), pltpu.SemaphoreType.DMA((count,))]
    results = pl.pallas_call(
        kernel,
        out_shape=shapes,
        in_specs=[vmem] * n_in + [anywhere] * len(carried),
        out_specs=specs,
        scratch_shapes=scratch,
        compiler_params=pltpu.CompilerParams(
            collective_id=cid, has_side_effects=True, vmem_limit_bytes=vmem_mib << 20
        ),
        name=f"exchange_{cid}",
    )(*inputs, *carried)
    plain, rest = list(results[:n_out]), list(results[n_out:])
    if gather:
        plain.append(rest.pop())
    brought = []
    for c in cargo:
        brought.append(rest[: len(c.outputs)])
        rest = rest[len(c.outputs) :]
    return plain, brought


def norm_tile(values):
    centre = values - jnp.mean(values, -1, keepdims=True)
    scale_inv = lax.rsqrt(jnp.mean(centre * centre, -1, keepdims=True) + epsilon)
    return centre * scale_inv, scale_inv


def norm_back_tile(grad_out, normed, scale_inv, gain):
    grad_normed = grad_out * gain
    centred = grad_normed - jnp.mean(grad_normed, -1, keepdims=True)
    return scale_inv * (centred - normed * jnp.mean(grad_normed * normed, -1, keepdims=True))


def each_tile(half, body):
    for hs in range(2):
        row_tiles(half, lambda r, hs=hs: body(hs, r, pl.ds(hs * half + r, ROW_TILE)))


def fold(values):
    return jnp.sum(values.reshape(-1, 8, values.shape[-1]), 0)


def gather_middle(half, summed, ins, outs, own):
    def body(hs, r, at):
        own[at] = ins[0][at]

    each_tile(half, body)


def first_middle(half, summed, ins, outs, own):
    _, tokens, b_out, gain, shift = ins

    def body(hs, r, at):
        first = deep_alpha * tokens[at].astype(f32) + (summed(hs, r) + b_out[...])
        outs[0][at] = first
        normed, _ = norm_tile(first)
        own[at] = (normed * gain[...] + shift[...]).astype(bf16)

    each_tile(half, body)


def second_middle(half, summed, ins, outs, own):
    _, first_sum, cotangent, b_down, gain_one, shift_one, gain_two, shift_two = ins
    layer_rows, grad_second, sums = outs
    sums[...] = jnp.zeros_like(sums)

    def body(hs, r, at):
        normed, _ = norm_tile(first_sum[at])
        hidden = normed * gain_one[...] + shift_one[...]
        second = deep_alpha * hidden + (summed(hs, r) + b_down[...])
        normed, inv = norm_tile(second)
        layer_rows[at] = (normed * gain_two[...] + shift_two[...]).astype(bf16)
        grad = cotangent[at].astype(f32)
        back = norm_back_tile(grad, normed, inv, gain_two[...])
        grad_second[at] = back
        own[at] = back.astype(bf16)
        sums[0] += fold(grad * normed)
        sums[1] += fold(grad)
        sums[2] += fold(back)

    each_tile(half, body)


def third_middle(half, summed, ins, outs, own):
    _, first_sum, grad_second, gain_one = ins
    grad_first, sums = outs
    sums[...] = jnp.zeros_like(sums)

    def body(hs, r, at):
        normed, inv = norm_tile(first_sum[at])
        grad = summed(hs, r) + deep_alpha * grad_second[at]
        back = norm_back_tile(grad, normed, inv, gain_one[...])
        grad_first[at] = back
        own[at] = back.astype(bf16)
        sums[0] += fold(grad * normed)
        sums[1] += fold(grad)
        sums[2] += fold(back)

    each_tile(half, body)


def last_middle(half, summed, ins, outs, own):
    _, grad_first = ins

    def body(hs, r, at):
        outs[0][at] = (summed(hs, r) + deep_alpha * grad_first[at]).astype(bf16)

    each_tile(half, body)


def pick(index, values):
    out = values[0]
    for k, value in enumerate(values[1:], 1):
        out = jnp.where(index == k, value, out)
    return out


def across(value, n_dp):
    got = {0: value}
    for bit in reversed(bits_of(n_dp)):
        for offset in list(got):
            got[offset | bit] = permute(got[offset], "dp", n_dp, bit)
    return [got[offset] for offset in range(n_dp)]


def turn(vectors, cos_table, sin_table):
    return vectors * cos_table + pltpu.roll(vectors, HD // 2, 1) * sin_table


def score_tile(queries, keys, base, key_at, prefix_len):
    scores = lax.dot_general(
        queries, keys, (((1,), (1,)), ((), ())), preferred_element_type=f32
    ) * HD ** (-0.5)
    query_at = base + lax.broadcasted_iota(jnp.int32, (queries.shape[0], 1), 0)
    allowed = (key_at < prefix_len) | (key_at <= query_at)
    return jnp.where(allowed, scores, negative)


def attend_kernel(
    heads, rows, place, own, other, bias, cos_table, sin_table, key_at, turned, context
):
    prefix_len = place[0]
    size = heads * HD
    for head in range(heads):
        for c in range(3):
            at = pl.ds(c * size + head * HD, HD)
            p, local = divmod(head, heads // 2)
            came = pl.ds(local * HD, HD)
            value = (own, other)[p][c, :, came] + bias[p, c : c + 1, came]
            if c < 2:
                value = turn(value, cos_table[...], sin_table[...])
            turned[:, at] = value.astype(bf16)
    for head in range(heads):
        at = head * HD

        def one_block(i, carry, at=at):
            run = pl.ds(pl.multiple_of(i * rows, rows), rows)
            scores = score_tile(
                turned[run, at : at + HD],
                turned[:, size + at : size + at + HD],
                place[1 + i],
                key_at[...],
                prefix_len,
            )
            raw = jnp.exp(scores - jnp.max(scores, -1, keepdims=True))
            weights = (raw / jnp.sum(raw, -1, keepdims=True)).astype(bf16)
            context[run, at : at + HD] = jnp.dot(
                weights, turned[:, 2 * size + at : 2 * size + at + HD], preferred_element_type=f32
            ).astype(bf16)
            return carry

        lax.fori_loop(0, LEN // rows, one_block, 0)


def attend(linear, bias, place, cos_table, sin_table, key_at, rows):
    size = 2 * 3 * linear[0].shape[2]
    heads = size // (3 * HD)
    vmem = pl.BlockSpec(memory_space=pltpu.VMEM)
    return pl.pallas_call(
        functools.partial(attend_kernel, heads, rows),
        out_shape=[
            jax.ShapeDtypeStruct((LEN, size), bf16),
            jax.ShapeDtypeStruct((LEN, size // 3), bf16),
        ],
        in_specs=[pl.BlockSpec(memory_space=pltpu.SMEM)] + [vmem] * 6,
        out_specs=[vmem] * 2,
        compiler_params=pltpu.CompilerParams(vmem_limit_bytes=40 << 20),
        name="attend",
    )(place, *linear, bias, cos_table, sin_table, key_at)


def attend_back_kernel(
    heads, rows, place, turned, grad_context, cos_table, sin_table, key_at, own, other, dk, dv
):
    prefix_len = place[0]
    size = heads * HD
    scale = HD ** (-0.5)
    over_rows = (((0,), (0,)), ((), ()))
    over_last = (((1,), (1,)), ((), ()))
    for head in range(heads):
        at = head * HD
        p, local = divmod(head, heads // 2)
        came = pl.ds(local * HD, HD)
        grad_linear = (own, other)[p]
        dk[...] = jnp.zeros_like(dk)
        dv[...] = jnp.zeros_like(dv)

        def one_block(i, carry, at=at, grad_linear=grad_linear, came=came):
            run = pl.ds(pl.multiple_of(i * rows, rows), rows)
            queries = turned[run, at : at + HD]
            keys = turned[:, size + at : size + at + HD]
            scores = score_tile(queries, keys, place[1 + i], key_at[...], prefix_len)
            raw = jnp.exp(scores - jnp.max(scores, -1, keepdims=True))
            probs = raw / jnp.sum(raw, -1, keepdims=True)
            grad = grad_context[run, at : at + HD]
            grad_weights = lax.dot_general(
                grad,
                turned[:, 2 * size + at : 2 * size + at + HD],
                over_last,
                preferred_element_type=f32,
            )
            inner = jnp.sum(probs * grad_weights, -1, keepdims=True)
            grad_scores = (probs * (grad_weights - inner)).astype(bf16)
            dq = jnp.dot(grad_scores, keys, preferred_element_type=f32) * scale
            grad_linear[0, run, came] = turn(dq, cos_table[run], sin_table[run]).astype(bf16)
            dk[...] += lax.dot_general(grad_scores, queries, over_rows, preferred_element_type=f32)
            dv[...] += lax.dot_general(
                probs.astype(bf16), grad, over_rows, preferred_element_type=f32
            )
            return carry

        lax.fori_loop(0, LEN // rows, one_block, 0)
        grad_linear[1, :, came] = turn(dk[...] * scale, cos_table[...], sin_table[...]).astype(bf16)
        grad_linear[2, :, came] = dv[...].astype(bf16)


def attend_back(turned, grad_context, place, cos_table, sin_table, key_at, rows):
    size = turned.shape[1]
    heads = size // (3 * HD)
    vmem = pl.BlockSpec(memory_space=pltpu.VMEM)
    return pl.pallas_call(
        functools.partial(attend_back_kernel, heads, rows),
        out_shape=[jax.ShapeDtypeStruct((3, LEN, size // 6), bf16)] * 2,
        in_specs=[pl.BlockSpec(memory_space=pltpu.SMEM)] + [vmem] * 5,
        out_specs=[vmem] * 2,
        scratch_shapes=[pltpu.VMEM((LEN, HD), f32), pltpu.VMEM((LEN, HD), f32)],
        compiler_params=pltpu.CompilerParams(vmem_limit_bytes=40 << 20),
        name="attend_back",
    )(place, turned, grad_context, cos_table, sin_table, key_at)


def on_device(
    n_dp,
    n_tensor,
    tokens,
    cotangent,
    w_qkv,
    b_qkv,
    w_out,
    b_out,
    gain_one,
    shift_one,
    w_gu,
    b_gu,
    w_down,
    b_down,
    gain_two,
    shift_two,
    prefix,
    span_offset,
    cluster,
):
    d = lax.axis_index("dp")
    t = lax.axis_index("tensor")
    width = n_tensor // 2
    h = t // width
    q = t % width
    rows = LEN // width
    model = tokens.shape[1]
    block = LEN // n_tensor

    counts = jnp.sum((cluster[None, :] == jnp.arange(n_dp)[:, None]).astype(jnp.int32), 1)
    spare = jnp.maximum(2 - counts, 0)
    extra = (counts == CAP).astype(jnp.int32)
    spare_before = jnp.cumsum(spare) - spare
    extra_rank = jnp.cumsum(extra) - extra

    def overflow_source(index, place):
        rank = spare_before[index] + place - counts[index]
        hit = (extra == 1) & (extra_rank == rank)
        return jnp.sum(jnp.where(hit, jnp.arange(n_dp), 0))

    source_here = overflow_source(d, h)
    source_other = overflow_source(d, 0)
    foreign = counts[d] <= h
    any_empty = jnp.any(counts == 0)
    rank_out = extra_rank[d]
    ends = spare_before + spare
    out_index = jnp.sum((ends <= rank_out).astype(jnp.int32))
    out_place = jnp.minimum(counts[out_index], 2) + rank_out - spare_before[out_index]

    def chosen(item, third):
        def with_empty(item):
            sent = permute(third[source_other], "tensor", n_tensor, width)
            return jnp.where((h == 0) & foreign, sent, item)

        item = lax.cond(any_empty, with_empty, lambda v: v, item)
        return jnp.where((h == 1) & foreign, third[source_here], item)

    def sorted_out(item, everywhere, absolute):
        third = everywhere[out_index if absolute else d ^ out_index]

        def with_empty(third):
            other = across(permute(item, "tensor", n_tensor, width), n_dp)
            return jnp.where(out_place == 0, pick(d ^ out_index, other), third)

        third = lax.cond(any_empty, with_empty, lambda v: v, third)
        return jnp.where(foreign, 0, item), jnp.where(counts[d] == CAP, third, 0)

    def flipped(array):
        return permute(array, "tensor", n_tensor, width)

    width_qkv = w_qkv.shape[2]
    width_ffn = w_gu.shape[2]
    wq = w_qkv.transpose(1, 0, 2)
    wg = w_gu.transpose(2, 1, 0)
    cut_ffn = 0 if width_ffn % n_dp == 0 else 2
    columns = jnp.arange(width_ffn)
    live_columns = [s * width_ffn + columns < FF for s in (t, t ^ width)]
    pairs = (0, 1)

    def row(vector):
        return vector.reshape(1, -1)

    def tile_of(array):
        return jnp.pad(array, ((0, 8 - array.shape[0]), (0, -array.shape[1] % 128)))

    swap = functools.partial(exchange, n_dp=n_dp, n_tensor=n_tensor, rows=rows, model=model)
    facts = jnp.stack([prefix, span_offset])

    _, (spread_tokens, (wq_other,), (facts_all,), (bq_other,), (bg_other,)) = swap(
        0,
        cargo=[
            spread_cargo(tokens, n_dp, n_tensor),
            fetch(wq, 1, n_dp),
            rows_dp(tile_of(facts), n_dp, upper=False),
            swap_cargo(tile_of(b_qkv), "tensor", width),
            swap_cargo(tile_of(b_gu), "tensor", width),
        ],
    )
    wq = [wq, wq_other]
    bq = jnp.stack([b_qkv, bq_other[:3, :width_qkv]])
    bg = [b_gu, bg_other[:2, :width_ffn]]
    facts_all = facts_all[:, :2, :CAP]
    own_tokens = chosen(*spread_tokens)
    (tokens_all,), ((wo_other,), (wg_share,)) = swap(
        1,
        inputs=[own_tokens],
        middle=gather_middle,
        gather=True,
        cargo=[fetch(w_out, 0, n_dp), send_share(wg, cut_ffn, n_dp)],
    )
    fact = jnp.where(foreign, facts_all[source_here][:, 2], jnp.where(h == 0, facts[:, 0], facts[:, 1]))
    prefix_len, span_start = fact[0], fact[1]

    starts = (q ^ jnp.arange(width)) * rows
    position = (starts[:, None] + jnp.arange(rows)[None, :]).reshape(LEN)
    placed = jnp.where(position < prefix_len, position, span_start + position - prefix_len).astype(f32)
    frequency = theta_base ** (-(jnp.arange(HD // 2).astype(f32) * 2.0 / HD))
    angles = placed[:, None] * frequency[None, :]
    cos_half, sin_half = jnp.cos(angles), jnp.sin(angles)
    cos_table = jnp.concatenate([cos_half, cos_half], 1)
    sin_table = jnp.concatenate([-sin_half, sin_half], 1)
    key_at = position[None, :].astype(jnp.int32)
    place = jnp.concatenate([prefix_len[None], starts]).astype(jnp.int32)

    def dot(a, b):
        return jnp.dot(a, b, preferred_element_type=f32)

    def sum_of(spec, a, b):
        terms = [jnp.einsum(spec, a[p], b[p], preferred_element_type=f32) for p in pairs]
        return (terms[0] + terms[1]).astype(bf16)

    wo = jnp.concatenate([w_out, wo_other], 0)
    linear = [jnp.einsum("td,cdn->ctn", tokens_all, wq[p], preferred_element_type=f32) for p in pairs]
    turned, context = attend(linear, bq, place, cos_table, sin_table, key_at, rows)
    partial_out = dot(context, wo).astype(bf16)
    full = ((rows, model), f32)
    (first_sum, hidden_all), (spread_cotangent, (wg_other,), (wd_other,)) = swap(
        2,
        inputs=[partial_out, own_tokens, row(b_out), row(gain_one), row(shift_one)],
        outputs=[full],
        middle=first_middle,
        scatter=True,
        gather=True,
        cargo=[
            spread_cargo(cotangent, n_dp, n_tensor),
            join_shares(wg_share, cut_ffn, n_dp),
            fetch(w_down, 1, n_dp),
        ],
    )
    wg = [wg, wg_other]
    wd = [w_down, wd_other]
    own_cotangent = chosen(*spread_cotangent)

    def activate(live, gate_up):
        return jnp.where(live, jax.nn.gelu(gate_up[0], approximate=True) * gate_up[1], 0.0)

    inner, pull = [], []
    for p in pairs:
        gate_up = jnp.einsum("td,ncd->ctn", hidden_all, wg[p], preferred_element_type=f32)
        activated, pull_act = jax.vjp(
            functools.partial(activate, live_columns[p]), gate_up + bg[p][:, None]
        )
        inner.append(activated.astype(bf16))
        pull.append(pull_act)
    partial_fed = sum_of("tn,nd->td", inner, wd)
    sums_shape = ((3, 8, model), f32)
    (layer_rows, grad_second, sums_two, grad_fed_all), _ = swap(
        3,
        inputs=[
            partial_fed,
            first_sum,
            own_cotangent,
            row(b_down),
            row(gain_one),
            row(shift_one),
            row(gain_two),
            row(shift_two),
        ],
        outputs=[((rows, model), bf16), full, sums_shape],
        middle=second_middle,
        scatter=True,
        gather=True,
    )

    def halve(value, axis, bit):
        part = value.shape[axis] // 2
        upper = ((d & bit) != 0).astype(jnp.int32)
        return (
            lax.dynamic_slice_in_dim(value, upper * part, part, axis),
            lax.dynamic_slice_in_dim(value, (1 - upper) * part, part, axis),
        )

    def add(a, b):
        return (a.astype(f32) + b.astype(f32)).astype(bf16)

    dp_bits = bits_of(n_dp)

    def dot_rows(a, b):
        return lax.dot_general(a, b, (((0,), (0,)), ((), ())), preferred_element_type=f32)

    def halve_first(value, axis):
        for bit in dp_bits[:-1]:
            keep, send = halve(value, axis, bit)
            value = add(keep, permute(send, "dp", n_dp, bit))
        return halve(value, axis, dp_bits[-1])

    def across_dp(value):
        return swap_cargo(value, "dp", dp_bits[-1])

    def across_pair(value):
        return swap_cargo(value, "tensor", width)

    grad_gate_up = [
        pull[p](jnp.einsum("td,nd->tn", grad_fed_all, wd[p], preferred_element_type=f32))[0].astype(bf16)
        for p in pairs
    ]

    def halve_pair(values, axis):
        halves = [halve_first(v.astype(bf16), axis) for v in values]
        return [x[0] for x in halves], [x[1] for x in halves]

    grad_w_gu = [
        jnp.einsum("td,ctn->ncd", hidden_all, grad_gate_up[p], preferred_element_type=f32)
        for p in pairs
    ]
    gu_keep, gu_send = halve_pair(grad_w_gu, cut_ffn)
    grad_w_down = [
        jnp.einsum("tn,td->nd", inner[p], grad_fed_all, preferred_element_type=f32) for p in pairs
    ]
    down_keep, down_send = halve_pair(grad_w_down, 1)
    grad_b_gu = jnp.stack([jnp.sum(grad_gate_up[p].astype(f32), 1) for p in pairs])
    partial_hidden = sum_of("ctn,ncd->td", grad_gate_up, wg)
    (grad_first, sums_one, grad_att_all), ((gu_came0,), (gu_came1,)) = swap(
        4,
        inputs=[partial_hidden, first_sum, grad_second, row(gain_one)],
        outputs=[full, sums_shape],
        middle=third_middle,
        scatter=True,
        gather=True,
        cargo=[across_dp(gu_send[0]), across_dp(gu_send[1])],
    )
    gu = add(gu_keep[0], gu_came0)
    gu_other = add(gu_keep[1], gu_came1)
    gu = add(gu, flipped(gu_other))
    down = [add(down_keep[p], permute(down_send[p], "dp", n_dp, dp_bits[-1])) for p in pairs]
    layer_everywhere = jnp.stack(across(layer_rows, n_dp))
    grad_context = lax.dot_general(
        grad_att_all, wo, (((1,), (1,)), ((), ())), preferred_element_type=f32
    ).astype(bf16)
    grad_linear = attend_back(turned, grad_context, place, cos_table, -sin_table, key_at, rows)
    grad_w_out = dot_rows(context, grad_att_all).astype(bf16).reshape(2, width_qkv, model)
    grad_w_qkv = [
        jnp.einsum("td,ctn->cdn", tokens_all, grad_linear[p], preferred_element_type=f32)
        for p in pairs
    ]
    grad_b_qkv = jnp.stack([jnp.sum(grad_linear[p].astype(f32), 1) for p in pairs])
    out_keep, out_send = halve_first(grad_w_out, 1)
    qkv_keep, qkv_send = halve_pair(grad_w_qkv, 1)
    partial_in = sum_of("ctn,cdn->td", grad_linear, wq)
    (
        (input_rows,),
        ((out_came,), (qkv_came0,), (qkv_came1,), (down_came,), (layer_out,), (gu,)),
    ) = swap(
        5,
        inputs=[partial_in, grad_first],
        outputs=[((rows, model), bf16)],
        middle=last_middle,
        scatter=True,
        cargo=[
            across_dp(out_send),
            across_dp(qkv_send[0]),
            across_dp(qkv_send[1]),
            across_pair(down[1]),
            return_cargo(*sorted_out(layer_rows, layer_everywhere, False), n_tensor),
            gather_dp(gu, cut_ffn, n_dp),
        ],
    )
    down = add(down[0], down_came)
    out = add(out_keep, out_came)
    qkv = [add(qkv_keep[0], qkv_came0), add(qkv_keep[1], qkv_came1)]
    _, ((input_everywhere,), (out_came,), (qkv_came,), (down,)) = swap(
        6,
        cargo=[
            rows_dp(input_rows, n_dp),
            across_pair(out[1]),
            across_pair(qkv[1]),
            gather_dp(down, 1, n_dp),
        ],
    )
    out = add(out[0], out_came)
    qkv = add(qkv[0], qkv_came)
    _, ((input_grad,), (out,), (qkv,)) = swap(
        7,
        cargo=[
            return_cargo(*sorted_out(input_rows, input_everywhere, True), n_tensor),
            gather_dp(out, 0, n_dp),
            gather_dp(qkv, 1, n_dp),
        ],
    )

    def reduce_small(everywhere, pair):
        for bit in dp_bits:
            everywhere, pair = jax.tree.map(
                lambda v: v + permute(v, "dp", n_dp, bit), (everywhere, pair)
            )
        own = pair[0] + flipped(pair[1])
        for bit in bits_of(n_tensor):
            everywhere = everywhere + permute(everywhere, "tensor", n_tensor, bit)
        return everywhere, own

    norm_grads = jnp.concatenate([jnp.sum(sums_one, 1), jnp.sum(sums_two, 1)])
    bias = jnp.concatenate(
        [grad_b_qkv.reshape(2, 3 * width_qkv), grad_b_gu.reshape(2, 2 * width_ffn)], 1
    )
    norm_grads, bias = reduce_small(norm_grads, bias)
    grad_b_qkv = bias[: 3 * width_qkv].reshape(3, width_qkv)
    grad_b_gu = bias[3 * width_qkv :].reshape(2, width_ffn)
    return (
        layer_out.astype(f32),
        input_grad.astype(f32),
        qkv.astype(f32).transpose(1, 0, 2),
        grad_b_qkv,
        out.astype(f32),
        norm_grads[2],
        norm_grads[0],
        norm_grads[1],
        gu.astype(f32).transpose(2, 1, 0),
        grad_b_gu,
        down.astype(f32),
        norm_grads[5],
        norm_grads[3],
        norm_grads[4],
    )


def solution(mesh):
    rows = P(("dp", "tensor"), None)
    weights = (P(None, None, "tensor"), P(None, "tensor"), P("tensor", None), P(), P(), P())
    placed_ffn = (P(None, None, "tensor"), P(None, "tensor"), P("tensor", None), P(), P(), P())
    placed = (rows, rows) + weights + placed_ffn + (P("dp"), P("dp"), P())
    n_dp, n_tensor = mesh.shape["dp"], mesh.shape["tensor"]

    def body(*arguments):
        return on_device(n_dp, n_tensor, *arguments)

    return jax.shard_map(
        body,
        mesh=mesh,
        in_specs=placed,
        out_specs=(rows, rows) + weights + placed_ffn,
        check_vma=False,
    )
```

```python
import functools
import math

import jax
import jax.numpy as jnp
from jax import lax
from jax.experimental import pallas as pl
from jax.experimental.pallas import tpu as pltpu
from jax.sharding import PartitionSpec as P

HD = 128
FF = 5461
LEN = 1024
CAP = 3

deep_alpha = math.sqrt(48.0)
epsilon = 1e-05
negative = -1e30
theta_base = 10000.0
f32 = jnp.float32
bf16 = jnp.bfloat16


def bits_of(count):
    return [1 << b for b in range(count.bit_length() - 1)]


def permute(value, axis, size, bit):
    return lax.ppermute(value, axis, [(i, i ^ bit) for i in range(size)])


def top_bit(number):
    return 1 << (number.bit_length() - 1)


def low_bit(number):
    return number & -number


def popcount(number):
    return bin(number).count("1")


def partner(t, bit):
    return t + bit - 2 * bit * ((t // bit) % 2)


def step(ref, start, count):
    return ref.at[pl.ds(start, count)]


ROW_TILE = 16
UP1, UP2, UP4, UP5 = 2, 2, 2, 2


def row_tiles(count, body):
    def run(i, carry):
        body(pl.multiple_of(i * ROW_TILE, ROW_TILE))
        return carry

    lax.fori_loop(0, count // ROW_TILE, run, 0)


class Ship:
    def __init__(self, n_dp, n_tensor, send, recv, local):
        self.n_dp, self.n_tensor = n_dp, n_tensor
        self.width = n_tensor // 2
        self.send, self.recv, self.local_sems = send, recv, local
        self.used = 0
        self.d, self.t = lax.axis_index("dp"), lax.axis_index("tensor")
        self.h, self.q = self.t // self.width, self.t % self.width

    def slots(self, count):
        self.used += count
        return self.used - count

    def far(self, source, target, axis, place, k, k_recv=None):
        return pltpu.make_async_remote_copy(
            src_ref=source,
            dst_ref=target,
            send_sem=self.send.at[k],
            recv_sem=self.recv.at[k if k_recv is None else k_recv],
            device_id={axis: place},
            device_id_type=pl.DeviceIdType.MESH,
        )

    def near(self, source, target, k):
        return pltpu.make_async_copy(source, target, self.local_sems.at[k])


def along(ref, axis, start, count):
    return ref.at[(slice(None),) * axis + (pl.ds(start, count),)]


def mixed(index, offset):
    for bit in bits_of(offset * 2):
        if offset & bit:
            index = partner(index, bit)
    return index


def dp_copies(n_dp):
    return n_dp - 1


def dp_steps(ship, view, first=None, only=None):
    base = ship.slots(dp_copies(ship.n_dp))
    guard = (lambda f: f()) if only is None else pl.when(only)
    offsets, copies = [0], []
    for bit in reversed(bits_of(ship.n_dp)):
        new = []
        for o in offsets:
            at = view(mixed(ship.d, o))
            source = first if (first is not None and o == 0) else at
            new.append(ship.far(source, at, "dp", partner(ship.d, bit), base + len(copies) + len(new)))

        @guard
        def _():
            for c in new:
                c.start()

        yield

        @guard
        def _():
            for c in new:
                c.wait_recv()

        copies += new
        offsets += [o | bit for o in offsets]

    @guard
    def _():
        for c in copies:
            c.wait_send()


class Cargo:
    def __init__(self, inputs, outputs, count, run, early=0, from_out=None):
        self.inputs, self.outputs, self.count, self.run = inputs, outputs, count, run
        self.early, self.from_out = early, from_out

    def sooner(self, count=1):
        self.early = count
        return self


def portion_bounds(part, last_axis, portion):
    if portion is None:
        return 0, part
    cut = part // 2 // 128 * 128 if last_axis else part // 2
    return ((0, cut), (cut, part))[portion]


def send_share(weight, axis, n_dp, portion=None):
    part = weight.shape[axis] // n_dp
    low, high = portion_bounds(part, axis == weight.ndim - 1, portion)
    shape = list(weight.shape)
    shape[axis] = high - low

    def run(ship, ins, outs):
        c = ship.far(
            along(ins[0], axis, ship.d * part + low, high - low),
            outs[0],
            "tensor",
            partner(ship.t, ship.width),
            ship.slots(1),
        )
        c.start()
        yield
        c.wait()

    return Cargo([weight], [(tuple(shape), weight.dtype)], 1, run)


def join_shares(weight, share, axis, n_dp, portion=None):
    part = weight.shape[axis] // n_dp
    cut = share.shape[axis]

    def run(ship, ins, outs):
        first = lambda i: along(outs[0], axis, i * part, cut)
        second = lambda i: along(outs[0], axis, i * part + cut, part - cut)
        steps = [dp_steps(ship, first, first=ins[0])]
        put = ship.near(ins[0], first(ship.d), ship.slots(1))
        put.start()
        if cut < part:
            c = ship.far(
                along(ins[1], axis, ship.d * part + cut, part - cut),
                second(ship.d),
                "tensor",
                partner(ship.t, ship.width),
                ship.slots(1),
            )
            c.start()
        next(steps[0])
        yield
        if cut < part:
            c.wait()
            steps.append(dp_steps(ship, second))
        while steps:
            steps = [g for g in steps if next(g, g) is not g]
            if steps:
                yield
        put.wait()

    inputs = [share] + ([weight] if cut < part else [])
    return Cargo(inputs, [(weight.shape, weight.dtype)], 2 + 2 * dp_copies(n_dp), run)


def fetch(weight, axis, n_dp):
    part = weight.shape[axis] // n_dp

    def run(ship, ins, outs):
        view = lambda i: along(outs[0], axis, i * part, part)
        c = ship.far(
            along(ins[0], axis, ship.d * part, part),
            view(ship.d),
            "tensor",
            partner(ship.t, ship.width),
            ship.slots(1),
        )
        c.start()
        yield
        c.wait()
        yield from dp_steps(ship, view)

    return Cargo([weight], [(weight.shape, weight.dtype)], 1 + dp_copies(n_dp), run)


def present(array):
    def run(ship, ins, outs):
        yield

    return Cargo([array], [], 0, run)


def swap_cargo(array, axis, bit):
    def run(ship, ins, outs):
        index = ship.d if axis == "dp" else ship.t
        c = ship.far(ins[0], outs[0], axis, partner(index, bit), ship.slots(1))
        c.start()
        yield
        c.wait()

    return Cargo([array], [(array.shape, array.dtype)], 1, run)


def gather_dp(share, axis, n_dp):
    part = share.shape[axis]
    shape = list(share.shape)
    shape[axis] = part * n_dp

    def run(ship, ins, outs):
        view = lambda i: along(outs[0], axis, i * part, part)
        put = ship.near(ins[0], view(ship.d), ship.slots(1))
        put.start()
        yield from dp_steps(ship, view, first=ins[0])
        put.wait()

    return Cargo([share], [(tuple(shape), share.dtype)], 1 + dp_copies(n_dp), run)


def rows_dp(array, n_dp, upper=True, from_out=None):
    def run(ship, ins, outs):
        view = lambda i: outs[0].at[i]
        only = ship.h >= int(upper)
        k = ship.slots(1)

        @pl.when(only)
        def _():
            ship.near(ins[0], view(ship.d), k).start()

        yield from dp_steps(ship, view, first=ins[0], only=only)

        @pl.when(only)
        def _():
            ship.near(ins[0], view(ship.d), k).wait()

    outputs = [((n_dp,) + array.shape, array.dtype)]
    inputs = [array] if from_out is None else []
    return Cargo(inputs, outputs, 1 + dp_copies(n_dp), run, from_out=from_out)


@functools.lru_cache
def move_plan(size):
    width = size // 2
    moves, tables = [], []
    for slot in range(CAP):
        owners = range(width if slot else 0, size if slot else width)
        room = {t: [0, 1] for t in owners}
        table = [[0, 0] for _ in range(width)]
        away = []

        def put(j, target):
            b = slot * size + j
            place = room[target].pop(0)
            table[target % width][place] = j
            moves.append((slot // 2, b // CAP, b % CAP, target, place))

        for j in range(size):
            at = (slot * size + j) // CAP
            if room.get(at):
                put(j, at)
            else:
                away.append((j, at))
        for j, at in away:
            put(j, min((t for t in owners if room[t]), key=lambda t: (popcount(t ^ at), t)))
        tables.append(table)
    return tuple(moves), tables


def at_device(t, number, body):
    pl.when(t == number)(body)


def spread_cargo(array, n_dp, n_tensor):
    block = array.shape[0] // CAP
    model = array.shape[1]
    moves, _ = move_plan(n_tensor)

    def run(ship, ins, outs):
        item, third = outs
        t, d = ship.t, ship.d
        base = ship.slots(4)

        def into(kind, place):
            return step(third.at[d] if kind else item, place * block, block)

        def copy(move):
            kind, source, i, target, place = move
            rows = step(ins[0], i * block, block)
            if source == target:
                return ship.near(rows, into(kind, place), base + i)
            return ship.far(rows, into(kind, place), "tensor", target, base + i, base + 2 * kind + place)

        def visit(chosen, action):
            for number in range(n_tensor):
                mine = [m for m in moves if chosen(m, number)]
                if mine:
                    at_device(t, number, lambda mine=mine: [action(copy(m)) for m in mine] and None)

        start, wait = (lambda c: c.start()), (lambda c: c.wait())
        came, left = (lambda c: c.wait_recv()), (lambda c: c.wait_send())
        stays = lambda m: m[1] == m[3]
        visit(lambda m, n: m[1] == n and m[0] == 1, start)
        visit(lambda m, n: m[1] == n and m[0] == 0, start)
        yield
        visit(lambda m, n: m[3] == n and m[0] == 1 and not stays(m), came)
        visit(lambda m, n: m[3] == n and m[0] == 1 and stays(m), wait)
        yield from dp_steps(ship, lambda i: third.at[i], only=ship.h == 1)
        visit(lambda m, n: m[3] == n and m[0] == 0 and not stays(m), came)
        visit(lambda m, n: m[3] == n and m[0] == 0 and stays(m), wait)
        visit(lambda m, n: m[1] == n and not stays(m), left)

    outputs = [((2 * block, model), array.dtype), ((n_dp, 2 * block, model), array.dtype)]
    return Cargo([array], outputs, 4 + dp_copies(n_dp), run)


def return_cargo(item, third, n_tensor):
    block = item.shape[0] // 2
    model = item.shape[1]
    moves, _ = move_plan(n_tensor)

    def run(ship, ins, outs):
        t = ship.t
        base = ship.slots(4)

        def copy(move):
            kind, target, i, holder, place = move
            rows = step(ins[kind], place * block, block)
            to = step(outs[0], i * block, block)
            k = base + 2 * kind + place
            if holder == target:
                return ship.near(rows, to, k)
            return ship.far(rows, to, "tensor", target, k, base + i)

        def visit(chosen, action):
            for number in range(n_tensor):
                mine = [m for m in moves if chosen(m, number)]
                if mine:
                    at_device(t, number, lambda mine=mine: [action(copy(m)) for m in mine] and None)

        stays = lambda m: m[1] == m[3]
        visit(lambda m, n: m[3] == n, lambda c: c.start())
        yield
        visit(lambda m, n: m[1] == n and not stays(m), lambda c: c.wait_recv())
        visit(lambda m, n: m[3] == n and stays(m), lambda c: c.wait())
        visit(lambda m, n: m[3] == n and not stays(m), lambda c: c.wait_send())

    return Cargo([item, third], [((CAP * block, model), item.dtype)], 4, run)


def gather_tensor(array, n_tensor, cut=False):
    share = array.shape[1] // n_tensor if cut else array.shape[1]

    def run(ship, ins, outs):
        base = ship.slots(n_tensor)
        part = lambda i: along(ins[0], 1, i * share, share) if cut else ins[0]
        put = ship.near(part(ship.t), outs[0].at[ship.t], base)
        put.start()
        others = [(k, (ship.t + k) % n_tensor) for k in range(1, n_tensor)]
        copies = [
            ship.far(part(other), outs[0].at[ship.t], "tensor", other, base + k) for k, other in others
        ]
        for c in copies:
            c.start()
        yield
        for c in copies:
            c.wait()
        put.wait()

    shape = (n_tensor, array.shape[0], share)
    return Cargo([array], [(shape, array.dtype)], n_tensor, run)


def exchange(
    cid,
    n_dp,
    n_tensor,
    rows,
    model,
    inputs=(),
    outputs=(),
    middle=None,
    scatter=False,
    gather=False,
    cargo=(),
    upper_part=2,
    vmem_mib=40,
):
    width = n_tensor // 2
    cut = rows // upper_part
    begins, sizes = (0, cut), (cut, rows - cut)
    pieces = [(o, hs) for o in range(1, width) for hs in range(2)]
    number = {piece: k for k, piece in enumerate(pieces)}
    bits = bits_of(width)

    def last_bit(piece):
        return top_bit(piece[0]) if piece[1] == 0 else low_bit(piece[0])

    def incoming(piece):
        return [p for p in pieces if p[1] == piece[1] and p[0] ^ last_bit(p) == piece[0]]

    scatter_order = sorted(pieces, key=lambda p: (-popcount(p[0]), len(incoming(p)), p[0]))
    gather_order = sorted(
        pieces, key=lambda p: (popcount(p[0]), p[1] if last_bit(p) != bits[-1] else 1 - p[1])
    )
    n_in, n_out = len(inputs), len(outputs)
    carried = [array for c in cargo for array in c.inputs]
    landed = [shape for c in cargo for shape in c.outputs]
    cargo_copies = max(sum(c.count for c in cargo), 1)

    def kernel(*refs):
        rest = list(refs)

        def take(count):
            taken = rest[:count]
            del rest[:count]
            return taken

        ins, cargo_ins, outs, cargo_outs = take(n_in), take(len(carried)), take(n_out), take(len(landed))
        gathered = rest.pop(0) if gather else None
        ship = Ship(n_dp, n_tensor, *take(3))
        own = rest.pop(0)
        local_sem = rest.pop(0)
        if scatter:
            arrived, s_send, s_recv = rest.pop(0), rest.pop(0), rest.pop(0)
        if gather:
            g_send, g_recv = rest.pop(0), rest.pop(0)
        t, d = ship.t, ship.d
        barrier = pltpu.get_barrier_semaphore()
        greeted = [("tensor", (t + k) % n_tensor) for k in range(1, n_tensor)]
        greeted += [("dp", partner(d, bit)) for bit in bits_of(n_dp)]
        for axis, place in greeted:
            pl.semaphore_signal(
                barrier, inc=1, device_id={axis: place}, device_id_type=pl.DeviceIdType.MESH
            )
        pl.semaphore_wait(barrier, len(greeted))

        stages, waiting, soon = [], [], []
        for c in cargo:
            c_ins, cargo_ins = cargo_ins[: len(c.inputs)], cargo_ins[len(c.inputs) :]
            c_outs, cargo_outs = cargo_outs[: len(c.outputs)], cargo_outs[len(c.outputs) :]
            if c.from_out is None:
                stage = c.run(ship, c_ins, c_outs)
                next(stage)
                stages.append(stage)
                soon.append([stage, c.early])
            else:
                waiting.append(c.run(ship, [outs[c.from_out]], c_outs))

        def advance():
            for entry in soon:
                if entry[1]:
                    entry[1] -= 1
                    next(entry[0])

        if scatter:
            part = ins[0]
            copies = {}
            for piece in scatter_order:
                o, hs = piece
                came = incoming(piece)
                base, half = o * rows + begins[hs], sizes[hs]
                for p in came:
                    copies[p].wait_recv()
                source = step(part, base, half)
                if came:
                    source = step(arrived.at[number[came[0]]], 0, half)

                    def add(r, base=base, came=came):
                        total = part[pl.ds(base + r, ROW_TILE)].astype(f32)
                        for p in came:
                            total = total + arrived[number[p], pl.ds(r, ROW_TILE)].astype(f32)
                        arrived[number[came[0]], pl.ds(r, ROW_TILE)] = total.astype(bf16)

                    row_tiles(half, add)
                k = number[piece]
                copies[piece] = pltpu.make_async_remote_copy(
                    src_ref=source,
                    dst_ref=step(arrived.at[k], 0, half),
                    send_sem=s_send.at[k],
                    recv_sem=s_recv.at[k],
                    device_id={"tensor": partner(t, last_bit(piece))},
                    device_id_type=pl.DeviceIdType.MESH,
                )
                copies[piece].start()
            advance()
            for piece in pieces:
                if popcount(piece[0]) == 1:
                    copies[piece].wait_recv()

        def summed(hs, r):
            total = ins[0][pl.ds(begins[hs] + r, ROW_TILE)].astype(f32)
            for bit in bits:
                total = total + arrived[number[(bit, hs)], pl.ds(r, ROW_TILE)].astype(f32)
            return total

        if middle is not None:
            middle((begins, sizes), summed, ins, outs, own)
        for stage in waiting:
            next(stage)
        stages = waiting + stages

        if gather:
            keep = pltpu.make_async_copy(own, step(gathered, 0, rows), local_sem)
            keep.start()
            sent = {}
            forwarding = False
            for piece in gather_order:
                o, hs = piece
                bit = last_bit(piece)
                before = o ^ bit
                if before and not forwarding:
                    forwarding = True
                    advance()
                if before:
                    sent[(before, hs)].wait_recv()
                    source = step(gathered, before * rows + begins[hs], sizes[hs])
                else:
                    source = step(own, begins[hs], sizes[hs])
                k = number[piece]
                sent[piece] = pltpu.make_async_remote_copy(
                    src_ref=source,
                    dst_ref=step(gathered, o * rows + begins[hs], sizes[hs]),
                    send_sem=g_send.at[k],
                    recv_sem=g_recv.at[k],
                    device_id={"tensor": partner(t, bit)},
                    device_id_type=pl.DeviceIdType.MESH,
                )
                sent[piece].start()
        while stages:
            stages = [stage for stage in stages if next(stage, stage) is not stage]
        if gather:
            used = {(p[0] ^ last_bit(p), p[1]) for p in pieces if p[0] ^ last_bit(p)}
            for piece in pieces:
                if piece not in used:
                    sent[piece].wait_recv()
            keep.wait()
            for piece in pieces:
                sent[piece].wait_send()
        if scatter:
            for piece in pieces:
                copies[piece].wait_send()

    vmem = pl.BlockSpec(memory_space=pltpu.VMEM)
    anywhere = pl.BlockSpec(memory_space=pl.ANY)
    shapes = [jax.ShapeDtypeStruct(*o) for o in list(outputs) + landed]
    specs = [vmem] * n_out + [anywhere] * len(landed)
    if gather:
        shapes.append(jax.ShapeDtypeStruct((width * rows, model), bf16))
        specs.append(anywhere)
    scratch = [pltpu.SemaphoreType.DMA((cargo_copies,)) for _ in range(3)]
    scratch += [pltpu.VMEM((rows, model), bf16), pltpu.SemaphoreType.DMA]
    count = len(pieces)
    if scatter:
        scratch += [
            pltpu.VMEM((count, max(sizes), model), bf16),
            pltpu.SemaphoreType.DMA((count,)),
            pltpu.SemaphoreType.DMA((count,)),
        ]
    if gather:
        scratch += [pltpu.SemaphoreType.DMA((count,)), pltpu.SemaphoreType.DMA((count,))]
    results = pl.pallas_call(
        kernel,
        out_shape=shapes,
        in_specs=[vmem] * n_in + [anywhere] * len(carried),
        out_specs=specs,
        scratch_shapes=scratch,
        compiler_params=pltpu.CompilerParams(
            collective_id=cid, has_side_effects=True, vmem_limit_bytes=vmem_mib << 20
        ),
        name=f"exchange_{cid}",
    )(*inputs, *carried)
    plain, rest = list(results[:n_out]), list(results[n_out:])
    if gather:
        plain.append(rest.pop())
    brought = []
    for c in cargo:
        brought.append(rest[: len(c.outputs)])
        rest = rest[len(c.outputs) :]
    return plain, brought


def norm_tile(values):
    centre = values - jnp.mean(values, -1, keepdims=True)
    scale_inv = lax.rsqrt(jnp.mean(centre * centre, -1, keepdims=True) + epsilon)
    return centre * scale_inv, scale_inv


def norm_back_tile(grad_out, normed, scale_inv, gain):
    grad_normed = grad_out * gain
    centred = grad_normed - jnp.mean(grad_normed, -1, keepdims=True)
    return scale_inv * (centred - normed * jnp.mean(grad_normed * normed, -1, keepdims=True))


def each_tile(parts, body):
    begins, sizes = parts
    for hs in range(2):
        row_tiles(sizes[hs], lambda r, hs=hs: body(hs, r, pl.ds(begins[hs] + r, ROW_TILE)))


def fold(values):
    return jnp.sum(values.reshape(-1, 8, values.shape[-1]), 0)


def gather_middle(parts, summed, ins, outs, own):
    def body(hs, r, at):
        own[at] = ins[0][at]

    each_tile(parts, body)


def first_middle(parts, summed, ins, outs, own):
    _, tokens, b_out, gain, shift = ins

    def body(hs, r, at):
        first = deep_alpha * tokens[at].astype(f32) + (summed(hs, r) + b_out[...])
        outs[0][at] = first
        normed, _ = norm_tile(first)
        own[at] = (normed * gain[...] + shift[...]).astype(bf16)

    each_tile(parts, body)


def second_middle(parts, summed, ins, outs, own):
    _, first_sum, cotangent, b_down, gain_one, shift_one, gain_two, shift_two = ins
    layer_rows, grad_second, sums = outs
    sums[...] = jnp.zeros_like(sums)

    def body(hs, r, at):
        normed, _ = norm_tile(first_sum[at])
        hidden = normed * gain_one[...] + shift_one[...]
        second = deep_alpha * hidden + (summed(hs, r) + b_down[...])
        normed, inv = norm_tile(second)
        layer_rows[at] = (normed * gain_two[...] + shift_two[...]).astype(bf16)
        grad = cotangent[at].astype(f32)
        back = norm_back_tile(grad, normed, inv, gain_two[...])
        grad_second[at] = back
        own[at] = back.astype(bf16)
        sums[0] += fold(grad * normed)
        sums[1] += fold(grad)
        sums[2] += fold(back)

    each_tile(parts, body)


def third_middle(parts, summed, ins, outs, own):
    _, first_sum, grad_second, gain_one = ins
    grad_first, sums = outs
    sums[...] = jnp.zeros_like(sums)

    def body(hs, r, at):
        normed, inv = norm_tile(first_sum[at])
        grad = summed(hs, r) + deep_alpha * grad_second[at]
        back = norm_back_tile(grad, normed, inv, gain_one[...])
        grad_first[at] = back
        own[at] = back.astype(bf16)
        sums[0] += fold(grad * normed)
        sums[1] += fold(grad)
        sums[2] += fold(back)

    each_tile(parts, body)


def last_middle(parts, summed, ins, outs, own):
    _, grad_first = ins

    def body(hs, r, at):
        outs[0][at] = (summed(hs, r) + deep_alpha * grad_first[at]).astype(bf16)

    each_tile(parts, body)


def pick(index, values):
    out = values[0]
    for k, value in enumerate(values[1:], 1):
        out = jnp.where(index == k, value, out)
    return out


def across(value, n_dp):
    got = {0: value}
    for bit in reversed(bits_of(n_dp)):
        for offset in list(got):
            got[offset | bit] = permute(got[offset], "dp", n_dp, bit)
    return [got[offset] for offset in range(n_dp)]


def turn(vectors, cos_table, sin_table):
    return vectors * cos_table + pltpu.roll(vectors, HD // 2, 1) * sin_table


def score_tile(queries, keys, query_at, key_at, prefix_len):
    scores = lax.dot_general(
        queries, keys, (((1,), (1,)), ((), ())), preferred_element_type=f32
    ) * HD ** (-0.5)
    allowed = (key_at < prefix_len) | (key_at <= query_at)
    return jnp.where(allowed, scores, negative)


def attend_kernel(
    heads, rows, place, own, other, bias, cos_table, sin_table, key_at, query_at, turned, context
):
    prefix_len = place[0]
    size = heads * HD
    for head in range(heads):
        for c in range(3):
            at = pl.ds(c * size + head * HD, HD)
            p, local = divmod(head, heads // 2)
            came = pl.ds(local * HD, HD)
            value = (own, other)[p][c, :, came] + bias[p, c : c + 1, came]
            if c < 2:
                value = turn(value, cos_table[...], sin_table[...])
            turned[:, at] = value.astype(bf16)
    for head in range(heads):
        at = head * HD

        def one_block(i, carry, at=at):
            run = pl.ds(pl.multiple_of(i * rows, rows), rows)
            scores = score_tile(
                turned[run, at : at + HD],
                turned[:, size + at : size + at + HD],
                query_at[run],
                key_at[...],
                prefix_len,
            )
            raw = jnp.exp(scores - jnp.max(scores, -1, keepdims=True))
            weights = (raw / jnp.sum(raw, -1, keepdims=True)).astype(bf16)
            context[run, at : at + HD] = jnp.dot(
                weights, turned[:, 2 * size + at : 2 * size + at + HD], preferred_element_type=f32
            ).astype(bf16)
            return carry

        lax.fori_loop(0, LEN // rows, one_block, 0)


def attend(linear, bias, place, cos_table, sin_table, key_at, query_at, rows):
    size = 2 * 3 * linear[0].shape[2]
    heads = size // (3 * HD)
    vmem = pl.BlockSpec(memory_space=pltpu.VMEM)
    return pl.pallas_call(
        functools.partial(attend_kernel, heads, rows),
        out_shape=[
            jax.ShapeDtypeStruct((LEN, size), bf16),
            jax.ShapeDtypeStruct((LEN, size // 3), bf16),
        ],
        in_specs=[pl.BlockSpec(memory_space=pltpu.SMEM)] + [vmem] * 7,
        out_specs=[vmem] * 2,
        compiler_params=pltpu.CompilerParams(vmem_limit_bytes=40 << 20),
        name="attend",
    )(place, *linear, bias, cos_table, sin_table, key_at, query_at)


def attend_back_kernel(
    heads,
    rows,
    place,
    turned,
    grad_context,
    cos_table,
    sin_table,
    key_at,
    query_at,
    own,
    other,
    dk,
    dv,
):
    prefix_len = place[0]
    size = heads * HD
    scale = HD ** (-0.5)
    over_rows = (((0,), (0,)), ((), ()))
    over_last = (((1,), (1,)), ((), ()))
    for head in range(heads):
        at = head * HD
        p, local = divmod(head, heads // 2)
        came = pl.ds(local * HD, HD)
        grad_linear = (own, other)[p]
        dk[...] = jnp.zeros_like(dk)
        dv[...] = jnp.zeros_like(dv)

        def one_block(i, carry, at=at, grad_linear=grad_linear, came=came):
            run = pl.ds(pl.multiple_of(i * rows, rows), rows)
            queries = turned[run, at : at + HD]
            keys = turned[:, size + at : size + at + HD]
            scores = score_tile(queries, keys, query_at[run], key_at[...], prefix_len)
            raw = jnp.exp(scores - jnp.max(scores, -1, keepdims=True))
            probs = raw / jnp.sum(raw, -1, keepdims=True)
            grad = grad_context[run, at : at + HD]
            grad_weights = lax.dot_general(
                grad,
                turned[:, 2 * size + at : 2 * size + at + HD],
                over_last,
                preferred_element_type=f32,
            )
            inner = jnp.sum(probs * grad_weights, -1, keepdims=True)
            grad_scores = (probs * (grad_weights - inner)).astype(bf16)
            dq = jnp.dot(grad_scores, keys, preferred_element_type=f32) * scale
            grad_linear[0, run, came] = turn(dq, cos_table[run], sin_table[run]).astype(bf16)
            dk[...] += lax.dot_general(grad_scores, queries, over_rows, preferred_element_type=f32)
            dv[...] += lax.dot_general(
                probs.astype(bf16), grad, over_rows, preferred_element_type=f32
            )
            return carry

        lax.fori_loop(0, LEN // rows, one_block, 0)
        grad_linear[1, :, came] = turn(dk[...] * scale, cos_table[...], sin_table[...]).astype(bf16)
        grad_linear[2, :, came] = dv[...].astype(bf16)


def attend_back(turned, grad_context, place, cos_table, sin_table, key_at, query_at, rows):
    size = turned.shape[1]
    heads = size // (3 * HD)
    vmem = pl.BlockSpec(memory_space=pltpu.VMEM)
    return pl.pallas_call(
        functools.partial(attend_back_kernel, heads, rows),
        out_shape=[jax.ShapeDtypeStruct((3, LEN, size // 6), bf16)] * 2,
        in_specs=[pl.BlockSpec(memory_space=pltpu.SMEM)] + [vmem] * 6,
        out_specs=[vmem] * 2,
        scratch_shapes=[pltpu.VMEM((LEN, HD), f32), pltpu.VMEM((LEN, HD), f32)],
        compiler_params=pltpu.CompilerParams(vmem_limit_bytes=40 << 20),
        name="attend_back",
    )(place, turned, grad_context, cos_table, sin_table, key_at, query_at)


def interleave_kernel(gate, up, out):
    out[:, 0, :] = gate[...].astype(f32)
    out[:, 1, :] = up[...].astype(f32)


def interleave(gate, up):
    count, model = gate.shape
    size = 64
    block = pl.BlockSpec((size, model), lambda i: (i, 0))
    return pl.pallas_call(
        interleave_kernel,
        grid=(pl.cdiv(count, size),),
        in_specs=[block, block],
        out_specs=pl.BlockSpec((size, 2, model), lambda i: (i, 0, 0)),
        out_shape=jax.ShapeDtypeStruct((count, 2, model), f32),
        compiler_params=pltpu.CompilerParams(vmem_limit_bytes=24 << 20),
        name="interleave",
    )(gate, up)


def on_device(
    n_dp,
    n_tensor,
    tokens,
    cotangent,
    w_qkv,
    b_qkv,
    w_out,
    b_out,
    gain_one,
    shift_one,
    w_gu,
    b_gu,
    w_down,
    b_down,
    gain_two,
    shift_two,
    prefix,
    span_offset,
    cluster,
):
    d = lax.axis_index("dp")
    t = lax.axis_index("tensor")
    width = n_tensor // 2
    h = t // width
    q = t % width
    rows = LEN // width
    model = tokens.shape[1]

    counts = jnp.sum((cluster[None, :] == jnp.arange(n_dp)[:, None]).astype(jnp.int32), 1)
    spare = jnp.maximum(2 - counts, 0)
    extra = (counts == CAP).astype(jnp.int32)
    spare_before = jnp.cumsum(spare) - spare
    extra_rank = jnp.cumsum(extra) - extra

    def overflow_source(index, place):
        rank = spare_before[index] + place - counts[index]
        hit = (extra == 1) & (extra_rank == rank)
        return jnp.sum(jnp.where(hit, jnp.arange(n_dp), 0))

    source_here = overflow_source(d, h)
    source_other = overflow_source(d, 0)
    foreign = counts[d] <= h
    any_empty = jnp.any(counts == 0)
    rank_out = extra_rank[d]
    ends = spare_before + spare
    out_index = jnp.sum((ends <= rank_out).astype(jnp.int32))
    out_place = jnp.minimum(counts[out_index], 2) + rank_out - spare_before[out_index]

    def chosen(item, third):
        def with_empty(item):
            sent = permute(third[source_other], "tensor", n_tensor, width)
            return jnp.where((h == 0) & foreign, sent, item)

        item = lax.cond(any_empty, with_empty, lambda v: v, item)
        return jnp.where((h == 1) & foreign, third[source_here], item)

    def sorted_out(item, everywhere):
        third = everywhere[out_index]

        def with_empty(third):
            other = across(permute(item, "tensor", n_tensor, width), n_dp)
            return jnp.where(out_place == 0, pick(d ^ out_index, other), third)

        third = lax.cond(any_empty, with_empty, lambda v: v, third)
        return jnp.where(foreign, 0, item), jnp.where(counts[d] == CAP, third, 0)

    def flipped(array):
        return permute(array, "tensor", n_tensor, width)

    width_qkv = w_qkv.shape[2]
    width_ffn = w_gu.shape[2]
    wq = w_qkv.transpose(1, 0, 2)
    wg = w_gu.transpose(2, 1, 0)
    cut_ffn = 0 if width_ffn % n_dp == 0 else 2
    columns = jnp.arange(width_ffn)
    live_columns = [s * width_ffn + columns < FF for s in (t, t ^ width)]
    pairs = (0, 1)

    def row(vector):
        return vector.reshape(1, -1)

    def tile_of(array):
        return jnp.pad(array, ((0, 8 - array.shape[0]), (0, -array.shape[1] % 128)))

    swap = functools.partial(exchange, n_dp=n_dp, n_tensor=n_tensor, rows=rows, model=model)
    facts = jnp.stack([prefix, span_offset])

    _, (spread_tokens, (wq_share,), (facts_all,), (bq_other,), (bg_other,)) = swap(
        0,
        cargo=[
            spread_cargo(tokens, n_dp, n_tensor),
            send_share(wq, 1, n_dp, 0),
            rows_dp(tile_of(facts), n_dp, upper=False),
            swap_cargo(tile_of(b_qkv), "tensor", width),
            swap_cargo(tile_of(b_gu), "tensor", width),
        ],
    )
    bq = jnp.stack([b_qkv, bq_other[:3, :width_qkv]])
    bg = [b_gu, bg_other[:2, :width_ffn]]
    facts_all = facts_all[:, :2, :CAP]
    own_tokens = chosen(*spread_tokens)
    (tokens_all,), ((wq_other,), (wo_other,)) = swap(
        1,
        upper_part=UP1,
        inputs=[own_tokens],
        middle=gather_middle,
        gather=True,
        cargo=[
            join_shares(wq, wq_share, 1, n_dp, 1).sooner(1),
            fetch(w_out, 0, n_dp),
        ],
    )
    wq = [wq, wq_other]
    wd_part = model // n_dp
    wd_share = lax.dynamic_slice_in_dim(w_down, d * wd_part, wd_part, 1)
    wg_part = wg.shape[cut_ffn] // n_dp
    wg_low, wg_high = portion_bounds(wg_part, cut_ffn == 2, 0)
    wg_share = lax.dynamic_slice_in_dim(wg, d * wg_part + wg_low, wg_high - wg_low, cut_ffn)
    wg_share, wd_share, tokens_all = lax.optimization_barrier((wg_share, wd_share, tokens_all))
    wg_share, wd_share = flipped(wg_share), flipped(wd_share)
    fact = jnp.where(foreign, facts_all[source_here][:, 2], jnp.where(h == 0, facts[:, 0], facts[:, 1]))
    prefix_len, span_start = fact[0], fact[1]

    block = LEN // n_tensor
    tables = jnp.asarray(move_plan(n_tensor)[1], jnp.int32)
    starts = tables[jnp.where(foreign, CAP - 1, h)][q ^ jnp.arange(width)].reshape(n_tensor) * block
    position = (starts[:, None] + jnp.arange(block)[None, :]).reshape(LEN)
    placed = jnp.where(position < prefix_len, position, span_start + position - prefix_len).astype(f32)
    frequency = theta_base ** (-(jnp.arange(HD // 2).astype(f32) * 2.0 / HD))
    angles = placed[:, None] * frequency[None, :]
    cos_half, sin_half = jnp.cos(angles), jnp.sin(angles)
    cos_table = jnp.concatenate([cos_half, cos_half], 1)
    sin_table = jnp.concatenate([-sin_half, sin_half], 1)
    key_at = position[None, :].astype(jnp.int32)
    query_at = position[:, None].astype(jnp.int32)
    place = prefix_len[None].astype(jnp.int32)

    def dot(a, b):
        return jnp.dot(a, b, preferred_element_type=f32)

    def sum_of(spec, a, b):
        terms = [jnp.einsum(spec, a[p], b[p], preferred_element_type=f32) for p in pairs]
        return (terms[0] + terms[1]).astype(bf16)

    wo = jnp.concatenate([w_out, wo_other], 0)
    linear = [jnp.einsum("td,cdn->ctn", tokens_all, wq[p], preferred_element_type=f32) for p in pairs]
    turned, context = attend(linear, bq, place, cos_table, sin_table, key_at, query_at, rows)
    partial_out = dot(context, wo).astype(bf16)
    full = ((rows, model), f32)
    (first_sum, hidden_all), ((wg_other,), (wd_other,), spread_cotangent) = swap(
        2,
        upper_part=UP2,
        inputs=[partial_out, own_tokens, row(b_out), row(gain_one), row(shift_one)],
        outputs=[full],
        middle=first_middle,
        scatter=True,
        gather=True,
        cargo=[
            join_shares(wg, wg_share, cut_ffn, n_dp, 1).sooner(2),
            join_shares(w_down, wd_share, 1, n_dp).sooner(1),
            spread_cargo(cotangent, n_dp, n_tensor).sooner(2),
        ],
    )
    wg = [wg, wg_other]
    wd = [w_down, wd_other]
    own_cotangent = chosen(*spread_cotangent)

    def activate(live, gate_up):
        return jnp.where(live, jax.nn.gelu(gate_up[0], approximate=True) * gate_up[1], 0.0)

    inner, pull = [], []
    for p in pairs:
        gate_up = jnp.einsum("td,ncd->ctn", hidden_all, wg[p], preferred_element_type=f32)
        activated, pull_act = jax.vjp(
            functools.partial(activate, live_columns[p]), gate_up + bg[p][:, None]
        )
        inner.append(activated.astype(bf16))
        pull.append(pull_act)
    partial_fed = sum_of("tn,nd->td", inner, wd)
    sums_shape = ((3, 8, model), f32)
    layer_shape = jax.ShapeDtypeStruct((rows, model), bf16)
    (layer_rows, grad_second, sums_two, grad_fed_all), ((layer_everywhere,),) = swap(
        3,
        inputs=[
            partial_fed,
            first_sum,
            own_cotangent,
            row(b_down),
            row(gain_one),
            row(shift_one),
            row(gain_two),
            row(shift_two),
        ],
        outputs=[((rows, model), bf16), full, sums_shape],
        middle=second_middle,
        scatter=True,
        gather=True,
        cargo=[rows_dp(layer_shape, n_dp, from_out=0)],
    )

    def add(a, b):
        return (a.astype(f32) + b.astype(f32)).astype(bf16)

    dp_bits = bits_of(n_dp)

    share = model // n_dp

    def columns_of(array):
        return [lax.dynamic_slice_in_dim(array, (d ^ o) * share, share, 1) for o in range(n_dp)]

    def halve(columns, make, axis):
        odd = range(1, n_dp, 2)
        sent = make(jnp.concatenate([columns[o] for o in odd], 1)).astype(bf16)
        came = permute(sent, "dp", n_dp, 1)
        pieces = {}
        for k, o in enumerate(odd):
            piece = lax.slice_in_dim(came, k * share, (k + 1) * share, axis=axis)
            pieces[o - 1] = (make(columns[o - 1]) + piece.astype(f32)).astype(bf16)
        for bit in dp_bits[1:-1]:
            for o in [o for o in pieces if o & bit]:
                pieces[o ^ bit] = add(pieces[o ^ bit], permute(pieces.pop(o), "dp", n_dp, bit))
        return pieces[0], pieces[dp_bits[-1]]

    def across_dp(value):
        return swap_cargo(value, "dp", dp_bits[-1])

    def across_pair(value):
        return swap_cargo(value, "tensor", width)

    grad_gate_up = [
        pull[p](jnp.einsum("td,nd->tn", grad_fed_all, wd[p], preferred_element_type=f32))[0].astype(bf16)
        for p in pairs
    ]

    hidden_columns = columns_of(hidden_all)
    fed_columns = columns_of(grad_fed_all)

    def ein(spec, a):
        return lambda b: jnp.einsum(spec, a, b, preferred_element_type=f32)

    down_keep, down_send = zip(*[halve(fed_columns, ein("tn,td->nd", inner[p]), 1) for p in pairs])
    gu_keep, gu_send = zip(
        *[
            halve(hidden_columns, ein("tn,td->nd", grad_gate_up[p][c]), 1)
            for p in pairs
            for c in range(2)
        ]
    )
    down = [add(down_keep[p], permute(down_send[p], "dp", n_dp, dp_bits[-1])) for p in pairs]
    grad_b_gu = jnp.stack([jnp.sum(grad_gate_up[p].astype(f32), 1) for p in pairs])
    partial_hidden = sum_of("ctn,ncd->td", grad_gate_up, wg)
    (
        (grad_first, sums_one, grad_att_all),
        (*gu_came, _),
    ) = swap(
        4,
        upper_part=UP4,
        inputs=[partial_hidden, first_sum, grad_second, row(gain_one)],
        outputs=[full, sums_shape],
        middle=third_middle,
        scatter=True,
        gather=True,
        cargo=[
            *[across_dp(v) for v in gu_send],
            present(down[1]),
        ],
    )
    down_sent, grad_att_all = lax.optimization_barrier((down[1], grad_att_all))
    down = add(down[0], flipped(down_sent))
    gu = [add(gu_keep[k], gu_came[k][0]) for k in range(4)]
    gate_came = flipped(gu[2])
    grad_context = lax.dot_general(
        grad_att_all, wo, (((1,), (1,)), ((), ())), preferred_element_type=f32
    ).astype(bf16)
    grad_linear = attend_back(
        turned, grad_context, place, cos_table, -sin_table, key_at, query_at, rows
    )
    out_keep, out_send = halve(columns_of(grad_att_all), ein("tn,td->nd", context), 1)
    token_columns = columns_of(tokens_all)
    qkv_keep, qkv_send = zip(
        *[halve(token_columns, ein("ctn,td->cdn", grad_linear[p]), 1) for p in pairs]
    )
    grad_b_qkv = jnp.stack([jnp.sum(grad_linear[p].astype(f32), 1) for p in pairs])
    partial_in = sum_of("ctn,cdn->td", grad_linear, wq)
    bias = jnp.concatenate(
        [grad_b_qkv.reshape(2, 3 * width_qkv), grad_b_gu.reshape(2, 2 * width_ffn)], 1
    )
    bias = jnp.pad(bias, ((0, 0), (0, -bias.shape[1] % model))).reshape(-1, model)
    bias_rows = bias.shape[0] // 2
    upto = lambda array: jnp.pad(array, ((0, -array.shape[0] % 8), (0, 0)))
    norm_grads = jnp.concatenate([jnp.sum(sums_one, 1), jnp.sum(sums_two, 1)])
    small = jnp.concatenate([upto(norm_grads), upto(bias[:bias_rows]), upto(bias[bias_rows:])])
    bias_at = small.shape[0] - 2 * upto(bias[:bias_rows]).shape[0]
    (
        (input_rows,),
        (
            (input_everywhere,),
            (out_came,),
            (qkv_came0,),
            (qkv_came1,),
            _,
            _,
            (up_came,),
            (small,),
        ),
    ) = swap(
        5,
        upper_part=UP5,
        inputs=[partial_in, grad_first],
        outputs=[((rows, model), bf16)],
        middle=last_middle,
        scatter=True,
        cargo=[
            rows_dp(layer_shape, n_dp, from_out=0),
            across_dp(out_send),
            across_dp(qkv_send[0]),
            across_dp(qkv_send[1]),
            present(gate_came),
            present(down),
            across_pair(gu[3]),
            rows_dp(small, n_dp, upper=False),
        ],
    )
    gate, up = add(gu[0], gate_came), add(gu[1], up_came)
    out = add(out_keep, out_came).reshape(2, width_qkv, share)
    qkv = [add(qkv_keep[0], qkv_came0), add(qkv_keep[1], qkv_came1)]
    small = jnp.sum(small, 0)
    bias_own, bias_other = jnp.split(small[bias_at:], 2)
    _, ((input_grad,), (out_came,), (qkv_came,), (gate,), (up,), (down,), (norms,), (bias_came,)) = swap(
        6,
        cargo=[
            return_cargo(*sorted_out(input_rows, input_everywhere), n_tensor),
            across_pair(out[1]),
            across_pair(qkv[1]),
            gather_dp(gate, 1, n_dp),
            gather_dp(up, 1, n_dp),
            gather_dp(down, 1, n_dp),
            gather_tensor(small[:bias_at], n_tensor, cut=True),
            swap_cargo(bias_other, "tensor", width),
        ],
    )
    bias = (bias_own + bias_came)[:bias_rows].reshape(-1)
    out = add(out[0], out_came)
    qkv = add(qkv[0], qkv_came)
    _, ((out,), (qkv,), (norms,), (layer_out,)) = swap(
        7,
        cargo=[
            gather_dp(out, 1, n_dp),
            gather_dp(qkv, 1, n_dp),
            gather_tensor(jnp.sum(norms, 0), n_tensor),
            return_cargo(*sorted_out(layer_rows, layer_everywhere), n_tensor),
        ],
    )

    norm_grads = norms.transpose(1, 0, 2).reshape(-1, model)
    grad_b_qkv = bias[: 3 * width_qkv].reshape(3, width_qkv)
    grad_b_gu = bias[3 * width_qkv : 3 * width_qkv + 2 * width_ffn].reshape(2, width_ffn)
    return (
        layer_out.astype(f32),
        input_grad.astype(f32),
        qkv.astype(f32).transpose(1, 0, 2),
        grad_b_qkv,
        out.astype(f32),
        norm_grads[2],
        norm_grads[0],
        norm_grads[1],
        interleave(gate, up).transpose(2, 1, 0),
        grad_b_gu,
        down.astype(f32),
        norm_grads[5],
        norm_grads[3],
        norm_grads[4],
    )


def solution(mesh):
    rows = P(("dp", "tensor"), None)
    weights = (P(None, None, "tensor"), P(None, "tensor"), P("tensor", None), P(), P(), P())
    placed_ffn = (P(None, None, "tensor"), P(None, "tensor"), P("tensor", None), P(), P(), P())
    placed = (rows, rows) + weights + placed_ffn + (P("dp"), P("dp"), P())
    n_dp, n_tensor = mesh.shape["dp"], mesh.shape["tensor"]

    def body(*arguments):
        return on_device(n_dp, n_tensor, *arguments)

    return jax.shard_map(
        body,
        mesh=mesh,
        in_specs=placed,
        out_specs=(rows, rows) + weights + placed_ffn,
        check_vma=False,
    )
```

```python
import functools
import math

import jax
import jax.numpy as jnp
from jax import lax
from jax.experimental import pallas as pl
from jax.experimental.pallas import tpu as pltpu
from jax.sharding import PartitionSpec as P

HD = 128
FF = 5461
LEN = 1024
CAP = 3

deep_alpha = math.sqrt(48.0)
epsilon = 1e-05
negative = -1e30
theta_base = 10000.0
f32 = jnp.float32
bf16 = jnp.bfloat16


def bits_of(count):
    return [1 << b for b in range(count.bit_length() - 1)]


def permute(value, axis, size, bit):
    return lax.ppermute(value, axis, [(i, i ^ bit) for i in range(size)])


def top_bit(number):
    return 1 << (number.bit_length() - 1)


def low_bit(number):
    return number & -number


def popcount(number):
    return bin(number).count("1")


def partner(t, bit):
    return t + bit - 2 * bit * ((t // bit) % 2)


def step(ref, start, count):
    return ref.at[pl.ds(start, count)]


ROW_TILE = 16
UP1, UP2, UP4, UP5 = 2, 2, 2, 2


def row_tiles(count, body):
    def run(i, carry):
        body(pl.multiple_of(i * ROW_TILE, ROW_TILE))
        return carry

    lax.fori_loop(0, count // ROW_TILE, run, 0)


class Ship:
    def __init__(self, n_dp, n_tensor, send, recv, local):
        self.n_dp, self.n_tensor = n_dp, n_tensor
        self.width = n_tensor // 2
        self.send, self.recv, self.local_sems = send, recv, local
        self.used = 0
        self.d, self.t = lax.axis_index("dp"), lax.axis_index("tensor")
        self.h, self.q = self.t // self.width, self.t % self.width

    def slots(self, count):
        self.used += count
        return self.used - count

    def far(self, source, target, axis, place, k, k_recv=None):
        return pltpu.make_async_remote_copy(
            src_ref=source,
            dst_ref=target,
            send_sem=self.send.at[k],
            recv_sem=self.recv.at[k if k_recv is None else k_recv],
            device_id={axis: place},
            device_id_type=pl.DeviceIdType.MESH,
        )

    def near(self, source, target, k):
        return pltpu.make_async_copy(source, target, self.local_sems.at[k])


def along(ref, axis, start, count):
    return ref.at[(slice(None),) * axis + (pl.ds(start, count),)]


def mixed(index, offset):
    for bit in bits_of(offset * 2):
        if offset & bit:
            index = partner(index, bit)
    return index


def dp_copies(n_dp):
    return n_dp - 1


def dp_steps(ship, view, first=None, only=None):
    base = ship.slots(dp_copies(ship.n_dp))
    guard = (lambda f: f()) if only is None else pl.when(only)
    offsets, copies = [0], []
    for bit in reversed(bits_of(ship.n_dp)):
        new = []
        for o in offsets:
            at = view(mixed(ship.d, o))
            source = first if (first is not None and o == 0) else at
            new.append(ship.far(source, at, "dp", partner(ship.d, bit), base + len(copies) + len(new)))

        @guard
        def _():
            for c in new:
                c.start()

        yield

        @guard
        def _():
            for c in new:
                c.wait_recv()

        copies += new
        offsets += [o | bit for o in offsets]

    @guard
    def _():
        for c in copies:
            c.wait_send()


class Cargo:
    def __init__(self, inputs, outputs, count, run, early=0, from_out=None):
        self.inputs, self.outputs, self.count, self.run = inputs, outputs, count, run
        self.early, self.from_out, self.late = early, from_out, from_out is not None

    def sooner(self, count=1):
        self.early = count
        return self

    def later(self):
        self.late = True
        return self


def portion_bounds(part, last_axis, portion):
    if portion is None:
        return 0, part
    cut = part // 2 // 128 * 128 if last_axis else part // 2
    return ((0, cut), (cut, part))[portion]


def send_share(weight, axis, n_dp, portion=None):
    part = weight.shape[axis] // n_dp
    low, high = portion_bounds(part, axis == weight.ndim - 1, portion)
    shape = list(weight.shape)
    shape[axis] = high - low

    def run(ship, ins, outs):
        c = ship.far(
            along(ins[0], axis, ship.d * part + low, high - low),
            outs[0],
            "tensor",
            partner(ship.t, ship.width),
            ship.slots(1),
        )
        c.start()
        yield
        c.wait()

    return Cargo([weight], [(tuple(shape), weight.dtype)], 1, run)


def join_shares(weight, share, axis, n_dp, portion=None):
    part = weight.shape[axis] // n_dp
    cut = share.shape[axis]

    def run(ship, ins, outs):
        first = lambda i: along(outs[0], axis, i * part, cut)
        second = lambda i: along(outs[0], axis, i * part + cut, part - cut)
        steps = [dp_steps(ship, first, first=ins[0])]
        put = ship.near(ins[0], first(ship.d), ship.slots(1))
        put.start()
        if cut < part:
            c = ship.far(
                along(ins[1], axis, ship.d * part + cut, part - cut),
                second(ship.d),
                "tensor",
                partner(ship.t, ship.width),
                ship.slots(1),
            )
            c.start()
        next(steps[0])
        yield
        if cut < part:
            c.wait()
            steps.append(dp_steps(ship, second))
        while steps:
            steps = [g for g in steps if next(g, g) is not g]
            if steps:
                yield
        put.wait()

    inputs = [share] + ([weight] if cut < part else [])
    return Cargo(inputs, [(weight.shape, weight.dtype)], 2 + 2 * dp_copies(n_dp), run)


def fetch(weight, axis, n_dp):
    part = weight.shape[axis] // n_dp

    def run(ship, ins, outs):
        view = lambda i: along(outs[0], axis, i * part, part)
        c = ship.far(
            along(ins[0], axis, ship.d * part, part),
            view(ship.d),
            "tensor",
            partner(ship.t, ship.width),
            ship.slots(1),
        )
        c.start()
        yield
        c.wait()
        yield from dp_steps(ship, view)

    return Cargo([weight], [(weight.shape, weight.dtype)], 1 + dp_copies(n_dp), run)


def present(array):
    def run(ship, ins, outs):
        yield

    return Cargo([array], [], 0, run)


def swap_cargo(array, axis, bit):
    def run(ship, ins, outs):
        index = ship.d if axis == "dp" else ship.t
        c = ship.far(ins[0], outs[0], axis, partner(index, bit), ship.slots(1))
        c.start()
        yield
        c.wait()

    return Cargo([array], [(array.shape, array.dtype)], 1, run)


def gather_dp(share, axis, n_dp):
    part = share.shape[axis]
    shape = list(share.shape)
    shape[axis] = part * n_dp

    def run(ship, ins, outs):
        view = lambda i: along(outs[0], axis, i * part, part)
        put = ship.near(ins[0], view(ship.d), ship.slots(1))
        put.start()
        yield from dp_steps(ship, view, first=ins[0])
        put.wait()

    return Cargo([share], [(tuple(shape), share.dtype)], 1 + dp_copies(n_dp), run)


def rows_dp(array, n_dp, upper=True, from_out=None):
    def run(ship, ins, outs):
        view = lambda i: outs[0].at[i]
        only = ship.h >= int(upper)
        k = ship.slots(1)

        @pl.when(only)
        def _():
            ship.near(ins[0], view(ship.d), k).start()

        yield from dp_steps(ship, view, first=ins[0], only=only)

        @pl.when(only)
        def _():
            ship.near(ins[0], view(ship.d), k).wait()

    outputs = [((n_dp,) + array.shape, array.dtype)]
    inputs = [array] if from_out is None else []
    return Cargo(inputs, outputs, 1 + dp_copies(n_dp), run, from_out=from_out)


@functools.lru_cache
def move_plan(size):
    width = size // 2
    moves, tables = [], []
    for slot in range(CAP):
        owners = range(width if slot else 0, size if slot else width)
        room = {t: [0, 1] for t in owners}
        table = [[0, 0] for _ in range(width)]
        away = []

        def put(j, target):
            b = slot * size + j
            place = room[target].pop(0)
            table[target % width][place] = j
            moves.append((slot // 2, b // CAP, b % CAP, target, place))

        for j in range(size):
            at = (slot * size + j) // CAP
            if room.get(at):
                put(j, at)
            else:
                away.append((j, at))
        for j, at in away:
            put(j, min((t for t in owners if room[t]), key=lambda t: (popcount(t ^ at), t)))
        tables.append(table)
    return tuple(moves), tables


def at_device(t, number, body):
    pl.when(t == number)(body)


def spread_cargo(array, n_dp, n_tensor):
    block = array.shape[0] // CAP
    model = array.shape[1]
    moves, _ = move_plan(n_tensor)

    def run(ship, ins, outs):
        item, third = outs
        t, d = ship.t, ship.d
        base = ship.slots(4)

        def into(kind, place):
            return step(third.at[d] if kind else item, place * block, block)

        def copy(move):
            kind, source, i, target, place = move
            rows = step(ins[0], i * block, block)
            if source == target:
                return ship.near(rows, into(kind, place), base + i)
            return ship.far(rows, into(kind, place), "tensor", target, base + i, base + 2 * kind + place)

        def visit(chosen, action):
            for number in range(n_tensor):
                mine = [m for m in moves if chosen(m, number)]
                if mine:
                    at_device(t, number, lambda mine=mine: [action(copy(m)) for m in mine] and None)

        start, wait = (lambda c: c.start()), (lambda c: c.wait())
        came, left = (lambda c: c.wait_recv()), (lambda c: c.wait_send())
        stays = lambda m: m[1] == m[3]
        visit(lambda m, n: m[1] == n and m[0] == 1, start)
        visit(lambda m, n: m[1] == n and m[0] == 0, start)
        yield
        visit(lambda m, n: m[3] == n and m[0] == 1 and not stays(m), came)
        visit(lambda m, n: m[3] == n and m[0] == 1 and stays(m), wait)
        yield from dp_steps(ship, lambda i: third.at[i], only=ship.h == 1)
        visit(lambda m, n: m[3] == n and m[0] == 0 and not stays(m), came)
        visit(lambda m, n: m[3] == n and m[0] == 0 and stays(m), wait)
        visit(lambda m, n: m[1] == n and not stays(m), left)

    outputs = [((2 * block, model), array.dtype), ((n_dp, 2 * block, model), array.dtype)]
    return Cargo([array], outputs, 4 + dp_copies(n_dp), run)


def return_cargo(item, third, n_tensor):
    block = item.shape[0] // 2
    model = item.shape[1]
    moves, _ = move_plan(n_tensor)

    def run(ship, ins, outs):
        t = ship.t
        base = ship.slots(4)

        def copy(move):
            kind, target, i, holder, place = move
            rows = step(ins[kind], place * block, block)
            to = step(outs[0], i * block, block)
            k = base + 2 * kind + place
            if holder == target:
                return ship.near(rows, to, k)
            return ship.far(rows, to, "tensor", target, k, base + i)

        def visit(chosen, action):
            for number in range(n_tensor):
                mine = [m for m in moves if chosen(m, number)]
                if mine:
                    at_device(t, number, lambda mine=mine: [action(copy(m)) for m in mine] and None)

        stays = lambda m: m[1] == m[3]
        visit(lambda m, n: m[3] == n, lambda c: c.start())
        yield
        visit(lambda m, n: m[1] == n and not stays(m), lambda c: c.wait_recv())
        visit(lambda m, n: m[3] == n and stays(m), lambda c: c.wait())
        visit(lambda m, n: m[3] == n and not stays(m), lambda c: c.wait_send())

    return Cargo([item, third], [((CAP * block, model), item.dtype)], 4, run)


def gather_tensor(array, n_tensor, cut=False):
    share = array.shape[1] // n_tensor if cut else array.shape[1]

    def run(ship, ins, outs):
        base = ship.slots(n_tensor)
        part = lambda i: along(ins[0], 1, i * share, share) if cut else ins[0]
        put = ship.near(part(ship.t), outs[0].at[ship.t], base)
        put.start()
        others = [(k, (ship.t + k) % n_tensor) for k in range(1, n_tensor)]
        copies = [
            ship.far(part(other), outs[0].at[ship.t], "tensor", other, base + k) for k, other in others
        ]
        for c in copies:
            c.start()
        yield
        for c in copies:
            c.wait()
        put.wait()

    shape = (n_tensor, array.shape[0], share)
    return Cargo([array], [(shape, array.dtype)], n_tensor, run)


def exchange(
    cid,
    n_dp,
    n_tensor,
    rows,
    model,
    inputs=(),
    outputs=(),
    middle=None,
    scatter=False,
    gather=False,
    cargo=(),
    upper_part=2,
    vmem_mib=40,
):
    width = n_tensor // 2
    cut = rows // upper_part
    begins, sizes = (0, cut), (cut, rows - cut)
    pieces = [(o, hs) for o in range(1, width) for hs in range(2)]
    number = {piece: k for k, piece in enumerate(pieces)}
    bits = bits_of(width)

    def last_bit(piece):
        return top_bit(piece[0]) if piece[1] == 0 else low_bit(piece[0])

    def incoming(piece):
        return [p for p in pieces if p[1] == piece[1] and p[0] ^ last_bit(p) == piece[0]]

    scatter_order = sorted(pieces, key=lambda p: (-popcount(p[0]), len(incoming(p)), p[0]))
    gather_order = sorted(
        pieces, key=lambda p: (popcount(p[0]), p[1] if last_bit(p) != bits[-1] else 1 - p[1])
    )
    n_in, n_out = len(inputs), len(outputs)
    carried = [array for c in cargo for array in c.inputs]
    landed = [shape for c in cargo for shape in c.outputs]
    cargo_copies = max(sum(c.count for c in cargo), 1)

    def kernel(*refs):
        rest = list(refs)

        def take(count):
            taken = rest[:count]
            del rest[:count]
            return taken

        ins, cargo_ins, outs, cargo_outs = take(n_in), take(len(carried)), take(n_out), take(len(landed))
        gathered = rest.pop(0) if gather else None
        ship = Ship(n_dp, n_tensor, *take(3))
        own = rest.pop(0)
        local_sem = rest.pop(0)
        if scatter:
            arrived, s_send, s_recv = rest.pop(0), rest.pop(0), rest.pop(0)
        if gather:
            g_send, g_recv = rest.pop(0), rest.pop(0)
        t, d = ship.t, ship.d
        barrier = pltpu.get_barrier_semaphore()
        greeted = [("tensor", (t + k) % n_tensor) for k in range(1, n_tensor)]
        greeted += [("dp", partner(d, bit)) for bit in bits_of(n_dp)]
        for axis, place in greeted:
            pl.semaphore_signal(
                barrier, inc=1, device_id={axis: place}, device_id_type=pl.DeviceIdType.MESH
            )
        pl.semaphore_wait(barrier, len(greeted))

        stages, waiting, soon = [], [], []
        for c in cargo:
            c_ins, cargo_ins = cargo_ins[: len(c.inputs)], cargo_ins[len(c.inputs) :]
            c_outs, cargo_outs = cargo_outs[: len(c.outputs)], cargo_outs[len(c.outputs) :]
            if not c.late:
                stage = c.run(ship, c_ins, c_outs)
                next(stage)
                stages.append(stage)
                soon.append([stage, c.early])
            else:
                source = c_ins if c.from_out is None else [outs[c.from_out]]
                waiting.append(c.run(ship, source, c_outs))

        def advance():
            for entry in soon:
                if entry[1]:
                    entry[1] -= 1
                    next(entry[0])

        if scatter:
            part = ins[0]
            copies = {}
            for piece in scatter_order:
                o, hs = piece
                came = incoming(piece)
                base, half = o * rows + begins[hs], sizes[hs]
                for p in came:
                    copies[p].wait_recv()
                source = step(part, base, half)
                if came:
                    source = step(arrived.at[number[came[0]]], 0, half)

                    def add(r, base=base, came=came):
                        total = part[pl.ds(base + r, ROW_TILE)].astype(f32)
                        for p in came:
                            total = total + arrived[number[p], pl.ds(r, ROW_TILE)].astype(f32)
                        arrived[number[came[0]], pl.ds(r, ROW_TILE)] = total.astype(bf16)

                    row_tiles(half, add)
                k = number[piece]
                copies[piece] = pltpu.make_async_remote_copy(
                    src_ref=source,
                    dst_ref=step(arrived.at[k], 0, half),
                    send_sem=s_send.at[k],
                    recv_sem=s_recv.at[k],
                    device_id={"tensor": partner(t, last_bit(piece))},
                    device_id_type=pl.DeviceIdType.MESH,
                )
                copies[piece].start()
            advance()
            for piece in pieces:
                if popcount(piece[0]) == 1:
                    copies[piece].wait_recv()

        def summed(hs, r):
            total = ins[0][pl.ds(begins[hs] + r, ROW_TILE)].astype(f32)
            for bit in bits:
                total = total + arrived[number[(bit, hs)], pl.ds(r, ROW_TILE)].astype(f32)
            return total

        if middle is not None:
            middle((begins, sizes), summed, ins, outs, own)
        for stage in waiting:
            next(stage)
        stages = waiting + stages

        if gather:
            keep = pltpu.make_async_copy(own, step(gathered, 0, rows), local_sem)
            keep.start()
            sent = {}
            forwarding = False
            for piece in gather_order:
                o, hs = piece
                bit = last_bit(piece)
                before = o ^ bit
                if before and not forwarding:
                    forwarding = True
                    advance()
                if before:
                    sent[(before, hs)].wait_recv()
                    source = step(gathered, before * rows + begins[hs], sizes[hs])
                else:
                    source = step(own, begins[hs], sizes[hs])
                k = number[piece]
                sent[piece] = pltpu.make_async_remote_copy(
                    src_ref=source,
                    dst_ref=step(gathered, o * rows + begins[hs], sizes[hs]),
                    send_sem=g_send.at[k],
                    recv_sem=g_recv.at[k],
                    device_id={"tensor": partner(t, bit)},
                    device_id_type=pl.DeviceIdType.MESH,
                )
                sent[piece].start()
        while stages:
            stages = [stage for stage in stages if next(stage, stage) is not stage]
        if gather:
            used = {(p[0] ^ last_bit(p), p[1]) for p in pieces if p[0] ^ last_bit(p)}
            for piece in pieces:
                if piece not in used:
                    sent[piece].wait_recv()
            keep.wait()
            for piece in pieces:
                sent[piece].wait_send()
        if scatter:
            for piece in pieces:
                copies[piece].wait_send()

    vmem = pl.BlockSpec(memory_space=pltpu.VMEM)
    anywhere = pl.BlockSpec(memory_space=pl.ANY)
    shapes = [jax.ShapeDtypeStruct(*o) for o in list(outputs) + landed]
    specs = [vmem] * n_out + [anywhere] * len(landed)
    if gather:
        shapes.append(jax.ShapeDtypeStruct((width * rows, model), bf16))
        specs.append(anywhere)
    scratch = [pltpu.SemaphoreType.DMA((cargo_copies,)) for _ in range(3)]
    scratch += [pltpu.VMEM((rows, model), bf16), pltpu.SemaphoreType.DMA]
    count = len(pieces)
    if scatter:
        scratch += [
            pltpu.VMEM((count, max(sizes), model), bf16),
            pltpu.SemaphoreType.DMA((count,)),
            pltpu.SemaphoreType.DMA((count,)),
        ]
    if gather:
        scratch += [pltpu.SemaphoreType.DMA((count,)), pltpu.SemaphoreType.DMA((count,))]
    results = pl.pallas_call(
        kernel,
        out_shape=shapes,
        in_specs=[vmem] * n_in + [anywhere] * len(carried),
        out_specs=specs,
        scratch_shapes=scratch,
        compiler_params=pltpu.CompilerParams(
            collective_id=cid, has_side_effects=True, vmem_limit_bytes=vmem_mib << 20
        ),
        name=f"exchange_{cid}",
    )(*inputs, *carried)
    plain, rest = list(results[:n_out]), list(results[n_out:])
    if gather:
        plain.append(rest.pop())
    brought = []
    for c in cargo:
        brought.append(rest[: len(c.outputs)])
        rest = rest[len(c.outputs) :]
    return plain, brought


def norm_tile(values):
    centre = values - jnp.mean(values, -1, keepdims=True)
    scale_inv = lax.rsqrt(jnp.mean(centre * centre, -1, keepdims=True) + epsilon)
    return centre * scale_inv, scale_inv


def norm_back_tile(grad_out, normed, scale_inv, gain):
    grad_normed = grad_out * gain
    centred = grad_normed - jnp.mean(grad_normed, -1, keepdims=True)
    return scale_inv * (centred - normed * jnp.mean(grad_normed * normed, -1, keepdims=True))


def each_tile(parts, body):
    begins, sizes = parts
    for hs in range(2):
        row_tiles(sizes[hs], lambda r, hs=hs: body(hs, r, pl.ds(begins[hs] + r, ROW_TILE)))


def fold(values):
    return jnp.sum(values.reshape(-1, 8, values.shape[-1]), 0)


def gather_middle(parts, summed, ins, outs, own):
    def body(hs, r, at):
        own[at] = ins[0][at]

    each_tile(parts, body)


def first_middle(parts, summed, ins, outs, own):
    _, tokens, b_out, gain, shift = ins

    def body(hs, r, at):
        first = deep_alpha * tokens[at].astype(f32) + (summed(hs, r) + b_out[...])
        outs[0][at] = first
        normed, _ = norm_tile(first)
        own[at] = (normed * gain[...] + shift[...]).astype(bf16)

    each_tile(parts, body)


def second_middle(parts, summed, ins, outs, own):
    _, first_sum, cotangent, b_down, gain_one, shift_one, gain_two, shift_two = ins
    layer_rows, grad_second, sums = outs
    sums[...] = jnp.zeros_like(sums)

    def body(hs, r, at):
        normed, _ = norm_tile(first_sum[at])
        hidden = normed * gain_one[...] + shift_one[...]
        second = deep_alpha * hidden + (summed(hs, r) + b_down[...])
        normed, inv = norm_tile(second)
        layer_rows[at] = (normed * gain_two[...] + shift_two[...]).astype(bf16)
        grad = cotangent[at].astype(f32)
        back = norm_back_tile(grad, normed, inv, gain_two[...])
        grad_second[at] = back
        own[at] = back.astype(bf16)
        sums[0] += fold(grad * normed)
        sums[1] += fold(grad)
        sums[2] += fold(back)

    each_tile(parts, body)


def third_middle(parts, summed, ins, outs, own):
    _, first_sum, grad_second, gain_one = ins
    grad_first, sums = outs
    sums[...] = jnp.zeros_like(sums)

    def body(hs, r, at):
        normed, inv = norm_tile(first_sum[at])
        grad = summed(hs, r) + deep_alpha * grad_second[at]
        back = norm_back_tile(grad, normed, inv, gain_one[...])
        grad_first[at] = back
        own[at] = back.astype(bf16)
        sums[0] += fold(grad * normed)
        sums[1] += fold(grad)
        sums[2] += fold(back)

    each_tile(parts, body)


def last_middle(parts, summed, ins, outs, own):
    _, grad_first = ins

    def body(hs, r, at):
        outs[0][at] = (summed(hs, r) + deep_alpha * grad_first[at]).astype(bf16)

    each_tile(parts, body)


def pick(index, values):
    out = values[0]
    for k, value in enumerate(values[1:], 1):
        out = jnp.where(index == k, value, out)
    return out


def across(value, n_dp):
    got = {0: value}
    for bit in reversed(bits_of(n_dp)):
        for offset in list(got):
            got[offset | bit] = permute(got[offset], "dp", n_dp, bit)
    return [got[offset] for offset in range(n_dp)]


def turn(vectors, cos_table, sin_table):
    return vectors * cos_table + pltpu.roll(vectors, HD // 2, 1) * sin_table


def score_tile(queries, keys, query_at, key_at, prefix_len):
    scores = lax.dot_general(
        queries, keys, (((1,), (1,)), ((), ())), preferred_element_type=f32
    ) * HD ** (-0.5)
    allowed = (key_at < prefix_len) | (key_at <= query_at)
    return jnp.where(allowed, scores, negative)


def attend_kernel(
    heads, rows, place, own, other, bias, cos_table, sin_table, key_at, query_at, turned, context
):
    prefix_len = place[0]
    size = heads * HD
    for head in range(heads):
        for c in range(3):
            at = pl.ds(c * size + head * HD, HD)
            p, local = divmod(head, heads // 2)
            came = pl.ds(local * HD, HD)
            value = (own, other)[p][c, :, came] + bias[p, c : c + 1, came]
            if c < 2:
                value = turn(value, cos_table[...], sin_table[...])
            turned[:, at] = value.astype(bf16)
    for head in range(heads):
        at = head * HD

        def one_block(i, carry, at=at):
            run = pl.ds(pl.multiple_of(i * rows, rows), rows)
            scores = score_tile(
                turned[run, at : at + HD],
                turned[:, size + at : size + at + HD],
                query_at[run],
                key_at[...],
                prefix_len,
            )
            raw = jnp.exp(scores - jnp.max(scores, -1, keepdims=True))
            weights = (raw / jnp.sum(raw, -1, keepdims=True)).astype(bf16)
            context[run, at : at + HD] = jnp.dot(
                weights, turned[:, 2 * size + at : 2 * size + at + HD], preferred_element_type=f32
            ).astype(bf16)
            return carry

        lax.fori_loop(0, LEN // rows, one_block, 0)


def attend(linear, bias, place, cos_table, sin_table, key_at, query_at, rows):
    size = 2 * 3 * linear[0].shape[2]
    heads = size // (3 * HD)
    vmem = pl.BlockSpec(memory_space=pltpu.VMEM)
    return pl.pallas_call(
        functools.partial(attend_kernel, heads, rows),
        out_shape=[
            jax.ShapeDtypeStruct((LEN, size), bf16),
            jax.ShapeDtypeStruct((LEN, size // 3), bf16),
        ],
        in_specs=[pl.BlockSpec(memory_space=pltpu.SMEM)] + [vmem] * 7,
        out_specs=[vmem] * 2,
        compiler_params=pltpu.CompilerParams(vmem_limit_bytes=40 << 20),
        name="attend",
    )(place, *linear, bias, cos_table, sin_table, key_at, query_at)


def attend_back_kernel(
    heads,
    rows,
    place,
    turned,
    grad_context,
    cos_table,
    sin_table,
    key_at,
    query_at,
    own,
    other,
    dk,
    dv,
):
    prefix_len = place[0]
    size = heads * HD
    scale = HD ** (-0.5)
    over_rows = (((0,), (0,)), ((), ()))
    over_last = (((1,), (1,)), ((), ()))
    for head in range(heads):
        at = head * HD
        p, local = divmod(head, heads // 2)
        came = pl.ds(local * HD, HD)
        grad_linear = (own, other)[p]
        dk[...] = jnp.zeros_like(dk)
        dv[...] = jnp.zeros_like(dv)

        def one_block(i, carry, at=at, grad_linear=grad_linear, came=came):
            run = pl.ds(pl.multiple_of(i * rows, rows), rows)
            queries = turned[run, at : at + HD]
            keys = turned[:, size + at : size + at + HD]
            scores = score_tile(queries, keys, query_at[run], key_at[...], prefix_len)
            raw = jnp.exp(scores - jnp.max(scores, -1, keepdims=True))
            probs = raw / jnp.sum(raw, -1, keepdims=True)
            grad = grad_context[run, at : at + HD]
            grad_weights = lax.dot_general(
                grad,
                turned[:, 2 * size + at : 2 * size + at + HD],
                over_last,
                preferred_element_type=f32,
            )
            inner = jnp.sum(probs * grad_weights, -1, keepdims=True)
            grad_scores = (probs * (grad_weights - inner)).astype(bf16)
            dq = jnp.dot(grad_scores, keys, preferred_element_type=f32) * scale
            grad_linear[0, run, came] = turn(dq, cos_table[run], sin_table[run]).astype(bf16)
            dk[...] += lax.dot_general(grad_scores, queries, over_rows, preferred_element_type=f32)
            dv[...] += lax.dot_general(
                probs.astype(bf16), grad, over_rows, preferred_element_type=f32
            )
            return carry

        lax.fori_loop(0, LEN // rows, one_block, 0)
        grad_linear[1, :, came] = turn(dk[...] * scale, cos_table[...], sin_table[...]).astype(bf16)
        grad_linear[2, :, came] = dv[...].astype(bf16)


def attend_back(turned, grad_context, place, cos_table, sin_table, key_at, query_at, rows):
    size = turned.shape[1]
    heads = size // (3 * HD)
    vmem = pl.BlockSpec(memory_space=pltpu.VMEM)
    return pl.pallas_call(
        functools.partial(attend_back_kernel, heads, rows),
        out_shape=[jax.ShapeDtypeStruct((3, LEN, size // 6), bf16)] * 2,
        in_specs=[pl.BlockSpec(memory_space=pltpu.SMEM)] + [vmem] * 6,
        out_specs=[vmem] * 2,
        scratch_shapes=[pltpu.VMEM((LEN, HD), f32), pltpu.VMEM((LEN, HD), f32)],
        compiler_params=pltpu.CompilerParams(vmem_limit_bytes=40 << 20),
        name="attend_back",
    )(place, turned, grad_context, cos_table, sin_table, key_at, query_at)


def interleave_kernel(gate, up, out):
    out[:, 0, :] = gate[...].astype(f32)
    out[:, 1, :] = up[...].astype(f32)


def interleave(gate, up):
    count, model = gate.shape
    size = 64
    block = pl.BlockSpec((size, model), lambda i: (i, 0))
    return pl.pallas_call(
        interleave_kernel,
        grid=(pl.cdiv(count, size),),
        in_specs=[block, block],
        out_specs=pl.BlockSpec((size, 2, model), lambda i: (i, 0, 0)),
        out_shape=jax.ShapeDtypeStruct((count, 2, model), f32),
        compiler_params=pltpu.CompilerParams(vmem_limit_bytes=24 << 20),
        name="interleave",
    )(gate, up)


def on_device(
    n_dp,
    n_tensor,
    tokens,
    cotangent,
    w_qkv,
    b_qkv,
    w_out,
    b_out,
    gain_one,
    shift_one,
    w_gu,
    b_gu,
    w_down,
    b_down,
    gain_two,
    shift_two,
    prefix,
    span_offset,
    cluster,
):
    d = lax.axis_index("dp")
    t = lax.axis_index("tensor")
    width = n_tensor // 2
    h = t // width
    q = t % width
    rows = LEN // width
    model = tokens.shape[1]

    counts = jnp.sum((cluster[None, :] == jnp.arange(n_dp)[:, None]).astype(jnp.int32), 1)
    spare = jnp.maximum(2 - counts, 0)
    extra = (counts == CAP).astype(jnp.int32)
    spare_before = jnp.cumsum(spare) - spare
    extra_rank = jnp.cumsum(extra) - extra

    def overflow_source(index, place):
        rank = spare_before[index] + place - counts[index]
        hit = (extra == 1) & (extra_rank == rank)
        return jnp.sum(jnp.where(hit, jnp.arange(n_dp), 0))

    source_here = overflow_source(d, h)
    source_other = overflow_source(d, 0)
    foreign = counts[d] <= h
    any_empty = jnp.any(counts == 0)
    rank_out = extra_rank[d]
    ends = spare_before + spare
    out_index = jnp.sum((ends <= rank_out).astype(jnp.int32))
    out_place = jnp.minimum(counts[out_index], 2) + rank_out - spare_before[out_index]

    def chosen(item, third):
        def with_empty(item):
            sent = permute(third[source_other], "tensor", n_tensor, width)
            return jnp.where((h == 0) & foreign, sent, item)

        item = lax.cond(any_empty, with_empty, lambda v: v, item)
        return jnp.where((h == 1) & foreign, third[source_here], item)

    def sorted_out(item, everywhere):
        third = everywhere[out_index]

        def with_empty(third):
            other = across(permute(item, "tensor", n_tensor, width), n_dp)
            return jnp.where(out_place == 0, pick(d ^ out_index, other), third)

        third = lax.cond(any_empty, with_empty, lambda v: v, third)
        return jnp.where(foreign, 0, item), jnp.where(counts[d] == CAP, third, 0)

    def flipped(array):
        return permute(array, "tensor", n_tensor, width)

    width_qkv = w_qkv.shape[2]
    width_ffn = w_gu.shape[2]
    wq = w_qkv.transpose(1, 0, 2)
    wg = w_gu.transpose(2, 1, 0)
    cut_ffn = 0 if width_ffn % n_dp == 0 else 2
    columns = jnp.arange(width_ffn)
    live_columns = [s * width_ffn + columns < FF for s in (t, t ^ width)]
    pairs = (0, 1)

    def row(vector):
        return vector.reshape(1, -1)

    def tile_of(array):
        return jnp.pad(array, ((0, 8 - array.shape[0]), (0, -array.shape[1] % 128)))

    swap = functools.partial(exchange, n_dp=n_dp, n_tensor=n_tensor, rows=rows, model=model)
    facts = jnp.stack([prefix, span_offset])

    _, (spread_tokens, (wq_share,), (facts_all,), (bq_other,), (bg_other,)) = swap(
        0,
        cargo=[
            spread_cargo(tokens, n_dp, n_tensor),
            send_share(wq, 1, n_dp, 0),
            rows_dp(tile_of(facts), n_dp, upper=False),
            swap_cargo(tile_of(b_qkv), "tensor", width),
            swap_cargo(tile_of(b_gu), "tensor", width),
        ],
    )
    bq = jnp.stack([b_qkv, bq_other[:3, :width_qkv]])
    bg = [b_gu, bg_other[:2, :width_ffn]]
    facts_all = facts_all[:, :2, :CAP]
    own_tokens = chosen(*spread_tokens)
    (tokens_all,), ((wq_other,), (wo_other,)) = swap(
        1,
        upper_part=UP1,
        inputs=[own_tokens],
        middle=gather_middle,
        gather=True,
        cargo=[
            join_shares(wq, wq_share, 1, n_dp, 1).sooner(1),
            fetch(w_out, 0, n_dp),
        ],
    )
    wq = [wq, wq_other]
    wd_part = model // n_dp
    wd_share = lax.dynamic_slice_in_dim(w_down, d * wd_part, wd_part, 1)
    wg_part = wg.shape[cut_ffn] // n_dp
    wg_low, wg_high = portion_bounds(wg_part, cut_ffn == 2, 0)
    wg_share = lax.dynamic_slice_in_dim(wg, d * wg_part + wg_low, wg_high - wg_low, cut_ffn)
    wg_share, wd_share, tokens_all = lax.optimization_barrier((wg_share, wd_share, tokens_all))
    wg_share, wd_share = flipped(wg_share), flipped(wd_share)
    fact = jnp.where(foreign, facts_all[source_here][:, 2], jnp.where(h == 0, facts[:, 0], facts[:, 1]))
    prefix_len, span_start = fact[0], fact[1]

    block = LEN // n_tensor
    tables = jnp.asarray(move_plan(n_tensor)[1], jnp.int32)
    starts = tables[jnp.where(foreign, CAP - 1, h)][q ^ jnp.arange(width)].reshape(n_tensor) * block
    position = (starts[:, None] + jnp.arange(block)[None, :]).reshape(LEN)
    placed = jnp.where(position < prefix_len, position, span_start + position - prefix_len).astype(f32)
    frequency = theta_base ** (-(jnp.arange(HD // 2).astype(f32) * 2.0 / HD))
    angles = placed[:, None] * frequency[None, :]
    cos_half, sin_half = jnp.cos(angles), jnp.sin(angles)
    cos_table = jnp.concatenate([cos_half, cos_half], 1)
    sin_table = jnp.concatenate([-sin_half, sin_half], 1)
    key_at = position[None, :].astype(jnp.int32)
    query_at = position[:, None].astype(jnp.int32)
    place = prefix_len[None].astype(jnp.int32)

    def dot(a, b):
        return jnp.dot(a, b, preferred_element_type=f32)

    def sum_of(spec, a, b):
        terms = [jnp.einsum(spec, a[p], b[p], preferred_element_type=f32) for p in pairs]
        return (terms[0] + terms[1]).astype(bf16)

    wo = jnp.concatenate([w_out, wo_other], 0)
    linear = [jnp.einsum("td,cdn->ctn", tokens_all, wq[p], preferred_element_type=f32) for p in pairs]
    turned, context = attend(linear, bq, place, cos_table, sin_table, key_at, query_at, rows)
    partial_out = dot(context, wo).astype(bf16)
    full = ((rows, model), f32)
    (first_sum, hidden_all), ((wg_other,), (wd_other,), spread_cotangent) = swap(
        2,
        upper_part=UP2,
        inputs=[partial_out, own_tokens, row(b_out), row(gain_one), row(shift_one)],
        outputs=[full],
        middle=first_middle,
        scatter=True,
        gather=True,
        cargo=[
            join_shares(wg, wg_share, cut_ffn, n_dp, 1).sooner(2),
            join_shares(w_down, wd_share, 1, n_dp).sooner(1),
            spread_cargo(cotangent, n_dp, n_tensor).sooner(2),
        ],
    )
    wg = [wg, wg_other]
    wd = [w_down, wd_other]
    own_cotangent = chosen(*spread_cotangent)

    def activate(live, gate_up):
        return jnp.where(live, jax.nn.gelu(gate_up[0], approximate=True) * gate_up[1], 0.0)

    inner, pull = [], []
    for p in pairs:
        gate_up = jnp.einsum("td,ncd->ctn", hidden_all, wg[p], preferred_element_type=f32)
        activated, pull_act = jax.vjp(
            functools.partial(activate, live_columns[p]), gate_up + bg[p][:, None]
        )
        inner.append(activated.astype(bf16))
        pull.append(pull_act)
    partial_fed = sum_of("tn,nd->td", inner, wd)
    sums_shape = ((3, 8, model), f32)
    layer_shape = jax.ShapeDtypeStruct((rows, model), bf16)
    (layer_rows, grad_second, sums_two, grad_fed_all), ((layer_everywhere,),) = swap(
        3,
        inputs=[
            partial_fed,
            first_sum,
            own_cotangent,
            row(b_down),
            row(gain_one),
            row(shift_one),
            row(gain_two),
            row(shift_two),
        ],
        outputs=[((rows, model), bf16), full, sums_shape],
        middle=second_middle,
        scatter=True,
        gather=True,
        cargo=[rows_dp(layer_shape, n_dp, from_out=0)],
    )

    def add(a, b):
        return (a.astype(f32) + b.astype(f32)).astype(bf16)

    dp_bits = bits_of(n_dp)

    share = model // n_dp

    def columns_of(array):
        return [lax.dynamic_slice_in_dim(array, (d ^ o) * share, share, 1) for o in range(n_dp)]

    def halve(columns, make, axis):
        odd = range(1, n_dp, 2)
        sent = make(jnp.concatenate([columns[o] for o in odd], 1)).astype(bf16)
        came = permute(sent, "dp", n_dp, 1)
        pieces = {}
        for k, o in enumerate(odd):
            piece = lax.slice_in_dim(came, k * share, (k + 1) * share, axis=axis)
            pieces[o - 1] = (make(columns[o - 1]) + piece.astype(f32)).astype(bf16)
        for bit in dp_bits[1:-1]:
            for o in [o for o in pieces if o & bit]:
                pieces[o ^ bit] = add(pieces[o ^ bit], permute(pieces.pop(o), "dp", n_dp, bit))
        return pieces[0], pieces[dp_bits[-1]]

    def across_dp(value):
        return swap_cargo(value, "dp", dp_bits[-1])

    def across_pair(value):
        return swap_cargo(value, "tensor", width)

    grad_gate_up = [
        pull[p](jnp.einsum("td,nd->tn", grad_fed_all, wd[p], preferred_element_type=f32))[0].astype(bf16)
        for p in pairs
    ]

    hidden_columns = columns_of(hidden_all)
    fed_columns = columns_of(grad_fed_all)

    def ein(spec, a):
        return lambda b: jnp.einsum(spec, a, b, preferred_element_type=f32)

    down_keep, down_send = zip(*[halve(fed_columns, ein("tn,td->nd", inner[p]), 1) for p in pairs])
    gu_keep, gu_send = zip(
        *[
            halve(hidden_columns, ein("tn,td->nd", grad_gate_up[p][c]), 1)
            for p in pairs
            for c in range(2)
        ]
    )
    down = [add(down_keep[p], permute(down_send[p], "dp", n_dp, dp_bits[-1])) for p in pairs]
    grad_b_gu = jnp.stack([jnp.sum(grad_gate_up[p].astype(f32), 1) for p in pairs])
    partial_hidden = sum_of("ctn,ncd->td", grad_gate_up, wg)
    (
        (grad_first, sums_one, grad_att_all),
        (*gu_came, _),
    ) = swap(
        4,
        upper_part=UP4,
        inputs=[partial_hidden, first_sum, grad_second, row(gain_one)],
        outputs=[full, sums_shape],
        middle=third_middle,
        scatter=True,
        gather=True,
        cargo=[
            *[across_dp(v) for v in gu_send],
            present(down[1]),
        ],
    )
    down_sent, grad_att_all = lax.optimization_barrier((down[1], grad_att_all))
    down_came = flipped(down_sent)
    gu = [add(gu_keep[k], gu_came[k][0]) for k in range(4)]
    gate_came = flipped(gu[2])
    grad_context = lax.dot_general(
        grad_att_all, wo, (((1,), (1,)), ((), ())), preferred_element_type=f32
    ).astype(bf16)
    out_keep, out_send = halve(columns_of(grad_att_all), ein("tn,td->nd", context), 1)
    out = add(out_keep, permute(out_send, "dp", n_dp, dp_bits[-1])).reshape(2, width_qkv, share)
    grad_linear = attend_back(
        turned, grad_context, place, cos_table, -sin_table, key_at, query_at, rows
    )
    down_came, *grad_linear = lax.optimization_barrier((down_came, *grad_linear))
    down = add(down[0], down_came)
    token_columns = columns_of(tokens_all)
    qkv_keep, qkv_send = zip(
        *[halve(token_columns, ein("ctn,td->cdn", grad_linear[p]), 1) for p in pairs]
    )
    grad_b_qkv = jnp.stack([jnp.sum(grad_linear[p].astype(f32), 1) for p in pairs])
    partial_in = sum_of("ctn,cdn->td", grad_linear, wq)
    bias = jnp.concatenate(
        [grad_b_qkv.reshape(2, 3 * width_qkv), grad_b_gu.reshape(2, 2 * width_ffn)], 1
    )
    bias = jnp.pad(bias, ((0, 0), (0, -bias.shape[1] % model))).reshape(-1, model)
    bias_rows = bias.shape[0] // 2
    upto = lambda array: jnp.pad(array, ((0, -array.shape[0] % 8), (0, 0)))
    norm_grads = jnp.concatenate([jnp.sum(sums_one, 1), jnp.sum(sums_two, 1)])
    small = jnp.concatenate([upto(norm_grads), upto(bias[:bias_rows]), upto(bias[bias_rows:])])
    bias_at = small.shape[0] - 2 * upto(bias[:bias_rows]).shape[0]
    (
        (input_rows,),
        (
            (input_everywhere,),
            (out_came,),
            (qkv_came0,),
            (qkv_came1,),
            _,
            _,
            (up_came,),
            (small,),
        ),
    ) = swap(
        5,
        upper_part=UP5,
        inputs=[partial_in, grad_first],
        outputs=[((rows, model), bf16)],
        middle=last_middle,
        scatter=True,
        cargo=[
            rows_dp(layer_shape, n_dp, from_out=0),
            across_pair(out[1]).later(),
            across_dp(qkv_send[0]),
            across_dp(qkv_send[1]),
            present(gate_came),
            present(down),
            across_pair(gu[3]),
            rows_dp(small, n_dp, upper=False),
        ],
    )
    gate, up = add(gu[0], gate_came), add(gu[1], up_came)
    qkv = [add(qkv_keep[0], qkv_came0), add(qkv_keep[1], qkv_came1)]
    small = jnp.sum(small, 0)
    bias_own, bias_other = jnp.split(small[bias_at:], 2)
    _, ((input_grad,), (qkv_came,), (gate,), (up,), (down,), (norms,), (bias_came,)) = swap(
        6,
        cargo=[
            return_cargo(*sorted_out(input_rows, input_everywhere), n_tensor),
            across_pair(qkv[1]),
            gather_dp(gate, 1, n_dp),
            gather_dp(up, 1, n_dp),
            gather_dp(down, 1, n_dp),
            gather_tensor(small[:bias_at], n_tensor, cut=True),
            swap_cargo(bias_other, "tensor", width),
        ],
    )
    bias = (bias_own + bias_came)[:bias_rows].reshape(-1)
    out = add(out[0], out_came)
    qkv = add(qkv[0], qkv_came)
    _, ((out,), (qkv,), (norms,), (layer_out,)) = swap(
        7,
        cargo=[
            gather_dp(out, 1, n_dp),
            gather_dp(qkv, 1, n_dp),
            gather_tensor(jnp.sum(norms, 0), n_tensor),
            return_cargo(*sorted_out(layer_rows, layer_everywhere), n_tensor),
        ],
    )

    norm_grads = norms.transpose(1, 0, 2).reshape(-1, model)
    grad_b_qkv = bias[: 3 * width_qkv].reshape(3, width_qkv)
    grad_b_gu = bias[3 * width_qkv : 3 * width_qkv + 2 * width_ffn].reshape(2, width_ffn)
    return (
        layer_out.astype(f32),
        input_grad.astype(f32),
        qkv.astype(f32).transpose(1, 0, 2),
        grad_b_qkv,
        out.astype(f32),
        norm_grads[2],
        norm_grads[0],
        norm_grads[1],
        interleave(gate, up).transpose(2, 1, 0),
        grad_b_gu,
        down.astype(f32),
        norm_grads[5],
        norm_grads[3],
        norm_grads[4],
    )


def solution(mesh):
    rows = P(("dp", "tensor"), None)
    weights = (P(None, None, "tensor"), P(None, "tensor"), P("tensor", None), P(), P(), P())
    placed_ffn = (P(None, None, "tensor"), P(None, "tensor"), P("tensor", None), P(), P(), P())
    placed = (rows, rows) + weights + placed_ffn + (P("dp"), P("dp"), P())
    n_dp, n_tensor = mesh.shape["dp"], mesh.shape["tensor"]

    def body(*arguments):
        return on_device(n_dp, n_tensor, *arguments)

    return jax.shard_map(
        body,
        mesh=mesh,
        in_specs=placed,
        out_specs=(rows, rows) + weights + placed_ffn,
        check_vma=False,
    )
```

```python
import functools
import math

import jax
import jax.numpy as jnp
from jax import lax
from jax.experimental import pallas as pl
from jax.experimental.pallas import tpu as pltpu
from jax.sharding import PartitionSpec as P

HD = 128
FF = 5461
LEN = 1024
CAP = 3

deep_alpha = math.sqrt(48.0)
epsilon = 1e-05
negative = -1e30
theta_base = 10000.0
f32 = jnp.float32
bf16 = jnp.bfloat16


def bits_of(count):
    return [1 << b for b in range(count.bit_length() - 1)]


def permute(value, axis, size, bit):
    return lax.ppermute(value, axis, [(i, i ^ bit) for i in range(size)])


def top_bit(number):
    return 1 << (number.bit_length() - 1)


def low_bit(number):
    return number & -number


def popcount(number):
    return bin(number).count("1")


def partner(t, bit):
    return t + bit - 2 * bit * ((t // bit) % 2)


def step(ref, start, count):
    return ref.at[pl.ds(start, count)]


ROW_TILE = 16
UP1, UP2, UP4, UP5 = 2, 2, 2, 2


def row_tiles(count, body):
    def run(i, carry):
        body(pl.multiple_of(i * ROW_TILE, ROW_TILE))
        return carry

    lax.fori_loop(0, count // ROW_TILE, run, 0)


class Ship:
    def __init__(self, n_dp, n_tensor, send, recv, local):
        self.n_dp, self.n_tensor = n_dp, n_tensor
        self.width = n_tensor // 2
        self.send, self.recv, self.local_sems = send, recv, local
        self.used = 0
        self.d, self.t = lax.axis_index("dp"), lax.axis_index("tensor")
        self.h, self.q = self.t // self.width, self.t % self.width

    def slots(self, count):
        self.used += count
        return self.used - count

    def far(self, source, target, axis, place, k, k_recv=None):
        return pltpu.make_async_remote_copy(
            src_ref=source,
            dst_ref=target,
            send_sem=self.send.at[k],
            recv_sem=self.recv.at[k if k_recv is None else k_recv],
            device_id={axis: place},
            device_id_type=pl.DeviceIdType.MESH,
        )

    def near(self, source, target, k):
        return pltpu.make_async_copy(source, target, self.local_sems.at[k])


def along(ref, axis, start, count):
    return ref.at[(slice(None),) * axis + (pl.ds(start, count),)]


def mixed(index, offset):
    for bit in bits_of(offset * 2):
        if offset & bit:
            index = partner(index, bit)
    return index


def dp_copies(n_dp):
    return n_dp - 1


def dp_steps(ship, view, first=None, only=None):
    base = ship.slots(dp_copies(ship.n_dp))
    guard = (lambda f: f()) if only is None else pl.when(only)
    offsets, copies = [0], []
    for bit in reversed(bits_of(ship.n_dp)):
        new = []
        for o in offsets:
            at = view(mixed(ship.d, o))
            source = first if (first is not None and o == 0) else at
            new.append(ship.far(source, at, "dp", partner(ship.d, bit), base + len(copies) + len(new)))

        @guard
        def _():
            for c in new:
                c.start()

        yield

        @guard
        def _():
            for c in new:
                c.wait_recv()

        copies += new
        offsets += [o | bit for o in offsets]

    @guard
    def _():
        for c in copies:
            c.wait_send()


class Cargo:
    def __init__(self, inputs, outputs, count, run, early=0, from_out=None):
        self.inputs, self.outputs, self.count, self.run = inputs, outputs, count, run
        self.early, self.from_out, self.late = early, from_out, from_out is not None

    def sooner(self, count=1):
        self.early = count
        return self

    def later(self):
        self.late = True
        return self


def portion_bounds(part, last_axis, portion):
    if portion is None:
        return 0, part
    cut = part // 2 // 128 * 128 if last_axis else part // 2
    return ((0, cut), (cut, part))[portion]


def send_share(weight, axis, n_dp, portion=None):
    part = weight.shape[axis] // n_dp
    low, high = portion_bounds(part, axis == weight.ndim - 1, portion)
    shape = list(weight.shape)
    shape[axis] = high - low

    def run(ship, ins, outs):
        c = ship.far(
            along(ins[0], axis, ship.d * part + low, high - low),
            outs[0],
            "tensor",
            partner(ship.t, ship.width),
            ship.slots(1),
        )
        c.start()
        yield
        c.wait()

    return Cargo([weight], [(tuple(shape), weight.dtype)], 1, run)


def join_shares(weight, share, axis, n_dp, portion=None):
    part = weight.shape[axis] // n_dp
    cut = share.shape[axis]

    def run(ship, ins, outs):
        first = lambda i: along(outs[0], axis, i * part, cut)
        second = lambda i: along(outs[0], axis, i * part + cut, part - cut)
        steps = [dp_steps(ship, first, first=ins[0])]
        put = ship.near(ins[0], first(ship.d), ship.slots(1))
        put.start()
        if cut < part:
            c = ship.far(
                along(ins[1], axis, ship.d * part + cut, part - cut),
                second(ship.d),
                "tensor",
                partner(ship.t, ship.width),
                ship.slots(1),
            )
            c.start()
        next(steps[0])
        yield
        if cut < part:
            c.wait()
            steps.append(dp_steps(ship, second))
        while steps:
            steps = [g for g in steps if next(g, g) is not g]
            if steps:
                yield
        put.wait()

    inputs = [share] + ([weight] if cut < part else [])
    return Cargo(inputs, [(weight.shape, weight.dtype)], 2 + 2 * dp_copies(n_dp), run)


def fetch(weight, axis, n_dp):
    part = weight.shape[axis] // n_dp

    def run(ship, ins, outs):
        view = lambda i: along(outs[0], axis, i * part, part)
        c = ship.far(
            along(ins[0], axis, ship.d * part, part),
            view(ship.d),
            "tensor",
            partner(ship.t, ship.width),
            ship.slots(1),
        )
        c.start()
        yield
        c.wait()
        yield from dp_steps(ship, view)

    return Cargo([weight], [(weight.shape, weight.dtype)], 1 + dp_copies(n_dp), run)


def present(array):
    def run(ship, ins, outs):
        yield

    return Cargo([array], [], 0, run)


def swap_cargo(array, axis, bit):
    def run(ship, ins, outs):
        index = ship.d if axis == "dp" else ship.t
        c = ship.far(ins[0], outs[0], axis, partner(index, bit), ship.slots(1))
        c.start()
        yield
        c.wait()

    return Cargo([array], [(array.shape, array.dtype)], 1, run)


def gather_dp(share, axis, n_dp):
    part = share.shape[axis]
    shape = list(share.shape)
    shape[axis] = part * n_dp

    def run(ship, ins, outs):
        view = lambda i: along(outs[0], axis, i * part, part)
        put = ship.near(ins[0], view(ship.d), ship.slots(1))
        put.start()
        yield from dp_steps(ship, view, first=ins[0])
        put.wait()

    return Cargo([share], [(tuple(shape), share.dtype)], 1 + dp_copies(n_dp), run)


def rows_dp(array, n_dp, upper=True, from_out=None):
    def run(ship, ins, outs):
        view = lambda i: outs[0].at[i]
        only = ship.h >= int(upper)
        k = ship.slots(1)

        @pl.when(only)
        def _():
            ship.near(ins[0], view(ship.d), k).start()

        yield from dp_steps(ship, view, first=ins[0], only=only)

        @pl.when(only)
        def _():
            ship.near(ins[0], view(ship.d), k).wait()

    outputs = [((n_dp,) + array.shape, array.dtype)]
    inputs = [array] if from_out is None else []
    return Cargo(inputs, outputs, 1 + dp_copies(n_dp), run, from_out=from_out)


@functools.lru_cache
def move_plan(size):
    width = size // 2
    moves, tables = [], []
    for slot in range(CAP):
        owners = range(width if slot else 0, size if slot else width)
        room = {t: [0, 1] for t in owners}
        table = [[0, 0] for _ in range(width)]
        away = []

        def put(j, target):
            b = slot * size + j
            place = room[target].pop(0)
            table[target % width][place] = j
            moves.append((slot // 2, b // CAP, b % CAP, target, place))

        for j in range(size):
            at = (slot * size + j) // CAP
            if room.get(at):
                put(j, at)
            else:
                away.append((j, at))
        for j, at in away:
            put(j, min((t for t in owners if room[t]), key=lambda t: (popcount(t ^ at), t)))
        tables.append(table)
    return tuple(moves), tables


def at_device(t, number, body):
    pl.when(t == number)(body)


def spread_cargo(array, n_dp, n_tensor):
    block = array.shape[0] // CAP
    model = array.shape[1]
    moves, _ = move_plan(n_tensor)

    def run(ship, ins, outs):
        item, third = outs
        t, d = ship.t, ship.d
        base = ship.slots(4)

        def into(kind, place):
            return step(third.at[d] if kind else item, place * block, block)

        def copy(move):
            kind, source, i, target, place = move
            rows = step(ins[0], i * block, block)
            if source == target:
                return ship.near(rows, into(kind, place), base + i)
            return ship.far(rows, into(kind, place), "tensor", target, base + i, base + 2 * kind + place)

        def visit(chosen, action):
            for number in range(n_tensor):
                mine = [m for m in moves if chosen(m, number)]
                if mine:
                    at_device(t, number, lambda mine=mine: [action(copy(m)) for m in mine] and None)

        start, wait = (lambda c: c.start()), (lambda c: c.wait())
        came, left = (lambda c: c.wait_recv()), (lambda c: c.wait_send())
        stays = lambda m: m[1] == m[3]
        visit(lambda m, n: m[1] == n and m[0] == 1, start)
        visit(lambda m, n: m[1] == n and m[0] == 0, start)
        yield
        visit(lambda m, n: m[3] == n and m[0] == 1 and not stays(m), came)
        visit(lambda m, n: m[3] == n and m[0] == 1 and stays(m), wait)
        yield from dp_steps(ship, lambda i: third.at[i], only=ship.h == 1)
        visit(lambda m, n: m[3] == n and m[0] == 0 and not stays(m), came)
        visit(lambda m, n: m[3] == n and m[0] == 0 and stays(m), wait)
        visit(lambda m, n: m[1] == n and not stays(m), left)

    outputs = [((2 * block, model), array.dtype), ((n_dp, 2 * block, model), array.dtype)]
    return Cargo([array], outputs, 4 + dp_copies(n_dp), run)


def return_cargo(item, third, n_tensor):
    block = item.shape[0] // 2
    model = item.shape[1]
    moves, _ = move_plan(n_tensor)

    def run(ship, ins, outs):
        t = ship.t
        base = ship.slots(4)

        def copy(move):
            kind, target, i, holder, place = move
            rows = step(ins[kind], place * block, block)
            to = step(outs[0], i * block, block)
            k = base + 2 * kind + place
            if holder == target:
                return ship.near(rows, to, k)
            return ship.far(rows, to, "tensor", target, k, base + i)

        def visit(chosen, action):
            for number in range(n_tensor):
                mine = [m for m in moves if chosen(m, number)]
                if mine:
                    at_device(t, number, lambda mine=mine: [action(copy(m)) for m in mine] and None)

        stays = lambda m: m[1] == m[3]
        visit(lambda m, n: m[3] == n, lambda c: c.start())
        yield
        visit(lambda m, n: m[1] == n and not stays(m), lambda c: c.wait_recv())
        visit(lambda m, n: m[3] == n and stays(m), lambda c: c.wait())
        visit(lambda m, n: m[3] == n and not stays(m), lambda c: c.wait_send())

    return Cargo([item, third], [((CAP * block, model), item.dtype)], 4, run)


def gather_tensor(array, n_tensor, cut=False):
    share = array.shape[1] // n_tensor if cut else array.shape[1]

    def run(ship, ins, outs):
        base = ship.slots(n_tensor)
        part = lambda i: along(ins[0], 1, i * share, share) if cut else ins[0]
        put = ship.near(part(ship.t), outs[0].at[ship.t], base)
        put.start()
        others = [(k, (ship.t + k) % n_tensor) for k in range(1, n_tensor)]
        copies = [
            ship.far(part(other), outs[0].at[ship.t], "tensor", other, base + k) for k, other in others
        ]
        for c in copies:
            c.start()
        yield
        for c in copies:
            c.wait()
        put.wait()

    shape = (n_tensor, array.shape[0], share)
    return Cargo([array], [(shape, array.dtype)], n_tensor, run)


def exchange(
    cid,
    n_dp,
    n_tensor,
    rows,
    model,
    inputs=(),
    outputs=(),
    middle=None,
    scatter=False,
    gather=False,
    cargo=(),
    upper_part=2,
    vmem_mib=40,
):
    width = n_tensor // 2
    cut = rows // upper_part
    begins, sizes = (0, cut), (cut, rows - cut)
    pieces = [(o, hs) for o in range(1, width) for hs in range(2)]
    number = {piece: k for k, piece in enumerate(pieces)}
    bits = bits_of(width)

    def last_bit(piece):
        return top_bit(piece[0]) if piece[1] == 0 else low_bit(piece[0])

    def incoming(piece):
        return [p for p in pieces if p[1] == piece[1] and p[0] ^ last_bit(p) == piece[0]]

    scatter_order = sorted(pieces, key=lambda p: (-popcount(p[0]), len(incoming(p)), p[0]))
    gather_order = sorted(
        pieces, key=lambda p: (popcount(p[0]), p[1] if last_bit(p) != bits[-1] else 1 - p[1])
    )
    n_in, n_out = len(inputs), len(outputs)
    carried = [array for c in cargo for array in c.inputs]
    landed = [shape for c in cargo for shape in c.outputs]
    cargo_copies = max(sum(c.count for c in cargo), 1)

    def kernel(*refs):
        rest = list(refs)

        def take(count):
            taken = rest[:count]
            del rest[:count]
            return taken

        ins, cargo_ins, outs, cargo_outs = take(n_in), take(len(carried)), take(n_out), take(len(landed))
        gathered = rest.pop(0) if gather else None
        ship = Ship(n_dp, n_tensor, *take(3))
        own = rest.pop(0)
        local_sem = rest.pop(0)
        if scatter:
            arrived, s_send, s_recv = rest.pop(0), rest.pop(0), rest.pop(0)
        if gather:
            g_send, g_recv = rest.pop(0), rest.pop(0)
        t, d = ship.t, ship.d
        barrier = pltpu.get_barrier_semaphore()
        greeted = [("tensor", (t + k) % n_tensor) for k in range(1, n_tensor)]
        greeted += [("dp", partner(d, bit)) for bit in bits_of(n_dp)]
        for axis, place in greeted:
            pl.semaphore_signal(
                barrier, inc=1, device_id={axis: place}, device_id_type=pl.DeviceIdType.MESH
            )
        pl.semaphore_wait(barrier, len(greeted))

        stages, waiting, soon = [], [], []
        for c in cargo:
            c_ins, cargo_ins = cargo_ins[: len(c.inputs)], cargo_ins[len(c.inputs) :]
            c_outs, cargo_outs = cargo_outs[: len(c.outputs)], cargo_outs[len(c.outputs) :]
            if not c.late:
                stage = c.run(ship, c_ins, c_outs)
                next(stage)
                stages.append(stage)
                soon.append([stage, c.early])
            else:
                source = c_ins if c.from_out is None else [outs[c.from_out]]
                waiting.append(c.run(ship, source, c_outs))

        def advance():
            for entry in soon:
                if entry[1]:
                    entry[1] -= 1
                    next(entry[0])

        if scatter:
            part = ins[0]
            copies = {}
            for piece in scatter_order:
                o, hs = piece
                came = incoming(piece)
                base, half = o * rows + begins[hs], sizes[hs]
                for p in came:
                    copies[p].wait_recv()
                source = step(part, base, half)
                if came:
                    source = step(arrived.at[number[came[0]]], 0, half)

                    def add(r, base=base, came=came):
                        total = part[pl.ds(base + r, ROW_TILE)].astype(f32)
                        for p in came:
                            total = total + arrived[number[p], pl.ds(r, ROW_TILE)].astype(f32)
                        arrived[number[came[0]], pl.ds(r, ROW_TILE)] = total.astype(bf16)

                    row_tiles(half, add)
                k = number[piece]
                copies[piece] = pltpu.make_async_remote_copy(
                    src_ref=source,
                    dst_ref=step(arrived.at[k], 0, half),
                    send_sem=s_send.at[k],
                    recv_sem=s_recv.at[k],
                    device_id={"tensor": partner(t, last_bit(piece))},
                    device_id_type=pl.DeviceIdType.MESH,
                )
                copies[piece].start()
            advance()
            for piece in pieces:
                if popcount(piece[0]) == 1:
                    copies[piece].wait_recv()

        def summed(hs, r):
            total = ins[0][pl.ds(begins[hs] + r, ROW_TILE)].astype(f32)
            for bit in bits:
                total = total + arrived[number[(bit, hs)], pl.ds(r, ROW_TILE)].astype(f32)
            return total

        if middle is not None:
            middle((begins, sizes), summed, ins, outs, own)
        for stage in waiting:
            next(stage)
        stages = waiting + stages

        if gather:
            keep = pltpu.make_async_copy(own, step(gathered, 0, rows), local_sem)
            keep.start()
            sent = {}
            forwarding = False
            for piece in gather_order:
                o, hs = piece
                bit = last_bit(piece)
                before = o ^ bit
                if before and not forwarding:
                    forwarding = True
                    advance()
                if before:
                    sent[(before, hs)].wait_recv()
                    source = step(gathered, before * rows + begins[hs], sizes[hs])
                else:
                    source = step(own, begins[hs], sizes[hs])
                k = number[piece]
                sent[piece] = pltpu.make_async_remote_copy(
                    src_ref=source,
                    dst_ref=step(gathered, o * rows + begins[hs], sizes[hs]),
                    send_sem=g_send.at[k],
                    recv_sem=g_recv.at[k],
                    device_id={"tensor": partner(t, bit)},
                    device_id_type=pl.DeviceIdType.MESH,
                )
                sent[piece].start()
        while stages:
            stages = [stage for stage in stages if next(stage, stage) is not stage]
        if gather:
            used = {(p[0] ^ last_bit(p), p[1]) for p in pieces if p[0] ^ last_bit(p)}
            for piece in pieces:
                if piece not in used:
                    sent[piece].wait_recv()
            keep.wait()
            for piece in pieces:
                sent[piece].wait_send()
        if scatter:
            for piece in pieces:
                copies[piece].wait_send()

    vmem = pl.BlockSpec(memory_space=pltpu.VMEM)
    anywhere = pl.BlockSpec(memory_space=pl.ANY)
    shapes = [jax.ShapeDtypeStruct(*o) for o in list(outputs) + landed]
    specs = [vmem] * n_out + [anywhere] * len(landed)
    if gather:
        shapes.append(jax.ShapeDtypeStruct((width * rows, model), bf16))
        specs.append(anywhere)
    scratch = [pltpu.SemaphoreType.DMA((cargo_copies,)) for _ in range(3)]
    scratch += [pltpu.VMEM((rows, model), bf16), pltpu.SemaphoreType.DMA]
    count = len(pieces)
    if scatter:
        scratch += [
            pltpu.VMEM((count, max(sizes), model), bf16),
            pltpu.SemaphoreType.DMA((count,)),
            pltpu.SemaphoreType.DMA((count,)),
        ]
    if gather:
        scratch += [pltpu.SemaphoreType.DMA((count,)), pltpu.SemaphoreType.DMA((count,))]
    results = pl.pallas_call(
        kernel,
        out_shape=shapes,
        in_specs=[vmem] * n_in + [anywhere] * len(carried),
        out_specs=specs,
        scratch_shapes=scratch,
        compiler_params=pltpu.CompilerParams(
            collective_id=cid, has_side_effects=True, vmem_limit_bytes=vmem_mib << 20
        ),
        name=f"exchange_{cid}",
    )(*inputs, *carried)
    plain, rest = list(results[:n_out]), list(results[n_out:])
    if gather:
        plain.append(rest.pop())
    brought = []
    for c in cargo:
        brought.append(rest[: len(c.outputs)])
        rest = rest[len(c.outputs) :]
    return plain, brought


def norm_tile(values):
    centre = values - jnp.mean(values, -1, keepdims=True)
    scale_inv = lax.rsqrt(jnp.mean(centre * centre, -1, keepdims=True) + epsilon)
    return centre * scale_inv, scale_inv


def norm_back_tile(grad_out, normed, scale_inv, gain):
    grad_normed = grad_out * gain
    centred = grad_normed - jnp.mean(grad_normed, -1, keepdims=True)
    return scale_inv * (centred - normed * jnp.mean(grad_normed * normed, -1, keepdims=True))


def each_tile(parts, body):
    begins, sizes = parts
    for hs in range(2):
        row_tiles(sizes[hs], lambda r, hs=hs: body(hs, r, pl.ds(begins[hs] + r, ROW_TILE)))


def fold(values):
    return jnp.sum(values.reshape(-1, 8, values.shape[-1]), 0)


def gather_middle(parts, summed, ins, outs, own):
    def body(hs, r, at):
        own[at] = ins[0][at]

    each_tile(parts, body)


def first_middle(parts, summed, ins, outs, own):
    _, tokens, b_out, gain, shift = ins

    def body(hs, r, at):
        first = deep_alpha * tokens[at].astype(f32) + (summed(hs, r) + b_out[...])
        outs[0][at] = first
        normed, _ = norm_tile(first)
        own[at] = (normed * gain[...] + shift[...]).astype(bf16)

    each_tile(parts, body)


def second_middle(parts, summed, ins, outs, own):
    _, first_sum, cotangent, b_down, gain_one, shift_one, gain_two, shift_two = ins
    layer_rows, grad_second, sums = outs
    sums[...] = jnp.zeros_like(sums)

    def body(hs, r, at):
        normed, _ = norm_tile(first_sum[at])
        hidden = normed * gain_one[...] + shift_one[...]
        second = deep_alpha * hidden + (summed(hs, r) + b_down[...])
        normed, inv = norm_tile(second)
        layer_rows[at] = (normed * gain_two[...] + shift_two[...]).astype(bf16)
        grad = cotangent[at].astype(f32)
        back = norm_back_tile(grad, normed, inv, gain_two[...])
        grad_second[at] = back
        own[at] = back.astype(bf16)
        sums[0] += fold(grad * normed)
        sums[1] += fold(grad)
        sums[2] += fold(back)

    each_tile(parts, body)


def third_middle(parts, summed, ins, outs, own):
    _, first_sum, grad_second, gain_one = ins
    grad_first, sums = outs
    sums[...] = jnp.zeros_like(sums)

    def body(hs, r, at):
        normed, inv = norm_tile(first_sum[at])
        grad = summed(hs, r) + deep_alpha * grad_second[at]
        back = norm_back_tile(grad, normed, inv, gain_one[...])
        grad_first[at] = back
        own[at] = back.astype(bf16)
        sums[0] += fold(grad * normed)
        sums[1] += fold(grad)
        sums[2] += fold(back)

    each_tile(parts, body)


def last_middle(parts, summed, ins, outs, own):
    _, grad_first = ins

    def body(hs, r, at):
        outs[0][at] = (summed(hs, r) + deep_alpha * grad_first[at]).astype(bf16)

    each_tile(parts, body)


def pick(index, values):
    out = values[0]
    for k, value in enumerate(values[1:], 1):
        out = jnp.where(index == k, value, out)
    return out


def across(value, n_dp):
    got = {0: value}
    for bit in reversed(bits_of(n_dp)):
        for offset in list(got):
            got[offset | bit] = permute(got[offset], "dp", n_dp, bit)
    return [got[offset] for offset in range(n_dp)]


def turn(vectors, cos_table, sin_table):
    return vectors * cos_table + pltpu.roll(vectors, HD // 2, 1) * sin_table


def score_tile(queries, keys, query_at, key_at, prefix_len):
    scores = lax.dot_general(
        queries, keys, (((1,), (1,)), ((), ())), preferred_element_type=f32
    ) * HD ** (-0.5)
    allowed = (key_at < prefix_len) | (key_at <= query_at)
    return jnp.where(allowed, scores, negative)


def attend_kernel(
    heads, rows, place, own, other, bias, cos_table, sin_table, key_at, query_at, turned, context
):
    prefix_len = place[0]
    size = heads * HD
    for head in range(heads):
        for c in range(3):
            at = pl.ds(c * size + head * HD, HD)
            p, local = divmod(head, heads // 2)
            came = pl.ds(local * HD, HD)
            value = (own, other)[p][c, :, came] + bias[p, c : c + 1, came]
            if c < 2:
                value = turn(value, cos_table[...], sin_table[...])
            turned[:, at] = value.astype(bf16)
    for head in range(heads):
        at = head * HD

        def one_block(i, carry, at=at):
            run = pl.ds(pl.multiple_of(i * rows, rows), rows)
            scores = score_tile(
                turned[run, at : at + HD],
                turned[:, size + at : size + at + HD],
                query_at[run],
                key_at[...],
                prefix_len,
            )
            raw = jnp.exp(scores - jnp.max(scores, -1, keepdims=True))
            weights = (raw / jnp.sum(raw, -1, keepdims=True)).astype(bf16)
            context[run, at : at + HD] = jnp.dot(
                weights, turned[:, 2 * size + at : 2 * size + at + HD], preferred_element_type=f32
            ).astype(bf16)
            return carry

        lax.fori_loop(0, LEN // rows, one_block, 0)


def attend(linear, bias, place, cos_table, sin_table, key_at, query_at, rows):
    size = 2 * 3 * linear[0].shape[2]
    heads = size // (3 * HD)
    vmem = pl.BlockSpec(memory_space=pltpu.VMEM)
    return pl.pallas_call(
        functools.partial(attend_kernel, heads, rows),
        out_shape=[
            jax.ShapeDtypeStruct((LEN, size), bf16),
            jax.ShapeDtypeStruct((LEN, size // 3), bf16),
        ],
        in_specs=[pl.BlockSpec(memory_space=pltpu.SMEM)] + [vmem] * 7,
        out_specs=[vmem] * 2,
        compiler_params=pltpu.CompilerParams(vmem_limit_bytes=40 << 20),
        name="attend",
    )(place, *linear, bias, cos_table, sin_table, key_at, query_at)


def attend_back_kernel(
    heads,
    rows,
    place,
    turned,
    grad_context,
    cos_table,
    sin_table,
    key_at,
    query_at,
    own,
    other,
    dk,
    dv,
):
    prefix_len = place[0]
    size = heads * HD
    scale = HD ** (-0.5)
    over_rows = (((0,), (0,)), ((), ()))
    over_last = (((1,), (1,)), ((), ()))
    for head in range(heads):
        at = head * HD
        p, local = divmod(head, heads // 2)
        came = pl.ds(local * HD, HD)
        grad_linear = (own, other)[p]
        dk[...] = jnp.zeros_like(dk)
        dv[...] = jnp.zeros_like(dv)

        def one_block(i, carry, at=at, grad_linear=grad_linear, came=came):
            run = pl.ds(pl.multiple_of(i * rows, rows), rows)
            queries = turned[run, at : at + HD]
            keys = turned[:, size + at : size + at + HD]
            scores = score_tile(queries, keys, query_at[run], key_at[...], prefix_len)
            raw = jnp.exp(scores - jnp.max(scores, -1, keepdims=True))
            probs = raw / jnp.sum(raw, -1, keepdims=True)
            grad = grad_context[run, at : at + HD]
            grad_weights = lax.dot_general(
                grad,
                turned[:, 2 * size + at : 2 * size + at + HD],
                over_last,
                preferred_element_type=f32,
            )
            inner = jnp.sum(probs * grad_weights, -1, keepdims=True)
            grad_scores = (probs * (grad_weights - inner)).astype(bf16)
            dq = jnp.dot(grad_scores, keys, preferred_element_type=f32) * scale
            grad_linear[0, run, came] = turn(dq, cos_table[run], sin_table[run]).astype(bf16)
            dk[...] += lax.dot_general(grad_scores, queries, over_rows, preferred_element_type=f32)
            dv[...] += lax.dot_general(
                probs.astype(bf16), grad, over_rows, preferred_element_type=f32
            )
            return carry

        lax.fori_loop(0, LEN // rows, one_block, 0)
        grad_linear[1, :, came] = turn(dk[...] * scale, cos_table[...], sin_table[...]).astype(bf16)
        grad_linear[2, :, came] = dv[...].astype(bf16)


def attend_back(turned, grad_context, place, cos_table, sin_table, key_at, query_at, rows):
    size = turned.shape[1]
    heads = size // (3 * HD)
    vmem = pl.BlockSpec(memory_space=pltpu.VMEM)
    return pl.pallas_call(
        functools.partial(attend_back_kernel, heads, rows),
        out_shape=[jax.ShapeDtypeStruct((3, LEN, size // 6), bf16)] * 2,
        in_specs=[pl.BlockSpec(memory_space=pltpu.SMEM)] + [vmem] * 6,
        out_specs=[vmem] * 2,
        scratch_shapes=[pltpu.VMEM((LEN, HD), f32), pltpu.VMEM((LEN, HD), f32)],
        compiler_params=pltpu.CompilerParams(vmem_limit_bytes=40 << 20),
        name="attend_back",
    )(place, turned, grad_context, cos_table, sin_table, key_at, query_at)


def interleave_kernel(gate, up, out):
    out[:, 0, :] = gate[...].astype(f32)
    out[:, 1, :] = up[...].astype(f32)


def interleave(gate, up):
    count, model = gate.shape
    size = 64
    block = pl.BlockSpec((size, model), lambda i: (i, 0))
    return pl.pallas_call(
        interleave_kernel,
        grid=(pl.cdiv(count, size),),
        in_specs=[block, block],
        out_specs=pl.BlockSpec((size, 2, model), lambda i: (i, 0, 0)),
        out_shape=jax.ShapeDtypeStruct((count, 2, model), f32),
        compiler_params=pltpu.CompilerParams(vmem_limit_bytes=24 << 20),
        name="interleave",
    )(gate, up)


def on_device(
    n_dp,
    n_tensor,
    tokens,
    cotangent,
    w_qkv,
    b_qkv,
    w_out,
    b_out,
    gain_one,
    shift_one,
    w_gu,
    b_gu,
    w_down,
    b_down,
    gain_two,
    shift_two,
    prefix,
    span_offset,
    cluster,
):
    d = lax.axis_index("dp")
    t = lax.axis_index("tensor")
    width = n_tensor // 2
    h = t // width
    q = t % width
    rows = LEN // width
    model = tokens.shape[1]

    counts = jnp.sum((cluster[None, :] == jnp.arange(n_dp)[:, None]).astype(jnp.int32), 1)
    spare = jnp.maximum(2 - counts, 0)
    extra = (counts == CAP).astype(jnp.int32)
    spare_before = jnp.cumsum(spare) - spare
    extra_rank = jnp.cumsum(extra) - extra

    def overflow_source(index, place):
        rank = spare_before[index] + place - counts[index]
        hit = (extra == 1) & (extra_rank == rank)
        return jnp.sum(jnp.where(hit, jnp.arange(n_dp), 0))

    source_here = overflow_source(d, h)
    source_other = overflow_source(d, 0)
    foreign = counts[d] <= h
    any_empty = jnp.any(counts == 0)
    rank_out = extra_rank[d]
    ends = spare_before + spare
    out_index = jnp.sum((ends <= rank_out).astype(jnp.int32))
    out_place = jnp.minimum(counts[out_index], 2) + rank_out - spare_before[out_index]

    def chosen(item, third):
        def with_empty(item):
            sent = permute(third[source_other], "tensor", n_tensor, width)
            return jnp.where((h == 0) & foreign, sent, item)

        item = lax.cond(any_empty, with_empty, lambda v: v, item)
        return jnp.where((h == 1) & foreign, third[source_here], item)

    def sorted_out(item, everywhere):
        third = everywhere[out_index]

        def with_empty(third):
            other = across(permute(item, "tensor", n_tensor, width), n_dp)
            return jnp.where(out_place == 0, pick(d ^ out_index, other), third)

        third = lax.cond(any_empty, with_empty, lambda v: v, third)
        return jnp.where(foreign, 0, item), jnp.where(counts[d] == CAP, third, 0)

    def flipped(array):
        return permute(array, "tensor", n_tensor, width)

    width_qkv = w_qkv.shape[2]
    width_ffn = w_gu.shape[2]
    wq = w_qkv.transpose(1, 0, 2)
    wg = w_gu.transpose(2, 1, 0)
    cut_ffn = 0 if width_ffn % n_dp == 0 else 2
    columns = jnp.arange(width_ffn)
    live_columns = [s * width_ffn + columns < FF for s in (t, t ^ width)]
    pairs = (0, 1)

    def row(vector):
        return vector.reshape(1, -1)

    def tile_of(array):
        return jnp.pad(array, ((0, 8 - array.shape[0]), (0, -array.shape[1] % 128)))

    swap = functools.partial(exchange, n_dp=n_dp, n_tensor=n_tensor, rows=rows, model=model)
    facts = jnp.stack([prefix, span_offset])

    _, (spread_tokens, (wq_share,), (facts_all,), (bq_other,), (bg_other,)) = swap(
        0,
        cargo=[
            spread_cargo(tokens, n_dp, n_tensor),
            send_share(wq, 1, n_dp, 0),
            rows_dp(tile_of(facts), n_dp, upper=False),
            swap_cargo(tile_of(b_qkv), "tensor", width),
            swap_cargo(tile_of(b_gu), "tensor", width),
        ],
    )
    bq = jnp.stack([b_qkv, bq_other[:3, :width_qkv]])
    bg = [b_gu, bg_other[:2, :width_ffn]]
    facts_all = facts_all[:, :2, :CAP]
    own_tokens = chosen(*spread_tokens)
    (tokens_all,), ((wq_other,), (wo_other,)) = swap(
        1,
        upper_part=UP1,
        inputs=[own_tokens],
        middle=gather_middle,
        gather=True,
        cargo=[
            join_shares(wq, wq_share, 1, n_dp, 1).sooner(1),
            fetch(w_out, 0, n_dp),
        ],
    )
    wq = [wq, wq_other]
    wd_part = model // n_dp
    wd_share = lax.dynamic_slice_in_dim(w_down, d * wd_part, wd_part, 1)
    wg_part = wg.shape[cut_ffn] // n_dp
    wg_low, wg_high = portion_bounds(wg_part, cut_ffn == 2, 0)
    wg_share = lax.dynamic_slice_in_dim(wg, d * wg_part + wg_low, wg_high - wg_low, cut_ffn)
    wg_share, wd_share, tokens_all = lax.optimization_barrier((wg_share, wd_share, tokens_all))
    wg_share, wd_share = flipped(wg_share), flipped(wd_share)
    fact = jnp.where(foreign, facts_all[source_here][:, 2], jnp.where(h == 0, facts[:, 0], facts[:, 1]))
    prefix_len, span_start = fact[0], fact[1]

    block = LEN // n_tensor
    tables = jnp.asarray(move_plan(n_tensor)[1], jnp.int32)
    starts = tables[jnp.where(foreign, CAP - 1, h)][q ^ jnp.arange(width)].reshape(n_tensor) * block
    position = (starts[:, None] + jnp.arange(block)[None, :]).reshape(LEN)
    placed = jnp.where(position < prefix_len, position, span_start + position - prefix_len).astype(f32)
    frequency = theta_base ** (-(jnp.arange(HD // 2).astype(f32) * 2.0 / HD))
    angles = placed[:, None] * frequency[None, :]
    cos_half, sin_half = jnp.cos(angles), jnp.sin(angles)
    cos_table = jnp.concatenate([cos_half, cos_half], 1)
    sin_table = jnp.concatenate([-sin_half, sin_half], 1)
    key_at = position[None, :].astype(jnp.int32)
    query_at = position[:, None].astype(jnp.int32)
    place = prefix_len[None].astype(jnp.int32)

    def dot(a, b):
        return jnp.dot(a, b, preferred_element_type=f32)

    def sum_of(spec, a, b):
        terms = [jnp.einsum(spec, a[p], b[p], preferred_element_type=f32) for p in pairs]
        return (terms[0] + terms[1]).astype(bf16)

    wo = jnp.concatenate([w_out, wo_other], 0)
    linear = [jnp.einsum("td,cdn->ctn", tokens_all, wq[p], preferred_element_type=f32) for p in pairs]
    turned, context = attend(linear, bq, place, cos_table, sin_table, key_at, query_at, rows)
    partial_out = dot(context, wo).astype(bf16)
    full = ((rows, model), f32)
    (first_sum, hidden_all), ((wg_other,), (wd_other,), spread_cotangent) = swap(
        2,
        upper_part=UP2,
        inputs=[partial_out, own_tokens, row(b_out), row(gain_one), row(shift_one)],
        outputs=[full],
        middle=first_middle,
        scatter=True,
        gather=True,
        cargo=[
            join_shares(wg, wg_share, cut_ffn, n_dp, 1).sooner(2),
            join_shares(w_down, wd_share, 1, n_dp).sooner(1),
            spread_cargo(cotangent, n_dp, n_tensor).sooner(2),
        ],
    )
    wg = [wg, wg_other]
    wd = [w_down, wd_other]
    own_cotangent = chosen(*spread_cotangent)

    def activate(live, gate_up):
        return jnp.where(live, jax.nn.gelu(gate_up[0], approximate=True) * gate_up[1], 0.0)

    inner, pull = [], []
    for p in pairs:
        gate_up = jnp.einsum("td,ncd->ctn", hidden_all, wg[p], preferred_element_type=f32)
        activated, pull_act = jax.vjp(
            functools.partial(activate, live_columns[p]), gate_up + bg[p][:, None]
        )
        inner.append(activated.astype(bf16))
        pull.append(pull_act)
    partial_fed = sum_of("tn,nd->td", inner, wd)
    sums_shape = ((3, 8, model), f32)
    layer_shape = jax.ShapeDtypeStruct((rows, model), bf16)
    (layer_rows, grad_second, sums_two, grad_fed_all), ((layer_everywhere,),) = swap(
        3,
        inputs=[
            partial_fed,
            first_sum,
            own_cotangent,
            row(b_down),
            row(gain_one),
            row(shift_one),
            row(gain_two),
            row(shift_two),
        ],
        outputs=[((rows, model), bf16), full, sums_shape],
        middle=second_middle,
        scatter=True,
        gather=True,
        cargo=[rows_dp(layer_shape, n_dp, from_out=0)],
    )

    def add(a, b):
        return (a.astype(f32) + b.astype(f32)).astype(bf16)

    dp_bits = bits_of(n_dp)

    share = model // n_dp

    def columns_of(array):
        return [lax.dynamic_slice_in_dim(array, (d ^ o) * share, share, 1) for o in range(n_dp)]

    def halve(columns, make, axis):
        odd = range(1, n_dp, 2)
        sent = make(jnp.concatenate([columns[o] for o in odd], 1)).astype(bf16)
        came = permute(sent, "dp", n_dp, 1)
        pieces = {}
        for k, o in enumerate(odd):
            piece = lax.slice_in_dim(came, k * share, (k + 1) * share, axis=axis)
            pieces[o - 1] = (make(columns[o - 1]) + piece.astype(f32)).astype(bf16)
        for bit in dp_bits[1:-1]:
            for o in [o for o in pieces if o & bit]:
                pieces[o ^ bit] = add(pieces[o ^ bit], permute(pieces.pop(o), "dp", n_dp, bit))
        return pieces[0], pieces[dp_bits[-1]]

    def across_dp(value):
        return swap_cargo(value, "dp", dp_bits[-1])

    def across_pair(value):
        return swap_cargo(value, "tensor", width)

    grad_gate_up = [
        pull[p](jnp.einsum("td,nd->tn", grad_fed_all, wd[p], preferred_element_type=f32))[0].astype(bf16)
        for p in pairs
    ]

    hidden_columns = columns_of(hidden_all)
    fed_columns = columns_of(grad_fed_all)

    def ein(spec, a):
        return lambda b: jnp.einsum(spec, a, b, preferred_element_type=f32)

    down_keep, down_send = zip(*[halve(fed_columns, ein("tn,td->nd", inner[p]), 1) for p in pairs])
    gu_keep, gu_send = zip(
        *[
            halve(hidden_columns, ein("tn,td->nd", grad_gate_up[p][c]), 1)
            for p in pairs
            for c in range(2)
        ]
    )
    down = [add(down_keep[p], permute(down_send[p], "dp", n_dp, dp_bits[-1])) for p in pairs]
    grad_b_gu = jnp.stack([jnp.sum(grad_gate_up[p].astype(f32), 1) for p in pairs])
    partial_hidden = sum_of("ctn,ncd->td", grad_gate_up, wg)
    (
        (grad_first, sums_one, grad_att_all),
        (*gu_came, _),
    ) = swap(
        4,
        upper_part=UP4,
        inputs=[partial_hidden, first_sum, grad_second, row(gain_one)],
        outputs=[full, sums_shape],
        middle=third_middle,
        scatter=True,
        gather=True,
        cargo=[
            *[across_dp(v) for v in gu_send],
            present(down[1]),
        ],
    )
    down_sent, grad_att_all = lax.optimization_barrier((down[1], grad_att_all))
    down_came = flipped(down_sent)
    gu = [add(gu_keep[k], gu_came[k][0]) for k in range(4)]
    gate_came = flipped(gu[2])
    grad_context = lax.dot_general(
        grad_att_all, wo, (((1,), (1,)), ((), ())), preferred_element_type=f32
    ).astype(bf16)
    out_keep, out_send = halve(columns_of(grad_att_all), ein("tn,td->nd", context), 1)
    grad_linear = attend_back(
        turned, grad_context, place, cos_table, -sin_table, key_at, query_at, rows
    )
    down_came, out_send, *grad_linear = lax.optimization_barrier((down_came, out_send, *grad_linear))
    out = add(out_keep, permute(out_send, "dp", n_dp, dp_bits[-1])).reshape(2, width_qkv, share)
    down = add(down[0], down_came)
    token_columns = columns_of(tokens_all)
    qkv_keep, qkv_send = zip(
        *[halve(token_columns, ein("ctn,td->cdn", grad_linear[p]), 1) for p in pairs]
    )
    grad_b_qkv = jnp.stack([jnp.sum(grad_linear[p].astype(f32), 1) for p in pairs])
    partial_in = sum_of("ctn,cdn->td", grad_linear, wq)
    bias = jnp.concatenate(
        [grad_b_qkv.reshape(2, 3 * width_qkv), grad_b_gu.reshape(2, 2 * width_ffn)], 1
    )
    bias = jnp.pad(bias, ((0, 0), (0, -bias.shape[1] % model))).reshape(-1, model)
    bias_rows = bias.shape[0] // 2
    upto = lambda array: jnp.pad(array, ((0, -array.shape[0] % 8), (0, 0)))
    norm_grads = jnp.concatenate([jnp.sum(sums_one, 1), jnp.sum(sums_two, 1)])
    small = jnp.concatenate([upto(norm_grads), upto(bias[:bias_rows]), upto(bias[bias_rows:])])
    bias_at = small.shape[0] - 2 * upto(bias[:bias_rows]).shape[0]
    (
        (input_rows,),
        (
            (input_everywhere,),
            (out_came,),
            (qkv_came0,),
            (qkv_came1,),
            _,
            _,
            (up_came,),
            (small,),
        ),
    ) = swap(
        5,
        upper_part=UP5,
        inputs=[partial_in, grad_first],
        outputs=[((rows, model), bf16)],
        middle=last_middle,
        scatter=True,
        cargo=[
            rows_dp(layer_shape, n_dp, from_out=0),
            across_pair(out[1]).later(),
            across_dp(qkv_send[0]),
            across_dp(qkv_send[1]),
            present(gate_came),
            present(down),
            across_pair(gu[3]),
            rows_dp(small, n_dp, upper=False),
        ],
    )
    gate, up = add(gu[0], gate_came), add(gu[1], up_came)
    qkv = [add(qkv_keep[0], qkv_came0), add(qkv_keep[1], qkv_came1)]
    small = jnp.sum(small, 0)
    bias_own, bias_other = jnp.split(small[bias_at:], 2)
    _, ((input_grad,), (qkv_came,), (gate,), (up,), (down,), (norms,), (bias_came,)) = swap(
        6,
        cargo=[
            return_cargo(*sorted_out(input_rows, input_everywhere), n_tensor),
            across_pair(qkv[1]),
            gather_dp(gate, 1, n_dp),
            gather_dp(up, 1, n_dp),
            gather_dp(down, 1, n_dp),
            gather_tensor(small[:bias_at], n_tensor, cut=True),
            swap_cargo(bias_other, "tensor", width),
        ],
    )
    bias = (bias_own + bias_came)[:bias_rows].reshape(-1)
    out = add(out[0], out_came)
    qkv = add(qkv[0], qkv_came)
    _, ((out,), (qkv,), (norms,), (layer_out,)) = swap(
        7,
        cargo=[
            gather_dp(out, 1, n_dp),
            gather_dp(qkv, 1, n_dp),
            gather_tensor(jnp.sum(norms, 0), n_tensor),
            return_cargo(*sorted_out(layer_rows, layer_everywhere), n_tensor),
        ],
    )

    norm_grads = norms.transpose(1, 0, 2).reshape(-1, model)
    grad_b_qkv = bias[: 3 * width_qkv].reshape(3, width_qkv)
    grad_b_gu = bias[3 * width_qkv : 3 * width_qkv + 2 * width_ffn].reshape(2, width_ffn)
    return (
        layer_out.astype(f32),
        input_grad.astype(f32),
        qkv.astype(f32).transpose(1, 0, 2),
        grad_b_qkv,
        out.astype(f32),
        norm_grads[2],
        norm_grads[0],
        norm_grads[1],
        interleave(gate, up).transpose(2, 1, 0),
        grad_b_gu,
        down.astype(f32),
        norm_grads[5],
        norm_grads[3],
        norm_grads[4],
    )


def solution(mesh):
    rows = P(("dp", "tensor"), None)
    weights = (P(None, None, "tensor"), P(None, "tensor"), P("tensor", None), P(), P(), P())
    placed_ffn = (P(None, None, "tensor"), P(None, "tensor"), P("tensor", None), P(), P(), P())
    placed = (rows, rows) + weights + placed_ffn + (P("dp"), P("dp"), P())
    n_dp, n_tensor = mesh.shape["dp"], mesh.shape["tensor"]

    def body(*arguments):
        return on_device(n_dp, n_tensor, *arguments)

    return jax.shard_map(
        body,
        mesh=mesh,
        in_specs=placed,
        out_specs=(rows, rows) + weights + placed_ffn,
        check_vma=False,
    )
```
